32 devices in a mesh: row: 2 (over y), seq: 16 (over z, x, core).
Axes of the slice: x: 2, y: 2, z: 4, core: 2. Of those that a mesh axis runs over, the one named last changes fastest.
Arguments:
- frames: bfloat16 [2, 4096, 1024], P('row', 'seq'), may hold values from -6 to 6
- seg_lengths: int32 [2, 4], P('row'), may hold values from 1 to 3968, 4096 in all within a row
- ln1_gain: float32 [1024], replicated, may hold values from 0.5 to 1.5
- ln1_bias: float32 [1024], replicated, may hold values from -3 to 3
- w_qkv: bfloat16 [1024, 3072], replicated, may hold values from -0.1875 to 0.1875
- bias_qv: float32 [2048], replicated, may hold values from -3 to 3
- w_out: bfloat16 [1024, 1024], replicated, may hold values from -0.75 to 0.75
- bias_out: float32 [1024], replicated, may hold values from -3 to 3
- ln2_gain: float32 [1024], replicated, may hold values from 0.5 to 1.5
- ln2_bias: float32 [1024], replicated, may hold values from -3 to 3
- w_up: bfloat16 [1024, 4096], replicated, may hold values from -0.1875 to 0.1875
- bias_up: float32 [4096], replicated, may hold values from -3 to 3
- w_down: bfloat16 [4096, 1024], replicated, may hold values from -0.09375 to 0.09375
- bias_down: float32 [1024], replicated, may hold values from -6 to 6
- grad_out: bfloat16 [2, 4096, 1024], P('row', 'seq'), may hold values from -6 to 6
Outputs:
- out_frames: bfloat16 [2, 4096, 1024], P('row', 'seq')
- grad_frames: bfloat16 [2, 4096, 1024], P('row', 'seq')
- grad_ln1_gain: float32 [1024], P('seq')
- grad_ln1_bias: float32 [1024], P('seq')
- grad_w_qkv: float32 [1024, 3072], P('seq')
- grad_bias_qv: float32 [2048], P('seq')
- grad_w_out: float32 [1024, 1024], P('seq')
- grad_bias_out: float32 [1024], P('seq')
- grad_ln2_gain: float32 [1024], P('seq')
- grad_ln2_bias: float32 [1024], P('seq')
- grad_w_up: float32 [1024, 4096], P('seq')
- grad_bias_up: float32 [4096], P('seq')
- grad_w_down: float32 [4096, 1024], P('seq')
- grad_bias_down: float32 [1024], P('seq')
The draws below stay inside these ranges and needn't reach their ends.
Inputs may be any that keep to these rules, and one draw needn't show every extreme that they name: `seg_lengths`: the 4 segments of a packed row in order; their lengths sum to 4096.
All inputs are finite; a program needn't handle non-finite values.
Results may differ from the reference program's by a relative error of at most 0.024.
Values may be sent and summed in bfloat16 or wider, within the bound.
No kernel may reach another device: no remote copies, remote signals or barrier semaphores. Data moves between devices by JAX's collectives and lax.ppermute only.
A program may use at most 256 MiB of HBM per device.

```python
import math
import jax
import jax.numpy as jnp
import numpy as np
from jax import lax

D = 1024
HEADS = 16
HEAD_DIM = 64
FF = 4096
NSEG = 4
ROWS = 2
LEN = 4096
SHORT = 128


def level_of(rng, extent, cuts, smallest, largest):
    level, own = 1.0, jax.random.fold_in(rng, 6)
    for position, blocks in cuts:
        heights = jnp.exp(jax.random.uniform(jax.random.fold_in(own, position), (blocks,), jnp.float32, smallest / len(cuts), largest / len(cuts)))
        level = level * jnp.repeat(heights, extent[position] // blocks).reshape([-1 if axis == position else 1 for axis in range(len(extent))])
    return level


def length_profile(amount, total, limit, lean):
    weights = [(1 << 20) // math.isqrt(grade ** lean) + 1 for grade in range(2, amount + 1)]
    rest, counts = total - limit - (amount - 1), [1] * (amount - 1)
    while rest > 0:
        movable = [i for i in range(amount - 1) if counts[i] < limit]
        whole, budget = sum([weights[i] for i in movable]), rest
        for i in movable:
            more = min(limit - counts[i], max(1, budget * weights[i] // whole), rest)
            counts[i] = counts[i] + more
            rest = rest - more
    return np.array([limit] + counts)


def uneven(rng, amount, total, bound, slope):
    if amount == 2:
        one = jax.random.randint(rng, (), max(1, total - bound), min(bound, total - 1) + 1)
        return jnp.stack([one, total - one])
    tallies = jnp.asarray(length_profile(amount, total, bound, slope), jnp.int32)
    couples = (amount - 1) // 2
    giver, taker = tallies[1:1 + 2 * couples:2], tallies[2:2 + 2 * couples:2]
    margin = jnp.minimum(giver - 1, bound - taker)
    shifted = jax.random.randint(jax.random.fold_in(rng, 1), (couples,), 0, 1 << 20) % (margin + 1)
    tallies = tallies.at[1:1 + 2 * couples:2].set(giver - shifted).at[2:2 + 2 * couples:2].set(taker + shifted)
    return tallies[jax.random.permutation(jax.random.fold_in(rng, 2), amount)]


def scatter_about(key, dims, deviation, limit, split=(), kind=jnp.bfloat16):
    loudness = level_of(key, dims, split, -0.22, 0.18) if split else 1.0
    array = jax.random.normal(key, dims, jnp.float32) * deviation * loudness
    return jnp.minimum(jnp.maximum(array, -limit), limit).astype(kind)


def setup_inputs(seed: int = 0) -> dict:
    key_list = jax.random.split(jax.random.key(seed), 16)
    return {
        "frames": scatter_about(key_list[0], (ROWS, LEN, D), 1.0, 6.0, ((0, 2), (1, 16))),
        "seg_lengths": jax.vmap(lambda own: uneven(own, NSEG, LEN, LEN - SHORT, 0))(jax.random.split(key_list[1], ROWS)).reshape((ROWS, NSEG)).astype(jnp.int32),
        "ln1_gain": jnp.clip(1.0 + 0.1 * jax.random.normal(key_list[2], (D,), jnp.float32), 0.5, 1.5),
        "ln1_bias": scatter_about(key_list[3], (D,), 0.3, 3.0, (), jnp.float32),
        "w_qkv": scatter_about(key_list[4], (D, 3 * D), D ** -0.5, 0.1875),
        "bias_qv": scatter_about(key_list[5], (2 * D,), 0.3, 3.0, (), jnp.float32),
        "w_out": scatter_about(key_list[6], (D, D), 64 ** -0.5, 0.75),
        "bias_out": scatter_about(key_list[7], (D,), 0.3, 3.0, (), jnp.float32),
        "ln2_gain": jnp.clip(1.0 + 0.1 * jax.random.normal(key_list[8], (D,), jnp.float32), 0.5, 1.5),
        "ln2_bias": scatter_about(key_list[9], (D,), 0.3, 3.0, (), jnp.float32),
        "w_up": scatter_about(key_list[10], (D, FF), D ** -0.5, 0.1875),
        "bias_up": scatter_about(key_list[11], (FF,), 0.3, 3.0, (), jnp.float32),
        "w_down": scatter_about(key_list[12], (FF, D), FF ** -0.5, 0.09375),
        "bias_down": scatter_about(key_list[13], (D,), 1.5, 6.0, (), jnp.float32),
        "grad_out": scatter_about(key_list[14], (ROWS, LEN, D), 1.0, 6.0, ((0, 2), (1, 16))),
    }


EPSILON = 1e-05
NEGATIVE = -1e+30
HIGHEST = lax.Precision.HIGHEST

@jax.custom_vjp
def low(v):
    return lax.optimization_barrier(v.astype(jnp.bfloat16)).astype(jnp.float32)

@jax.custom_vjp
def low_back(v):
    return v

def low_keep(v):
    return (low(v), None)

def low_pass(kept, grad):
    return (grad,)

def back_keep(v):
    return (v, None)

def back_low(kept, grad):
    return (low(grad),)
low.defvjp(low_keep, low_pass)
low_back.defvjp(back_keep, back_low)

def normalize(values, norm_gain, norm_shift):
    centre = lax.optimization_barrier(jnp.mean(values, axis=-1, keepdims=True))
    centred = values - centre
    second = lax.optimization_barrier(jnp.mean(centred * centred, axis=-1, keepdims=True))
    return centred * lax.rsqrt(second + EPSILON) * norm_gain + norm_shift

def segment_first(lengths, positions):
    offsets = jnp.cumsum(lengths, dtype=jnp.int32) - lengths
    reached = offsets[None, :] <= positions[:, None]
    return lax.optimization_barrier(jnp.max(jnp.where(reached, offsets[None, :], 0), axis=1))

def layer_row(params, stream, lengths):
    ln1_gain, ln1_bias, w_qkv, bias_qv, w_out, bias_out, ln2_gain, ln2_bias, w_up, bias_up, w_down, bias_down = params
    feature = stream.shape[1]
    score_scale = HEAD_DIM ** (-0.5)
    normed = low(normalize(stream, ln1_gain, ln1_bias))
    bias_full = jnp.concatenate([bias_qv[:feature], jnp.zeros((feature,), jnp.float32), bias_qv[feature:]])
    projected = low_back(jnp.dot(normed, w_qkv, precision=HIGHEST) + bias_full)
    queries = low(projected[:, :feature])
    key_rows = low(projected[:, feature:2 * feature])
    value_rows = low(projected[:, 2 * feature:])
    positions = jnp.arange(LEN, dtype=jnp.int32)
    firsts = segment_first(lengths, positions)
    key_split = key_rows.reshape(LEN, HEADS, HEAD_DIM)
    value_split = value_rows.reshape(LEN, HEADS, HEAD_DIM)
    block_rows = math.gcd(LEN, 512)
    block_count = LEN // block_rows

    def attend_block(block_data):
        query_rows, query_pos, query_first = block_data
        query_split = query_rows.reshape(block_rows, HEADS, HEAD_DIM)
        raw_scores = jnp.einsum('qhd,khd->hqk', query_split, key_split, precision=HIGHEST) * score_scale
        scores = low_back(raw_scores)
        allowed = (positions[None, :] <= query_pos[:, None]) & (positions[None, :] >= query_first[:, None])
        masked = jnp.where(allowed[None], scores, NEGATIVE)
        row_top = lax.optimization_barrier(jnp.max(masked, axis=2, keepdims=True))
        weights = jnp.exp(masked - row_top)
        totals = lax.optimization_barrier(jnp.sum(weights, axis=2))
        summed = low_back(jnp.einsum('hqk,khd->qhd', low(weights), value_split, precision=HIGHEST))
        return (summed / totals.T[:, :, None]).reshape(block_rows, feature)
    attended = lax.map(jax.checkpoint(attend_block), (queries.reshape(block_count, block_rows, feature), positions.reshape(block_count, block_rows), firsts.reshape(block_count, block_rows))).reshape(LEN, feature)
    branch = low_back(jnp.dot(low(attended), w_out, precision=HIGHEST) + bias_out)
    residual = stream + branch
    normed_two = low(normalize(residual, ln2_gain, ln2_bias))
    up_proj = low_back(jnp.dot(normed_two, w_up, precision=HIGHEST) + bias_up)
    hidden = low(jax.nn.gelu(up_proj, approximate=False))
    return residual + low_back(jnp.dot(hidden, w_down, precision=HIGHEST) + bias_down)

def reference(frames, seg_lengths, ln1_gain, ln1_bias, w_qkv, bias_qv, w_out, bias_out, ln2_gain, ln2_bias, w_up, bias_up, w_down, bias_down, grad_out):
    params = (ln1_gain.astype(jnp.float32), ln1_bias.astype(jnp.float32), w_qkv.astype(jnp.float32), bias_qv.astype(jnp.float32), w_out.astype(jnp.float32), bias_out.astype(jnp.float32), ln2_gain.astype(jnp.float32), ln2_bias.astype(jnp.float32), w_up.astype(jnp.float32), bias_up.astype(jnp.float32), w_down.astype(jnp.float32), bias_down.astype(jnp.float32))

    def one_row(grad_sums, row_data):
        stream, lengths, cotangent = row_data

        def forward(weights_now, stream_now):
            return layer_row(weights_now, stream_now, lengths)
        result, backward = jax.vjp(forward, params, stream.astype(jnp.float32))
        weight_grads, stream_grad = backward(cotangent.astype(jnp.float32))
        grad_sums = jax.tree.map(jnp.add, grad_sums, weight_grads)
        return (grad_sums, (result.astype(jnp.bfloat16), stream_grad.astype(jnp.bfloat16)))
    initial = jax.tree.map(jnp.zeros_like, params)
    grad_sums, (outputs, input_grads) = lax.scan(one_row, initial, (frames, seg_lengths, grad_out))
    return (outputs, input_grads, grad_sums[0], grad_sums[1], grad_sums[2], grad_sums[3], grad_sums[4], grad_sums[5], grad_sums[6], grad_sums[7], grad_sums[8], grad_sums[9], grad_sums[10], grad_sums[11])
```

```python
import functools
import math

import jax
import jax.numpy as jnp
from jax import lax
from jax.experimental import pallas as pl
from jax.experimental.pallas import tpu as pltpu
from jax.sharding import PartitionSpec as P

EPSILON = 1e-05
HEADS=16; HEAD_DIM=64; NEGATIVE=-1e30
FWD_TILE=(512,1024); BWD_TILE=(1024,1024)
LOG2E=math.log2(math.e); LN2=math.log(2.0)
BF=jnp.bfloat16; F32=jnp.float32
NT=(((1,),(1,)),((),())); TN=(((0,),(0,)),((),())); NN=(((1,),(0,)),((),()))

def dotf(a,b,dims):
    return lax.dot_general(a,b,dims,preferred_element_type=F32)

def split3(v):
    hi=v.astype(BF); r=v-hi.astype(F32); mid=r.astype(BF); lo=(r-mid.astype(F32)).astype(BF)
    return hi.astype(F32),mid.astype(F32),lo.astype(F32)

def with_tail(base, stat):
    lane=lax.broadcasted_iota(jnp.int32, base.shape, 1)
    hi,mid,lo=split3(stat)
    tail=jnp.where(lane==HEAD_DIM,hi,jnp.where(lane==HEAD_DIM+1,mid,jnp.where(lane==HEAD_DIM+2,lo,0.0)))
    return jnp.where(lane<HEAD_DIM,base,tail).astype(BF)

def seg_start(starts, p, segs):
    best=jnp.int32(0)
    for k in range(segs):
        s=starts[k]
        best=jnp.where(s<=p, jnp.maximum(best,s), best)
    return best

def seg_end(starts, p, segs, full):
    best=jnp.int32(full)
    for k in range(segs):
        s=starts[k]
        best=jnp.where(s>p, jnp.minimum(best,s), best)
    return best

def fwd_kernel(starts, part, x_ref, low_ref, out_ref, qa_ref, ka_ref, va_ref, s_ref, *, bq, bk, segs, group):
    i=pl.program_id(0); full=x_ref.shape[0]
    @pl.when(i==0)
    def _():
        step=512
        def build(t,_):
            rows=pl.ds(pl.multiple_of(t*step,step),step)
            head=x_ref[rows,:128].astype(F32)
            tail=x_ref[rows,128:192].astype(F32)
            lane=lax.broadcasted_iota(jnp.int32,(step,128),1)
            mark=jnp.where(lane<HEAD_DIM+3,-1.0,0.0)
            ka_ref[rows,:]=jnp.where(lane<HEAD_DIM,pltpu.roll(head,64,1),mark).astype(BF)
            va_ref[rows,:]=jnp.where(lane<HEAD_DIM,jnp.concatenate([tail,tail],axis=1),mark).astype(BF)
            return 0
        lax.fori_loop(0,full//step,build,0)
    def skip():
        low_ref[...]=jnp.zeros_like(low_ref); out_ref[...]=jnp.zeros_like(out_ref)
        qa_ref[...]=with_tail(jnp.zeros((bq,128),F32),jnp.full((bq,1),1e30,F32))
    def work():
        a=i*bq; last=a+bq-1
        f0=seg_start(starts,a,segs); f1=seg_start(starts,last,segs)
        lo=f0//bk; hi=last//bk+1
        u0=jnp.minimum((f1+bk-1)//bk,hi); u1=jnp.maximum(u0,(a+1)//bk)
        lane=lax.broadcasted_iota(jnp.int32,(bq,128),1)
        qf=x_ref[pl.ds(pl.multiple_of(a,bq),bq),:128].astype(F32)
        q=jnp.where(lane<HEAD_DIM,qf,0.0)
        qb=q.astype(BF)
        row=a+lax.broadcasted_iota(jnp.int32,(bq,1),0)
        first=jnp.zeros((bq,1),jnp.int32)
        for k in range(segs):
            s=starts[k]; first=jnp.where(s<=row,jnp.maximum(first,s),first)
        def score(j,top,masked):
            s=dotf(qb,ka_ref[pl.ds(pl.multiple_of(j*bk,bk),bk),:],NT)
            if masked:
                key=j*bk+lax.broadcasted_iota(jnp.int32,(bq,bk),1)
                s=jnp.where((key<=row)&(key>=first),s,NEGATIVE)
            s_ref[j]=s
            for c in range(bk//128):
                top=jnp.maximum(top,s[:,c*128:(c+1)*128])
            return top
        top=jnp.full((bq,128),NEGATIVE,F32)
        top=lax.fori_loop(lo,u0,lambda j,t:score(j,t,True),top)
        top=lax.fori_loop(u0,u1,lambda j,t:score(j,t,False),top)
        top=lax.fori_loop(u1,hi,lambda j,t:score(j,t,True),top)
        peak=jnp.max(top,axis=1,keepdims=True)
        def gather(j,acc):
            p=jnp.exp2(s_ref[j]-peak).astype(BF)
            return acc+dotf(p,va_ref[pl.ds(pl.multiple_of(j*bk,bk),bk),:],NN)
        acc=lax.fori_loop(lo,hi,gather,jnp.zeros((bq,128),F32))
        total=-acc[:,HEAD_DIM:HEAD_DIM+1]
        out=acc/total
        out_ref[...]=out[:,:HEAD_DIM]
        low_ref[...]=out[:,:HEAD_DIM].astype(BF)
        qa_ref[...]=with_tail(q,peak+jnp.log2(total))
    if group==1: work()
    else:
        own=(i%group)==part[0]
        pl.when(own)(work); pl.when(jnp.logical_not(own))(skip)

def attend(starts, part, x, *, bq, bk, group):
    full=x.shape[0]; segs=starts.shape[0]
    whole=lambda w: pl.BlockSpec((full,w),lambda i,*_:(0,0))
    blk=lambda w: pl.BlockSpec((bq,w),lambda i,*_:(i,0))
    return pl.pallas_call(
        functools.partial(fwd_kernel,bq=bq,bk=bk,segs=segs,group=group),
        grid_spec=pltpu.PrefetchScalarGridSpec(num_scalar_prefetch=2,grid=(full//bq,),
            in_specs=[whole(192)],
            out_specs=[blk(64),blk(64),blk(128),whole(128),whole(128)],
            scratch_shapes=[pltpu.VMEM((full//bk,bq,bk),F32)]),
        out_shape=[jax.ShapeDtypeStruct((full,64),BF),jax.ShapeDtypeStruct((full,64),F32)]+[jax.ShapeDtypeStruct((full,128),BF)]*3,
        compiler_params=pltpu.CompilerParams(vmem_limit_bytes=50<<20),
        cost_estimate=pl.CostEstimate(flops=full*full*512,bytes_accessed=full*1600,transcendentals=full*full//2),
        name="attend")(starts,part,x)

def bwd_kernel(starts, qa_ref, ka_ref, va_ref, do_ref, out_ref, dx_ref, da_ref, dq_ref, kt_ref, *, bq, bk, segs, variant):
    j=pl.program_id(0); full=qa_ref.shape[0]; nq=full//bq
    @pl.when(j==0)
    def _():
        step=512
        def build(t,_):
            rows=pl.ds(pl.multiple_of(t*step,step),step)
            g=do_ref[rows,:].astype(F32)
            delta=jnp.sum(g*out_ref[rows,:],axis=1,keepdims=True)
            da_ref[rows,:]=with_tail(jnp.concatenate([g,g],axis=1),delta)
            return 0
        lax.fori_loop(0,full//step,build,0)
        def trans(t,_):
            if variant==0:
                kt_ref[t]=ka_ref[pl.ds(pl.multiple_of(t*bk,bk),bk),:].astype(F32).T[:HEAD_DIM].astype(BF)
            return 0
        lax.fori_loop(0,full//bk,trans,0)
        def clear(t,_):
            dq_ref[t]=jnp.zeros(dq_ref.shape[1:],F32)
            return 0
        lax.fori_loop(0,nq,clear,0)
    c=j*bk; d=c+bk
    e0=seg_end(starts,c,segs,full); e1=seg_end(starts,d-1,segs,full)
    lo=c//bq; hi=(e1+bq-1)//bq
    u0=jnp.minimum((d-1+bq-1)//bq,hi); u1=jnp.maximum(u0,e0//bq)
    rows=pl.ds(pl.multiple_of(c,bk),bk)
    ka=ka_ref[rows,:]; va=va_ref[rows,:]
    if variant==0: kt=kt_ref[j]
    def step(i,carry,masked):
        dk,dv=carry
        qrows=pl.ds(pl.multiple_of(i*bq,bq),bq)
        qa=qa_ref[qrows,:]; da=da_ref[qrows,:]
        p=jnp.exp2(dotf(ka,qa,NT))
        if masked:
            row=i*bq+lax.broadcasted_iota(jnp.int32,(1,bq),1)
            first=jnp.zeros((1,bq),jnp.int32)
            for k in range(segs):
                s=starts[k]; first=jnp.where(s<=row,jnp.maximum(first,s),first)
            key=c+lax.broadcasted_iota(jnp.int32,(bk,bq),0)
            p=jnp.where((key<=row)&(key>=first),p,0.0)
        dp=dotf(va,da,NT)
        pb=p.astype(BF); ds=(p*dp).astype(BF)
        dv=dv+dotf(pb,da,NN); dk=dk+dotf(ds,qa,NN)
        if variant==0:
            dq_ref[i]+=dotf(kt,ds,NN)
        else:
            dq_ref[i]+=dotf(ds,ka,TN)
        return dk,dv
    z=jnp.zeros((bk,128),F32)
    carry=lax.fori_loop(lo,u0,lambda i,t:step(i,t,True),(z,z))
    carry=lax.fori_loop(u0,u1,lambda i,t:step(i,t,False),carry)
    dk,dv=lax.fori_loop(u1,hi,lambda i,t:step(i,t,True),carry)
    dx_ref[rows,64:128]=(dk[:,:HEAD_DIM]*LN2).astype(BF)
    dx_ref[rows,128:192]=dv[:,:HEAD_DIM].astype(BF)
    @pl.when(j==pl.num_programs(0)-1)
    def _():
        def fin(t,_):
            r=pl.ds(pl.multiple_of(t*bq,bq),bq)
            g=dq_ref[t]
            if variant==0: g=g.T
            dx_ref[r,0:64]=(g[:,:HEAD_DIM]*HEAD_DIM**-0.5).astype(BF)
            return 0
        lax.fori_loop(0,nq,fin,0)

def attend_back(starts, qa, ka, va, do, out, *, bq, bk, variant=0):
    full=qa.shape[0]; segs=starts.shape[0]
    whole=lambda w: pl.BlockSpec((full,w),lambda i,*_:(0,0))
    return pl.pallas_call(
        functools.partial(bwd_kernel,bq=bq,bk=bk,segs=segs,variant=variant),
        grid_spec=pltpu.PrefetchScalarGridSpec(num_scalar_prefetch=1,grid=(full//bk,),
            in_specs=[whole(128)]*3+[whole(64)]*2, out_specs=whole(192),
            scratch_shapes=[pltpu.VMEM((full,128),BF),
              pltpu.VMEM((full//bq,64,bq) if variant==0 else (full//bq,bq,128),F32),pltpu.VMEM((full//bk,64,bk),BF)]),
        out_shape=jax.ShapeDtypeStruct((full,192),BF),
        compiler_params=pltpu.CompilerParams(vmem_limit_bytes=50<<20),
        cost_estimate=pl.CostEstimate(flops=full*full*1280,bytes_accessed=full*2000,transcendentals=full*full//2),
        name="attend_back")(starts,qa,ka,va,do,out)

def statistics(values):
    centre = jnp.mean(values, axis=-1, keepdims=True)
    centred = values - centre
    second = jnp.mean(centred * centred, axis=-1, keepdims=True)
    scale = lax.rsqrt(second + EPSILON)
    return centred * scale, scale


def norm_back(unit, scale, gain, grad):
    scaled = grad * gain
    first = jnp.mean(scaled, axis=-1, keepdims=True)
    second = jnp.mean(scaled * unit, axis=-1, keepdims=True)
    return (scaled - first - unit * second) * scale


def row_sum(value):
    low = lax.optimization_barrier(value.astype(BF))
    if lax.axis_size("row") == 2:
        return low.astype(F32) + lax.ppermute(low, "row", [(0, 1), (1, 0)]).astype(F32)
    return lax.psum(low.astype(F32), "row")


def exchange(value):
    return lax.all_to_all(value, "seq", 0, 0, tiled=True)


def scatter_sum(value):
    return row_sum(lax.psum_scatter(value.astype(BF), "seq", scatter_dimension=0, tiled=True).astype(F32))


def per_device(
    frames,
    seg_lengths,
    ln1_gain,
    ln1_bias,
    w_qkv,
    bias_qv,
    w_out,
    bias_out,
    ln2_gain,
    ln2_bias,
    w_up,
    bias_up,
    w_down,
    bias_down,
    grad_out,
):
    tokens, feature = frames.shape[1:]
    ranks = lax.axis_size("seq")
    me = lax.axis_index("seq")
    group = max(1, ranks // HEADS)
    full = ranks * tokens
    share = feature // ranks
    lengths = seg_lengths[0]
    starts = jnp.cumsum(lengths, dtype=jnp.int32) - lengths
    part = (me % group).astype(jnp.int32)[None]

    def to_heads(value):
        value = value.reshape(tokens, -1, HEADS, HEAD_DIM).transpose(2, 0, 1, 3)
        value = value.reshape(HEADS, tokens, -1)
        return jnp.repeat(value, group, axis=0) if group > 1 else value

    def fold(value):
        if group == 1:
            return value
        value = value.reshape((HEADS, group) + value.shape[1:])
        return jnp.sum(value.astype(F32), axis=1).astype(value.dtype)

    def from_heads(value):
        rows = value.shape[1]
        value = value.reshape(HEADS, rows, -1, HEAD_DIM).transpose(1, 2, 0, 3)
        return value.reshape(rows, -1)

    stream = frames[0].astype(F32)
    unit_one, scale_one = statistics(stream)
    normed_low = (unit_one * ln1_gain + ln1_bias).astype(BF)
    normed_all = lax.all_gather(normed_low, "seq", axis=0, tiled=True)
    bias_full = jnp.concatenate(
        [bias_qv[:feature], jnp.zeros((feature,), F32), bias_qv[feature:]]
    )
    column_scale = jnp.where(lax.iota(jnp.int32, 3 * feature) < feature, LOG2E * HEAD_DIM**-0.5, 1.0)
    projected = ((dotf(normed_low, w_qkv, NN) + bias_full) * column_scale).astype(BF)
    packed = exchange(to_heads(projected)).reshape(full, 3 * HEAD_DIM)
    low, out, qa, ka, va = attend(starts, part, packed, bq=FWD_TILE[0], bk=FWD_TILE[1], group=group)
    attended_low = from_heads(fold(exchange(low.reshape(ranks, tokens, HEAD_DIM))))

    residual = stream + (dotf(attended_low, w_out, NN) + bias_out)
    unit_two, scale_two = statistics(residual)
    normed_two_low = (unit_two * ln2_gain + ln2_bias).astype(BF)
    up_proj = dotf(normed_two_low, w_up, NN) + bias_up
    phi = 0.5 * (1.0 + lax.erf(up_proj * (0.5**0.5)))
    hidden = (up_proj * phi).astype(BF)
    slope = phi + up_proj * jnp.exp(-0.5 * up_proj * up_proj) * (1.0 / math.sqrt(2.0 * math.pi))
    out_frames = (residual + (dotf(hidden, w_down, NN) + bias_down)).astype(BF)
    cot_low = grad_out[0]
    cot = cot_low.astype(F32)
    up_grad = (dotf(cot_low, w_down, NT) * slope).astype(BF)
    normed_two_grad = dotf(up_grad, w_up, NT)
    residual_grad = cot + norm_back(unit_two, scale_two, ln2_gain, normed_two_grad)
    branch_grad = residual_grad.astype(BF)
    attended_grad = dotf(branch_grad, w_out, NT).astype(BF)

    def piece(value):
        return value.reshape(ranks, -1)

    smalls = jnp.concatenate(
        [
            piece(jnp.sum(normed_two_grad * unit_two, axis=0)),
            piece(jnp.sum(normed_two_grad, axis=0)),
            piece(jnp.sum(branch_grad, axis=0, dtype=F32)),
            piece(jnp.sum(up_grad, axis=0, dtype=F32)),
            piece(jnp.sum(cot, axis=0)),
        ],
        axis=1,
    ).astype(BF)
    extra = smalls.shape[1] // HEAD_DIM
    sent = jnp.concatenate([to_heads(attended_grad), smalls.reshape(ranks, extra, HEAD_DIM)], axis=1)
    got = exchange(sent)
    small_total = row_sum(jnp.sum(got[:, tokens:].astype(F32), axis=0).reshape(-1))
    grad_heads = got[:, :tokens].reshape(full, HEAD_DIM)

    total_down = scatter_sum(dotf(hidden, cot_low, TN))
    total_up = scatter_sum(dotf(normed_two_low, up_grad, TN))
    total_out = scatter_sum(dotf(attended_low, branch_grad, TN))

    dx = attend_back(starts, qa, ka, va, grad_heads, out, bq=BWD_TILE[0], bk=BWD_TILE[1])
    projected_grad = from_heads(fold(exchange(dx.reshape(ranks, tokens, 3 * HEAD_DIM))))
    normed_grad = dotf(projected_grad, w_qkv, NT)
    grad_frames = (residual_grad + norm_back(unit_one, scale_one, ln1_gain, normed_grad)).astype(BF)

    columns = jnp.sum(dx, axis=0, dtype=F32)
    columns_high = lax.reduce_precision(columns, 8, 7)
    marks = jnp.stack([columns_high, columns - columns_high] + [jnp.zeros_like(columns)] * 6)
    weight_part = dotf(normed_all, dx, TN).reshape(ranks, share, 3 * HEAD_DIM)
    message = jnp.concatenate(
        [weight_part, jnp.broadcast_to(marks[None], (ranks, 8, 3 * HEAD_DIM))], axis=1
    ).astype(BF)
    mine = from_heads(fold(exchange(message)))
    mine_total = row_sum(mine.astype(F32))
    grad_w_qkv = mine_total[:share]
    column_total = mine_total[share] + mine_total[share + 1]
    grad_bias_qv = jnp.concatenate([column_total[:feature], column_total[2 * feature :]])
    grad_bias_qv = lax.dynamic_slice(grad_bias_qv, (me * 2 * share,), (2 * share,))
    my_rows = lax.dynamic_slice(w_qkv, (me * share, 0), (share, 3 * feature)).astype(F32)
    my_gain = lax.dynamic_slice(ln1_gain, (me * share,), (share,))
    my_bias = lax.dynamic_slice(ln1_bias, (me * share,), (share,))
    grad_ln1_bias = jnp.sum(my_rows * column_total, axis=1)
    grad_ln1_gain = (jnp.sum(my_rows * grad_w_qkv, axis=1) - my_bias * grad_ln1_bias) / my_gain

    wide = w_up.shape[1] // ranks
    ends = [share, 2 * share, 3 * share, 3 * share + wide]
    grad_ln2_gain, grad_ln2_bias, grad_bias_out, grad_bias_up, grad_bias_down = jnp.split(small_total, ends)
    return (
        out_frames[None],
        grad_frames[None],
        grad_ln1_gain,
        grad_ln1_bias,
        grad_w_qkv,
        grad_bias_qv,
        total_out,
        grad_bias_out,
        grad_ln2_gain,
        grad_ln2_bias,
        total_up,
        grad_bias_up,
        total_down,
        grad_bias_down,
    )


def solution(mesh):
    frames_spec = P("row", "seq", None)
    vector, matrix = P("seq"), P("seq", None)
    return jax.shard_map(
        per_device,
        mesh=mesh,
        in_specs=(frames_spec, P("row", None)) + (P(),) * 12 + (frames_spec,),
        out_specs=(
            frames_spec,
            frames_spec,
            vector,
            vector,
            matrix,
            vector,
            matrix,
            vector,
            vector,
            vector,
            matrix,
            vector,
            matrix,
            vector,
        ),
        check_vma=False,
    )
```

```python
import functools
import math

import jax
import jax.numpy as jnp
from jax import lax
from jax.experimental import pallas as pl
from jax.experimental.pallas import tpu as pltpu
from jax.sharding import PartitionSpec as P

EPSILON = 1e-05
HEADS=16; HEAD_DIM=64; NEGATIVE=-1e30
FWD_TILE=(512,1024); BWD_TILE=(1024,1024)
LOG2E=math.log2(math.e); LN2=math.log(2.0)
BF=jnp.bfloat16; F32=jnp.float32
NT=(((1,),(1,)),((),())); TN=(((0,),(0,)),((),())); NN=(((1,),(0,)),((),()))

def dotf(a,b,dims):
    return lax.dot_general(a,b,dims,preferred_element_type=F32)

def split3(v):
    hi=v.astype(BF); r=v-hi.astype(F32); mid=r.astype(BF); lo=(r-mid.astype(F32)).astype(BF)
    return hi.astype(F32),mid.astype(F32),lo.astype(F32)

def with_tail(base, stat):
    lane=lax.broadcasted_iota(jnp.int32, base.shape, 1)
    hi,mid,lo=split3(stat)
    tail=jnp.where(lane==HEAD_DIM,hi,jnp.where(lane==HEAD_DIM+1,mid,jnp.where(lane==HEAD_DIM+2,lo,0.0)))
    return jnp.where(lane<HEAD_DIM,base,tail).astype(BF)

def seg_start(starts, p, segs):
    best=jnp.int32(0)
    for k in range(segs):
        s=starts[k]
        best=jnp.where(s<=p, jnp.maximum(best,s), best)
    return best

def seg_end(starts, p, segs, full):
    best=jnp.int32(full)
    for k in range(segs):
        s=starts[k]
        best=jnp.where(s>p, jnp.minimum(best,s), best)
    return best

def lanes_low(shape):
    return lax.broadcasted_iota(jnp.int32,shape,1)<HEAD_DIM

def pair_up(one, two):
    return jnp.where(lanes_low(one.shape),one,pltpu.roll(two,HEAD_DIM,1))

def pair_down(one, two):
    return jnp.where(lanes_low(one.shape),pltpu.roll(one,HEAD_DIM,1),two)

def fwd_kernel(starts, part, x_ref, low_ref, out_ref, qa_ref, ka_ref, va_ref, s_ref, q_ref, *, bq, bk, segs, group, tokens):
    i=pl.program_id(0); full=q_ref.shape[0]; half=tokens//2
    @pl.when(i==0)
    def _():
        mark=jnp.where(lax.broadcasted_iota(jnp.int32,(tokens,128),1)<HEAD_DIM+3,-1.0,0.0)
        def build(t,_):
            pair=x_ref[t,:tokens,:].astype(F32); v=x_ref[t,tokens:,:].astype(F32)
            rows=pl.ds(pl.multiple_of(t*tokens,tokens),tokens)
            low=lanes_low((tokens,128))
            q_ref[rows,:]=jnp.where(low,pair,0.0).astype(BF)
            ka_ref[rows,:]=jnp.where(low,pltpu.roll(pair,HEAD_DIM,1),mark).astype(BF)
            values=jnp.concatenate([v,pltpu.roll(v,HEAD_DIM,1)],axis=0)
            va_ref[rows,:]=jnp.where(low,values,mark).astype(BF)
            return 0
        lax.fori_loop(0,full//tokens,build,0)
    def skip():
        low_ref[...]=jnp.zeros_like(low_ref); out_ref[...]=jnp.zeros_like(out_ref)
        qa_ref[...]=with_tail(jnp.zeros((bq,128),F32),jnp.full((bq,1),1e30,F32))
    def work():
        a=i*bq; last=a+bq-1
        f0=seg_start(starts,a,segs); f1=seg_start(starts,last,segs)
        lo=f0//bk; hi=last//bk+1
        u0=jnp.minimum((f1+bk-1)//bk,hi); u1=jnp.maximum(u0,(a+1)//bk)
        qb=q_ref[pl.ds(pl.multiple_of(a,bq),bq),:]
        row=a+lax.broadcasted_iota(jnp.int32,(bq,1),0)
        first=jnp.zeros((bq,1),jnp.int32)
        for k in range(segs):
            s=starts[k]; first=jnp.where(s<=row,jnp.maximum(first,s),first)
        def score(j,top,masked):
            s=dotf(qb,ka_ref[pl.ds(pl.multiple_of(j*bk,bk),bk),:],NT)
            if masked:
                key=j*bk+lax.broadcasted_iota(jnp.int32,(bq,bk),1)
                s=jnp.where((key<=row)&(key>=first),s,NEGATIVE)
            s_ref[j]=s
            for c in range(bk//128):
                top=jnp.maximum(top,s[:,c*128:(c+1)*128])
            return top
        top=jnp.full((bq,128),NEGATIVE,F32)
        top=lax.fori_loop(lo,u0,lambda j,t:score(j,t,True),top)
        top=lax.fori_loop(u0,u1,lambda j,t:score(j,t,False),top)
        top=lax.fori_loop(u1,hi,lambda j,t:score(j,t,True),top)
        peak=jnp.max(top,axis=1,keepdims=True)
        def gather(j,acc):
            p=jnp.exp2(s_ref[j]-peak).astype(BF)
            return acc+dotf(p,va_ref[pl.ds(pl.multiple_of(j*bk,bk),bk),:],NN)
        acc=lax.fori_loop(lo,hi,gather,jnp.zeros((bq,128),F32))
        total=-acc[:,HEAD_DIM:HEAD_DIM+1]
        out=jnp.where(lanes_low((bq,128)),acc/total,0.0)
        out_ref[...]=out
        for c in range(bq//tokens):
            mid=c*tokens+half
            low_ref[c]=pair_up(out[c*tokens:mid],out[mid:mid+half]).astype(BF)
        qa_ref[...]=with_tail(qb.astype(F32),peak+jnp.log2(total))
    if group==1: work()
    else:
        own=(i%group)==part[0]
        pl.when(own)(work); pl.when(jnp.logical_not(own))(skip)

def attend(starts, part, x, *, bq, bk, group):
    ranks,rows,_=x.shape; tokens=rows//3*2; full=ranks*tokens; segs=starts.shape[0]
    if group>1: bq=tokens
    whole=lambda w: pl.BlockSpec((full,w),lambda i,*_:(0,0))
    blk=lambda w: pl.BlockSpec((bq,w),lambda i,*_:(i,0))
    return pl.pallas_call(
        functools.partial(fwd_kernel,bq=bq,bk=bk,segs=segs,group=group,tokens=tokens),
        grid_spec=pltpu.PrefetchScalarGridSpec(num_scalar_prefetch=2,grid=(full//bq,),
            in_specs=[pl.BlockSpec(x.shape,lambda i,*_:(0,0,0))],
            out_specs=[pl.BlockSpec((bq//tokens,tokens//2,128),lambda i,*_:(i,0,0)),blk(128),blk(128),whole(128),whole(128)],
            scratch_shapes=[pltpu.VMEM((full//bk,bq,bk),F32),pltpu.VMEM((full,128),BF)]),
        out_shape=[jax.ShapeDtypeStruct((ranks,tokens//2,128),BF),jax.ShapeDtypeStruct((full,128),F32)]+[jax.ShapeDtypeStruct((full,128),BF)]*3,
        compiler_params=pltpu.CompilerParams(vmem_limit_bytes=50<<20),
        cost_estimate=pl.CostEstimate(flops=full*full*512,bytes_accessed=full*1600,transcendentals=full*full//2),
        name="attend")(starts,part,x)

def bwd_kernel(starts, *refs, bq, bk, segs, begin, count, first, last, tokens):
    half=tokens//2
    refs=list(refs)
    qa_ref,ka_ref,va_ref=refs[:3]; refs=refs[3:]
    full=qa_ref.shape[0]; nq=full//bq
    if first:
        do_ref,out_ref=refs[:2]; refs=refs[2:]
    else:
        da_ref,dq_in,early_ref=refs[:3]; refs=refs[3:]
    if last:
        dx_ref,dq_ref,kt_ref,kv_ref=refs[:4]; refs=refs[4:]
        if first: da_ref=refs[0]
    else:
        if first: da_ref,refs=refs[0],refs[1:]
        dq_ref,kv_ref,kt_ref=refs[:3]
    j=pl.program_id(0)
    @pl.when(j==0)
    def _():
        if first:
            def build(t,_):
                rows=pl.ds(pl.multiple_of(t*tokens,tokens),tokens)
                g=do_ref[t,:half,:].astype(F32)
                g=jnp.concatenate([g,pltpu.roll(g,HEAD_DIM,1)],axis=0)
                delta=jnp.sum(g*out_ref[rows,:],axis=1,keepdims=True)
                da_ref[rows,:]=with_tail(g,delta)
                return 0
            lax.fori_loop(0,full//tokens,build,0)
        def clear(t,_):
            dq_ref[t]=jnp.zeros(dq_ref.shape[1:],F32) if first else dq_in[t]
            return 0
        lax.fori_loop(0,nq,clear,0)
        def trans(t,_):
            kt_ref[t]=ka_ref[pl.ds(pl.multiple_of((begin+t)*bk,bk),bk),:].astype(F32).T[:HEAD_DIM].astype(BF)
            return 0
        lax.fori_loop(0,count,trans,0)
    c=(begin+j)*bk; d=c+bk
    e0=seg_end(starts,c,segs,full); e1=seg_end(starts,d-1,segs,full)
    lo=c//bq; hi=(e1+bq-1)//bq
    u0=jnp.minimum((d-1+bq-1)//bq,hi); u1=jnp.maximum(u0,e0//bq)
    rows=pl.ds(pl.multiple_of(c,bk),bk)
    ka=ka_ref[rows,:]; va=va_ref[rows,:]; kt=kt_ref[j]
    def step(i,carry,masked):
        dk,dv=carry
        qrows=pl.ds(pl.multiple_of(i*bq,bq),bq)
        qa=qa_ref[qrows,:]; da=da_ref[qrows,:]
        p=jnp.exp2(dotf(ka,qa,NT))
        if masked:
            row=i*bq+lax.broadcasted_iota(jnp.int32,(1,bq),1)
            first_key=jnp.zeros((1,bq),jnp.int32)
            for k in range(segs):
                s=starts[k]; first_key=jnp.where(s<=row,jnp.maximum(first_key,s),first_key)
            key=c+lax.broadcasted_iota(jnp.int32,(bk,bq),0)
            p=jnp.where((key<=row)&(key>=first_key),p,0.0)
        dp=dotf(va,da,NT)
        pb=p.astype(BF); ds=(p*dp).astype(BF)
        dv=dv+dotf(pb,da,NN); dk=dk+dotf(ds,qa,NN)
        dq_ref[i]+=dotf(kt,ds,NN)
        return dk,dv
    z=jnp.zeros((bk,128),F32)
    carry=lax.fori_loop(lo,u0,lambda i,t:step(i,t,True),(z,z))
    carry=lax.fori_loop(u0,u1,lambda i,t:step(i,t,False),carry)
    dk,dv=lax.fori_loop(u1,hi,lambda i,t:step(i,t,True),carry)
    mine=pair_up(dv,dk*LN2).astype(BF)
    kv_ref[pl.ds(pl.multiple_of(j*bk,bk),bk),:]=mine
    if last:
        @pl.when(j==count-1)
        def _():
            for t in range(nq):
                dq=dq_ref[t].T*HEAD_DIM**-0.5
                dq=jnp.concatenate([dq,dq],axis=1)
                for c in range(bq//tokens):
                    r=t*bq+c*tokens
                    kv=early_ref[r:r+tokens,:] if r<begin*bk else kv_ref[r-begin*bk:r-begin*bk+tokens,:]
                    kv=kv.astype(F32)
                    dx_ref[r//tokens,:tokens,:]=jnp.where(lanes_low(kv.shape),dq[c*tokens:(c+1)*tokens],kv).astype(BF)
                    dx_ref[r//tokens,tokens:,:]=pair_up(kv[:half],kv[half:]).astype(BF)

def attend_back(starts, qa, ka, va, rest, *, bq, bk, begin, count, tokens):
    full=qa.shape[0]; segs=starts.shape[0]
    first=begin==0; last=begin+count==full//bk
    fixed=lambda shape: pl.BlockSpec(shape,lambda i,*_:(0,)*len(shape))
    dq_shape=(full//bq,64,bq); kt=pltpu.VMEM((count,64,bk),BF)
    if last:
        outs=[jax.ShapeDtypeStruct((full//tokens,tokens//2*3,128),BF)]
        scratch=[pltpu.VMEM(dq_shape,F32),kt,pltpu.VMEM((count*bk,128),BF)]
        if first: scratch.append(pltpu.VMEM((full,128),BF))
    else:
        outs=[jax.ShapeDtypeStruct(dq_shape,F32),jax.ShapeDtypeStruct((count*bk,128),BF)]
        if first: outs.insert(0,jax.ShapeDtypeStruct((full,128),BF))
        scratch=[kt]
    area=full*full*(count/(full//bk))
    return pl.pallas_call(
        functools.partial(bwd_kernel,bq=bq,bk=bk,segs=segs,begin=begin,count=count,first=first,last=last,tokens=tokens),
        grid_spec=pltpu.PrefetchScalarGridSpec(num_scalar_prefetch=1,grid=(count,),
            in_specs=[fixed(v.shape) for v in (qa,ka,va)+tuple(rest)],
            out_specs=[fixed(o.shape) for o in outs],
            scratch_shapes=scratch),
        out_shape=outs,
        compiler_params=pltpu.CompilerParams(vmem_limit_bytes=50<<20),
        cost_estimate=pl.CostEstimate(flops=int(area*1280),bytes_accessed=full*2000,transcendentals=int(area/2)),
        name="attend_back")(starts,qa,ka,va,*rest)

def fixed_block(shape):
    return pl.BlockSpec(shape,lambda s,*_:(0,)*len(shape))

def run_kernel(kernel, ids, grid, ins, in_specs, outs, out_specs, scratch, name, flops):
    moved=sum(math.prod(v.shape)*2 for v in ins)+sum(math.prod(o.shape)*2 for o in outs)
    return pl.pallas_call(kernel,
        grid_spec=pltpu.PrefetchScalarGridSpec(num_scalar_prefetch=1,grid=grid,in_specs=in_specs,out_specs=out_specs,scratch_shapes=scratch),
        out_shape=outs,compiler_params=pltpu.CompilerParams(vmem_limit_bytes=50<<20),
        cost_estimate=pl.CostEstimate(flops=flops,bytes_accessed=moved,transcendentals=0),name=name)(ids,*ins)

def pick_kernel(ids, h_ref, *outs, wide):
    for k,out in enumerate(outs):
        other=lax.bitwise_xor(ids[1]*2+ids[0],jnp.int32(k+1))
        for z in range(out.shape[1]//wide):
            out[:,z*wide:(z+1)*wide]=h_ref[:,pl.ds(pl.multiple_of((4*z+other)*wide,wide),wide)]

def pick_blocks(ids, hidden, ranks):
    tokens,inner=hidden.shape; out=jax.ShapeDtypeStruct((tokens,inner//4),hidden.dtype)
    return run_kernel(functools.partial(pick_kernel,wide=inner//ranks),ids,(1,),[hidden],[fixed_block(hidden.shape)],
        [out]*3,[fixed_block(out.shape)]*3,[],"pick_blocks",0)

def down_kernel(ids, *refs):
    lefts,rights,(sent_ref,keep_ref)=refs[:4],refs[4:8],refs[8:]
    s=pl.program_id(0)
    v=dotf(lefts[0][...],rights[0][...],TN)
    for a,b in zip(lefts[1:],rights[1:]): v=v+dotf(a[...],b[...],TN)
    v=v.astype(BF)
    @pl.when(s<2)
    def _(): sent_ref[0]=v
    @pl.when(s>=2)
    def _(): keep_ref[0]=v

def grads_down(ids, hidden, others, cots, ranks):
    tokens,inner=hidden.shape; width=cots[0].shape[1]; wide=inner//ranks
    def level(s,ids): return 2*(s%2)+jnp.where(s<2,1-ids[3],ids[3])
    mine=pl.BlockSpec((tokens,wide),lambda s,ids:(0,4*level(s,ids)+2*ids[1]+ids[0]))
    got=pl.BlockSpec((tokens,wide),lambda s,ids:(0,level(s,ids)))
    shape=jax.ShapeDtypeStruct((2,wide,width),BF)
    return run_kernel(down_kernel,ids,(4,),[hidden,*others,*cots],[mine,got,got,got]+[fixed_block(cots[0].shape)]*4,[shape,shape],
        [pl.BlockSpec((1,wide,width),lambda s,ids:(jnp.minimum(s,1),0,0)),
         pl.BlockSpec((1,wide,width),lambda s,ids:(jnp.maximum(s-2,0),0,0))],[],"grads_down",2*tokens*inner*width)

def up_kernel(ids, n_ref, no_ref, a_ref, ao_ref, ua_ref, uao_ref, ub_ref, ubo_ref, ba_ref, bao_ref, bb_ref, bbo_ref,
              as_ref, ak_ref, bs_ref, bk_ref, ln_ref, la_ref, *, share):
    s=pl.program_id(0); tokens,width=n_ref.shape; tile=width//2
    @pl.when(s==0)
    def _():
        f=lax.broadcasted_iota(jnp.int32,(width,tile),0); j=lax.broadcasted_iota(jnp.int32,(width,tile),1)
        pick=jnp.where(f==(j//share*2+ids[0])*share+j%share,1.0,0.0).astype(BF)
        for ref,pair in ((ln_ref,(n_ref,no_ref)),(la_ref,(a_ref,ao_ref))):
            for e,src in enumerate(pair):
                ref[e*tokens:(e+1)*tokens,:]=dotf(src[...],pick,NN).astype(BF)
    def product(left,one,two):
        return (dotf(left[:tokens],one[...],TN)+dotf(left[tokens:],two[...],TN)).astype(BF)
    def put_a(v):
        v=v.reshape(as_ref.shape[0],2,share,tile)
        low,high=v[:,0],v[:,1]
        cols=pl.ds(pl.multiple_of(s*tile,tile),tile)
        ak_ref[:,:,cols]=jnp.where(ids[1]==0,low,high)
        as_ref[:,:,cols]=jnp.where(ids[1]==0,high,low)
    @pl.when(s<4)
    def _():
        put_a(product(ln_ref,ua_ref,uao_ref))
        v=product(ln_ref,ub_ref,ubo_ref)
        cols=pl.ds(pl.multiple_of(s%2*tile,tile),tile)
        @pl.when(s//2==ids[2])
        def _(): bk_ref[:,cols]=v
        @pl.when(s//2!=ids[2])
        def _(): bs_ref[:,cols]=v
    @pl.when(s==4)
    def _():
        put_a(product(la_ref,ba_ref,bao_ref))
        v=product(la_ref,bb_ref,bbo_ref)
        low,high=v[:,:tile//2],v[:,tile//2:]
        bk_ref[:,2*tile:]=jnp.where(ids[2]==0,low,high)
        bs_ref[:,2*tile:]=jnp.where(ids[2]==0,high,low)

def grads_up(ids, normed, normed_other, att, att_other, up, up_other, branch, branch_other, ranks):
    tokens,width=normed.shape; share=width//ranks; tile=width//2
    f=fixed_block(normed.shape)
    at=lambda base:pl.BlockSpec((tokens,tile),lambda s,ids:(0,base+jnp.minimum(s,3)))
    fix=lambda col:pl.BlockSpec((tokens,tile),lambda s,ids:(0,col))
    a=jax.ShapeDtypeStruct((ranks//4,share,5*tile),BF); b=jax.ShapeDtypeStruct((tile,5*tile//2),BF)
    return run_kernel(functools.partial(up_kernel,share=share),ids,(5,),
        [normed,normed_other,att,att_other,up,up_other,up,up_other,branch,branch_other,branch,branch_other],
        [f,f,f,f,at(0),at(0),at(4),at(4),fix(0),fix(0),fix(1),fix(1)],[a,a,b,b],[fixed_block(v.shape) for v in (a,a,b,b)],
        [pltpu.VMEM((2*tokens,tile),BF)]*2,"grads_up",2*tokens*width*(up.shape[1]+width))

def add_kernel(ids, *refs, plan, joined):
    n=len(plan); ins,outs=refs[:2*n],refs[2*n:]
    for p,(mode,which) in enumerate(plan):
        k_ref,r_ref=ins[2*p:2*p+2]
        def total(index): return (k_ref[index].astype(F32)+r_ref[index].astype(F32)).astype(BF)
        if mode=="sum":
            outs[p][...]=total(...); continue
        for o in range(2):
            half=ids[which] if o else 1-ids[which]
            out=outs[o] if joined else outs[2*p+o]
            for i in range(out.shape[0]):
                if mode=="columns":
                    width=k_ref.shape[2]//2
                    v=total((i,slice(None),pl.ds(pl.multiple_of(half*width,128),width)))
                else:
                    v=total((2*i+half,))
                rows=v.shape[0]
                if joined: out[i,p*rows:(p+1)*rows,:]=v
                else: out[i]=v

def add_split(ids, plan, arrays, name, joined=False):
    shapes=[]
    for p,(mode,_) in enumerate(plan):
        m,r,c=arrays[2*p].shape
        shapes.append((m,r,c) if mode=="sum" else (m,r,c//2) if mode=="columns" else (m//2,r,c))
    if joined: outs=[(shapes[0][0],shapes[0][1]*len(plan),shapes[0][2])]*2
    else: outs=[s for s,(mode,_) in zip(shapes,plan) for _ in range(1 if mode=="sum" else 2)]
    return run_kernel(functools.partial(add_kernel,plan=plan,joined=joined),ids,(1,),arrays,[fixed_block(a.shape) for a in arrays],
        [jax.ShapeDtypeStruct(s,BF) for s in outs],[fixed_block(s) for s in outs],[],name,sum(math.prod(s) for s in outs))

def project_kernel(ids, x_ref, gain_ref, shift_ref, wq_ref, wk_ref, wv_ref, bq_ref, bv_ref, packed_ref, normed_ref):
    tokens=x_ref.shape[0]; half=tokens//2
    @pl.when(pl.program_id(0)==0)
    def _():
        x=x_ref[...].astype(F32)
        x=x-jnp.mean(x,axis=1,keepdims=True)
        x=x*lax.rsqrt(jnp.mean(x*x,axis=1,keepdims=True)+EPSILON)
        normed_ref[...]=(x*gain_ref[...]+shift_ref[...]).astype(BF)
    n=normed_ref[...]
    q=(dotf(n,wq_ref[...],NN)+bq_ref[...])*(LOG2E*HEAD_DIM**-0.5)
    k=dotf(n,wk_ref[...],NN)
    v=dotf(n,wv_ref[...],NN)+bv_ref[...]
    for h in range(q.shape[1]//HEAD_DIM):
        join=pair_down if h%2 else pair_up
        cols=slice(h//2*128,h//2*128+128)
        packed_ref[h,:tokens,:]=join(q[:,cols],k[:,cols]).astype(BF)
        packed_ref[h,tokens:,:]=join(v[:half,cols],v[half:,cols]).astype(BF)

def project(ids, x, gain, shift, w_qkv, bias_qv):
    tokens,width=x.shape; tile=256; steps=width//tile
    w=lambda base:pl.BlockSpec((width,tile),lambda s,ids:(0,base+s))
    c=lambda base:pl.BlockSpec((1,tile),lambda s,ids:(0,base+s))
    outs=[jax.ShapeDtypeStruct((HEADS,tokens//2*3,128),BF),jax.ShapeDtypeStruct((tokens,width),BF)]
    return run_kernel(project_kernel,ids,(steps,),[x,gain[None],shift[None],w_qkv,w_qkv,w_qkv,bias_qv[None],bias_qv[None]],
        [fixed_block(x.shape)]+[fixed_block((1,width))]*2+[w(0),w(steps),w(2*steps),c(0),c(steps)],outs,
        [pl.BlockSpec((tile//HEAD_DIM,tokens//2*3,128),lambda s,ids:(s,0,0)),fixed_block((tokens,width))],[],"project",6*tokens*width*width)

def unpack_tile(one, two):
    return jnp.concatenate([pair_up(one,two),pair_down(one,two)],axis=0)

def mix_kernel(ids, got_ref, w_ref, x_ref, bias_ref, gain_ref, shift_ref, left_ref, res_ref):
    s=pl.program_id(0); width=x_ref.shape[1]
    tiles=[unpack_tile(got_ref[2*p].astype(F32),got_ref[2*p+1].astype(F32)).astype(BF) for p in range(2)]
    att=jnp.concatenate(tiles,axis=1)
    left_ref[:,pl.ds(pl.multiple_of(width+s*256,256),256)]=att
    @pl.when(s==0)
    def _(): res_ref[...]=x_ref[...].astype(F32)+bias_ref[...]
    res_ref[...]+=dotf(att,w_ref[...],NN)
    @pl.when(s==pl.num_programs(0)-1)
    def _():
        x=res_ref[...]
        x=x-jnp.mean(x,axis=1,keepdims=True)
        x=x*lax.rsqrt(jnp.mean(x*x,axis=1,keepdims=True)+EPSILON)
        left_ref[:,:width]=(x*gain_ref[...]+shift_ref[...]).astype(BF)

def mix(ids, got, w_out, x, bias, gain, shift):
    tokens,width=x.shape; row=fixed_block((1,width))
    return run_kernel(mix_kernel,ids,(width//256,),[got,w_out,x,bias[None],gain[None],shift[None]],
        [pl.BlockSpec((4,tokens//2,128),lambda s,ids:(s,0,0)),pl.BlockSpec((256,width),lambda s,ids:(s,0)),fixed_block(x.shape),row,row,row],
        [jax.ShapeDtypeStruct((tokens,2*width),BF),jax.ShapeDtypeStruct((tokens,width),F32)],
        [fixed_block((tokens,2*width)),fixed_block((tokens,width))],[],"mix",2*tokens*width*width)

def grad_pack_kernel(ids, g_ref, w_ref, small_ref, out_ref):
    half=g_ref.shape[0]//2
    g=dotf(g_ref[...],w_ref[...],NT)
    for h in range(4):
        join=pair_down if h%2 else pair_up
        cols=slice(h//2*128,h//2*128+128)
        out_ref[h,:half,:]=join(g[:half,cols],g[half:,cols]).astype(BF)
    out_ref[:,half:,:]=small_ref[...]

def grad_pack(ids, g, w_out, smalls):
    tokens,width=g.shape; rows=tokens//2+smalls.shape[1]
    return run_kernel(grad_pack_kernel,ids,(width//256,),[g,w_out,smalls],
        [fixed_block(g.shape),pl.BlockSpec((256,width),lambda s,ids:(s,0)),pl.BlockSpec((4,)+smalls.shape[1:],lambda s,ids:(s,0,0))],
        [jax.ShapeDtypeStruct((HEADS,rows,128),BF)],[pl.BlockSpec((4,rows,128),lambda s,ids:(s,0,0))],[],"grad_pack",2*tokens*width*width)[0]

def message_kernel(ids, n_ref, dx_ref, out_ref, acc_ref, sum_ref, *, tokens, share):
    s=pl.program_id(0); half=tokens//2
    sides=[]
    for c in range(dx_ref.shape[0]):
        v=dx_ref[c,tokens:,:].astype(F32)
        v=jnp.concatenate([v,pltpu.roll(v,HEAD_DIM,1)],axis=0)
        v=jnp.where(lanes_low(v.shape),v,0.0).astype(BF)
        sides.append(jnp.concatenate([dx_ref[c,:tokens,:],v],axis=1))
    side=jnp.concatenate(sides,axis=0)
    @pl.when(s==0)
    def _():
        acc_ref[...]=jnp.zeros_like(acc_ref); sum_ref[...]=jnp.zeros_like(sum_ref)
    acc_ref[...]+=dotf(n_ref[...],side,TN)
    sum_ref[...]+=jnp.sum(side.astype(F32).reshape(-1,8,256),axis=0)
    @pl.when(s==pl.num_programs(0)-1)
    def _():
        total=jnp.sum(sum_ref[...],axis=0,keepdims=True)
        high=total.astype(BF).astype(F32); rest=total-high
        line=lax.broadcasted_iota(jnp.int32,(16,128),0)
        extra=jnp.where(line==0,high[:,:128],jnp.where(line==1,rest[:,:128],jnp.where(line==2,high[:,128:],jnp.where(line==3,rest[:,128:],0.0))))
        for r in range(out_ref.shape[0]):
            rows=slice(r*share,(r+1)*share)
            out_ref[r,:share,:]=acc_ref[rows,:128].astype(BF)
            v=acc_ref[rows,128:]
            out_ref[r,share:share+share//2,:]=pair_up(v[:share//2],v[share//2:]).astype(BF)
            out_ref[r,share+share//2:,:]=extra.astype(BF)

def weight_message(ids, normed_all, dx):
    ranks,rows,_=dx.shape; tokens=rows//3*2; full,width=normed_all.shape; share=width//ranks
    step=4; shape=(ranks,share//2*3+16,128)
    return run_kernel(functools.partial(message_kernel,tokens=tokens,share=share),ids,(ranks//step,),[normed_all,dx],
        [pl.BlockSpec((step*tokens,width),lambda s,ids:(s,0)),pl.BlockSpec((step,rows,128),lambda s,ids:(s,0,0))],
        [jax.ShapeDtypeStruct(shape,BF)],[fixed_block(shape)],
        [pltpu.VMEM((width,256),F32),pltpu.VMEM((8,256),F32)],"weight_message",2*full*width*192)[0]

def finish_kernel(ids, one_ref, two_ref, w_ref, gain_ref, shift_ref, grad_ref, cols_ref, lg_ref, lb_ref):
    share=grad_ref.shape[0]; width=grad_ref.shape[1]//3
    first=jnp.zeros((share,128),F32); second=jnp.zeros((share,128),F32)
    def both(h): return one_ref[h].astype(F32)+two_ref[h].astype(F32)
    for p in range(HEADS//2):
        a,b=both(2*p),both(2*p+1)
        end=share+share//2
        q=pair_up(a[:share],b[:share]); k=pair_down(a[:share],b[:share])
        v=unpack_tile(a[share:end],b[share:end])
        la=a[end:end+8],b[end:end+8]
        cq=pair_up(*la); ck=pair_down(*la)
        for base,tile,col in ((0,q,cq[0:1]+cq[1:2]),(width,k,ck[0:1]+ck[1:2]),(2*width,v,cq[2:3]+cq[3:4])):
            at=slice(base+p*128,base+p*128+128)
            w=w_ref[:,at].astype(F32)
            grad_ref[:,at]=tile; cols_ref[:,at]=col
            first=first+w*tile; second=second+w*col
    bias=jnp.sum(second,axis=1,keepdims=True)
    lb_ref[...]=bias
    lg_ref[...]=(jnp.sum(first,axis=1,keepdims=True)-shift_ref[...]*bias)/gain_ref[...]

def finish(ids, one, two, w_qkv, gain, shift, ranks):
    width=w_qkv.shape[0]; share=width//ranks
    mine=lambda c:pl.BlockSpec((share,c),lambda s,ids:(ids[5],0))
    outs=[jax.ShapeDtypeStruct(s,F32) for s in ((share,3*width),(1,3*width),(share,1),(share,1))]
    return run_kernel(finish_kernel,ids,(1,),[one,two,w_qkv,gain[:,None],shift[:,None]],
        [fixed_block(one.shape)]*2+[mine(3*width),mine(1),mine(1)],outs,[fixed_block(o.shape) for o in outs],[],"finish",share*width*12)

def input_kernel(ids, got_ref, wq_ref, wk_ref, wv_ref, x_ref, gain_ref, res_ref, out_ref, acc_ref):
    s=pl.program_id(0); tokens=x_ref.shape[0]
    @pl.when(s==0)
    def _(): acc_ref[...]=jnp.zeros_like(acc_ref)
    q,k,v=[],[],[]
    for p in range(2):
        a,b=got_ref[2*p].astype(F32),got_ref[2*p+1].astype(F32)
        q.append(pair_up(a[:tokens],b[:tokens])); k.append(pair_down(a[:tokens],b[:tokens]))
        v.append(unpack_tile(a[tokens:],b[tokens:]))
    total=acc_ref[...]
    for tiles,w_ref in ((q,wq_ref),(k,wk_ref),(v,wv_ref)):
        total=total+dotf(jnp.concatenate(tiles,axis=1).astype(BF),w_ref[...],NT)
    acc_ref[...]=total
    @pl.when(s==pl.num_programs(0)-1)
    def _():
        x=x_ref[...].astype(F32)
        x=x-jnp.mean(x,axis=1,keepdims=True)
        scale=lax.rsqrt(jnp.mean(x*x,axis=1,keepdims=True)+EPSILON)
        x=x*scale
        g=acc_ref[...]*gain_ref[...]
        g=(g-jnp.mean(g,axis=1,keepdims=True)-x*jnp.mean(g*x,axis=1,keepdims=True))*scale
        out_ref[...]=(res_ref[...]+g).astype(BF)

def input_grad(ids, got, w_qkv, x, gain, residual_grad):
    tokens,width=x.shape; steps=width//256
    w=lambda base:pl.BlockSpec((width,256),lambda s,ids:(0,base+s))
    return run_kernel(input_kernel,ids,(steps,),[got,w_qkv,w_qkv,w_qkv,x,gain[None],residual_grad],
        [pl.BlockSpec((4,)+got.shape[1:],lambda s,ids:(s,0,0)),w(0),w(steps),w(2*steps),fixed_block(x.shape),fixed_block((1,width)),fixed_block(x.shape)],
        [jax.ShapeDtypeStruct((tokens,width),BF)],[fixed_block((tokens,width))],[pltpu.VMEM((tokens,width),F32)],"input_grad",6*tokens*width*width)[0]

def statistics(values):
    centre = jnp.mean(values, axis=-1, keepdims=True)
    centred = values - centre
    second = jnp.mean(centred * centred, axis=-1, keepdims=True)
    scale = lax.rsqrt(second + EPSILON)
    return centred * scale, scale


def norm_back(unit, scale, gain, grad):
    scaled = grad * gain
    first = jnp.mean(scaled, axis=-1, keepdims=True)
    second = jnp.mean(scaled * unit, axis=-1, keepdims=True)
    return (scaled - first - unit * second) * scale


def row_sum(value):
    low = lax.optimization_barrier(value.astype(BF))
    if lax.axis_size("row") == 2:
        return low.astype(F32) + lax.ppermute(low, "row", [(0, 1), (1, 0)]).astype(F32)
    return lax.psum(low.astype(F32), "row")


def exchange(value):
    return lax.all_to_all(value, "seq", 0, 0, tiled=True)


def swap(value, bit):
    return lax.ppermute(value, "seq", [(i, i ^ bit) for i in range(lax.axis_size("seq"))])


def swap_row(value):
    return lax.ppermute(value, "row", [(0, 1), (1, 0)])


def half_step(value, axis, mine, move):
    keep = lax.dynamic_index_in_dim(value, mine, axis, keepdims=False)
    sent = lax.dynamic_index_in_dim(value, 1 - mine, axis, keepdims=False)
    return (keep.astype(F32) + move(sent).astype(F32)).astype(BF)


def outer_steps(value):
    me, bit = lax.axis_index("seq"), 4
    while value.shape[0] > 1:
        value = value.reshape((value.shape[0] // 2, 2) + value.shape[1:])
        value = half_step(value, 1, me // bit % 2, lambda v, bit=bit: swap(v, bit))
        bit *= 2
    return value[0]


def row_join(value):
    other = swap_row(value)
    first = lax.axis_index("row") == 0
    return jnp.where(first, value, other).astype(F32), jnp.where(first, other, value).astype(F32)


def per_device(
    frames,
    seg_lengths,
    ln1_gain,
    ln1_bias,
    w_qkv,
    bias_qv,
    w_out,
    bias_out,
    ln2_gain,
    ln2_bias,
    w_up,
    bias_up,
    w_down,
    bias_down,
    grad_out,
):
    tokens, feature = frames.shape[1:]
    ranks = lax.axis_size("seq")
    me = lax.axis_index("seq")
    group = max(1, ranks // HEADS)
    full = ranks * tokens
    share = feature // ranks
    lengths = seg_lengths[0]
    starts = jnp.cumsum(lengths, dtype=jnp.int32) - lengths
    part = (me % group).astype(jnp.int32)[None]

    def spread(value):
        return jnp.repeat(value, group, axis=0) if group > 1 else value

    def fold(value):
        if group == 1:
            return value
        value = value.reshape((HEADS, group) + value.shape[1:])
        return jnp.sum(value.astype(F32), axis=1).astype(value.dtype)

    place = [me % 2, me // 2 % 2, lax.axis_index("row"), me // 4 % 2, me // 8 % 2, me]
    ids = jnp.stack(place).astype(jnp.int32)
    packed, normed_low = project(ids, frames[0], ln1_gain, ln1_bias, w_qkv, bias_qv)
    packed = exchange(spread(packed))
    cot_low = grad_out[0]
    fast = ranks == 16 and lax.axis_size("row") == 2
    if fast:
        cot_two = swap(cot_low, 2)
        cots = [cot_low, swap(cot_low, 1), cot_two, swap(cot_two, 1)]
        cots, packed = lax.optimization_barrier((cots, packed))
    gather = lambda v: lax.all_gather(v, "seq", axis=0, tiled=True)
    normed_low, packed = lax.optimization_barrier((normed_low, packed))
    normed_all = gather(normed_low)
    low, out, qa, ka, va = attend(starts, part, packed, bq=FWD_TILE[0], bk=FWD_TILE[1], group=group)
    left, residual = mix(ids, fold(exchange(low)), w_out, frames[0], bias_out, ln2_gain, ln2_bias)
    normed_two_low, attended_low = left[:, :feature], left[:, feature:]
    unit_two, scale_two = statistics(residual)
    up_proj = dotf(normed_two_low, w_up, NN) + bias_up
    phi = 0.5 * (1.0 + lax.erf(up_proj * (0.5**0.5)))
    hidden = (up_proj * phi).astype(BF)
    slope = phi + up_proj * jnp.exp(-0.5 * up_proj * up_proj) * (1.0 / math.sqrt(2.0 * math.pi))
    out_frames = (residual + (dotf(hidden, w_down, NN) + bias_down)).astype(BF)
    cot = cot_low.astype(F32)
    if fast:
        picked, cot_low = lax.optimization_barrier((pick_blocks(ids, hidden, ranks), cot_low))
    up_grad = (dotf(cot_low, w_down, NT) * slope).astype(BF)
    normed_two_grad = dotf(up_grad, w_up, NT)
    residual_grad = cot + norm_back(unit_two, scale_two, ln2_gain, normed_two_grad)
    branch_grad = residual_grad.astype(BF)

    def piece(value):
        return value.reshape(ranks, -1)

    smalls = jnp.concatenate(
        [
            piece(jnp.sum(normed_two_grad * unit_two, axis=0)),
            piece(jnp.sum(normed_two_grad, axis=0)),
            piece(jnp.sum(branch_grad, axis=0, dtype=F32)),
            piece(jnp.sum(up_grad, axis=0, dtype=F32)),
            piece(jnp.sum(cot, axis=0)),
        ],
        axis=1,
    ).astype(BF)
    smalls = smalls.reshape(ranks, -1, 128)
    lines = smalls.shape[1]
    smalls = jnp.pad(smalls, ((0, 0), (0, 16 - lines), (0, 0)))
    if group == 1:
        sent = grad_pack(ids, branch_grad, w_out, smalls)
    else:
        sent = grad_pack(ids, branch_grad, w_out, jnp.zeros((HEADS, 16, 128), BF))
        sent = jnp.concatenate([spread(sent[:, : tokens // 2]), smalls], axis=1)
    sent, normed_all = lax.optimization_barrier((sent, normed_all))
    got = exchange(sent)
    small_total = row_sum(jnp.sum(got[:, tokens // 2 : tokens // 2 + lines].astype(F32), axis=0).reshape(-1))

    back = functools.partial(attend_back, starts, qa, ka, va, bq=BWD_TILE[0], bk=BWD_TILE[1], tokens=tokens)
    tiles = full // BWD_TILE[1]
    if fast:
        others = [swap(v, k + 1) for k, v in enumerate(picked)]
        others, up_grad, _ = lax.optimization_barrier((others, up_grad, sent))
        down_sent, down_keep = grads_down(ids, hidden, others, cots, ranks)
        down_got = swap(down_sent, 4)
        a_sent, a_keep, b_sent, b_keep = grads_up(
            ids,
            normed_two_low,
            swap(normed_two_low, 1),
            attended_low,
            swap(attended_low, 1),
            up_grad,
            swap(up_grad, 1),
            branch_grad,
            swap(branch_grad, 1),
            ranks,
        )
        a_got, b_got = swap(a_sent, 2), swap_row(b_sent)
        one = back((got, out), begin=0, count=tiles // 4)
        a_got, b_got, down_got, one = lax.optimization_barrier((a_got, b_got, down_got, one))
        blocks = lambda v: v.reshape(ranks // 2, share, -1)
        a_sent, a_keep, b_sent, b_keep, down_sent, down_keep = add_split(
            ids,
            (("columns", 2), ("blocks", 1), ("blocks", 4)),
            [a_keep, a_got, blocks(b_keep), blocks(b_got), down_keep, down_got],
            "add_one",
        )
        one, a_sent, b_sent, down_sent = lax.optimization_barrier((one, a_sent, b_sent, down_sent))
        a_got, b_got, down_got = swap_row(a_sent), swap(b_sent, 2), swap(down_sent, 8)
        two = back(one, begin=tiles // 4, count=tiles // 4)
        two = [one[0], two[0], jnp.concatenate([one[2], two[1]], axis=0)]
        a_got, b_got, two = lax.optimization_barrier((a_got, b_got, two))
        up_sent, up_keep = add_split(
            ids, (("blocks", 3), ("blocks", 3)), [a_keep, a_got, b_keep, b_got], "add_two", joined=True
        )
        two, up_sent = lax.optimization_barrier((two, up_sent))
        up_got = swap(up_sent, 4)
        (dx,) = back(two, begin=tiles // 2, count=tiles // 2)
        up_got, down_got, dx = lax.optimization_barrier((up_got, down_got, dx))
        message = weight_message(ids, normed_all, dx)
        up_got, down_got, message = lax.optimization_barrier((up_got, down_got, message))
        up_sent, up_keep, down_sent, down_keep = add_split(
            ids, (("blocks", 4), ("columns", 2)), [up_keep, up_got, down_keep, down_got], "add_three"
        )
        down_got = swap_row(down_sent)
        dx_got = exchange(dx)
        up_sent, dx_got = lax.optimization_barrier((up_sent, dx_got))
        up_got = swap(up_sent, 8)
        up_part, down_part = add_split(
            ids, (("sum", 0), ("sum", 0)), [up_keep, up_got, down_keep, down_got], "add_four"
        )
        total_down = jnp.concatenate(row_join(down_part[0]), axis=1)
        one_half, other_half = row_join(up_part[0])
        width = feature
        rows_a, rows_b = slice(0, share), slice(share, 2 * share)
        total_up = jnp.concatenate(
            [
                one_half[rows_a],
                other_half[rows_a, : 3 * width // 4],
                one_half[rows_b, :width],
                other_half[rows_b, :width],
            ],
            axis=1,
        )
        total_out = jnp.concatenate(
            [other_half[rows_a, 3 * width // 4 :], one_half[rows_b, width:], other_half[rows_b, width:]], axis=1
        )
    else:
        core, across = me % 2, me // 2 % 2

        def halves(value):
            parts = value.reshape(tokens, ranks // 2, 2, -1)
            keep = lax.dynamic_index_in_dim(parts, core, 2, keepdims=False).reshape(tokens, -1)
            sent = lax.dynamic_index_in_dim(parts, 1 - core, 2, keepdims=False).reshape(tokens, -1)
            return jnp.concatenate([keep, swap(sent, 1)], axis=0)

        def both(value):
            return jnp.concatenate([value, swap(value, 1)], axis=0)

        def reduced(value):
            value = value.astype(BF).reshape(ranks // 4, 2, -1, value.shape[-1])
            return row_sum(outer_steps(half_step(value, 1, across, lambda v: swap(v, 2))))

        total_down = reduced(dotf(halves(hidden), both(cot_low), TN))
        total_up = reduced(dotf(halves(normed_two_low), both(up_grad), TN))
        total_out = reduced(dotf(halves(attended_low), both(branch_grad), TN))
        (dx,) = back((got, out), begin=0, count=tiles)
        dx_got = exchange(dx)
        message = weight_message(ids, normed_all, dx)
    message, dx_got = lax.optimization_barrier((message, dx_got))
    grad_frames = input_grad(ids, fold(dx_got), w_qkv, frames[0], ln1_gain, residual_grad)
    mine = fold(exchange(message))
    if lax.axis_size("row") == 2:
        theirs = swap_row(mine)
    else:
        mine = lax.psum(mine.astype(F32), "row")
        theirs = jnp.zeros_like(mine)
    grad_w_qkv, column_total, grad_ln1_gain, grad_ln1_bias = finish(ids, mine, theirs, w_qkv, ln1_gain, ln1_bias, ranks)
    grad_ln1_gain, grad_ln1_bias = grad_ln1_gain[:, 0], grad_ln1_bias[:, 0]
    grad_bias_qv = jnp.concatenate([column_total[0, :feature], column_total[0, 2 * feature :]])
    grad_bias_qv = lax.dynamic_slice(grad_bias_qv, (me * 2 * share,), (2 * share,))

    wide = w_up.shape[1] // ranks
    ends = [share, 2 * share, 3 * share, 3 * share + wide]
    grad_ln2_gain, grad_ln2_bias, grad_bias_out, grad_bias_up, grad_bias_down = jnp.split(small_total, ends)
    return (
        out_frames[None],
        grad_frames[None],
        grad_ln1_gain,
        grad_ln1_bias,
        grad_w_qkv,
        grad_bias_qv,
        total_out,
        grad_bias_out,
        grad_ln2_gain,
        grad_ln2_bias,
        total_up,
        grad_bias_up,
        total_down,
        grad_bias_down,
    )


def solution(mesh):
    frames_spec = P("row", "seq", None)
    vector, matrix = P("seq"), P("seq", None)
    return jax.shard_map(
        per_device,
        mesh=mesh,
        in_specs=(frames_spec, P("row", None)) + (P(),) * 12 + (frames_spec,),
        out_specs=(
            frames_spec,
            frames_spec,
            vector,
            vector,
            matrix,
            vector,
            matrix,
            vector,
            vector,
            vector,
            matrix,
            vector,
            matrix,
            vector,
        ),
        check_vma=False,
    )
```

```python
import functools
import math

import jax
import jax.numpy as jnp
from jax import lax
from jax.experimental import pallas as pl
from jax.experimental.pallas import tpu as pltpu
from jax.sharding import PartitionSpec as P

EPSILON = 1e-05
HEADS=16; HEAD_DIM=64; NEGATIVE=-1e30
FWD_TILE=(512,1024); BWD_TILE=(1024,1024)
LOG2E=math.log2(math.e); LN2=math.log(2.0)
BF=jnp.bfloat16; F32=jnp.float32
NT=(((1,),(1,)),((),())); TN=(((0,),(0,)),((),())); NN=(((1,),(0,)),((),()))

def dotf(a,b,dims):
    return lax.dot_general(a,b,dims,preferred_element_type=F32)

def split3(v):
    hi=v.astype(BF); r=v-hi.astype(F32); mid=r.astype(BF); lo=(r-mid.astype(F32)).astype(BF)
    return hi.astype(F32),mid.astype(F32),lo.astype(F32)

def with_tail(base, stat):
    lane=lax.broadcasted_iota(jnp.int32, base.shape, 1)
    hi,mid,lo=split3(stat)
    tail=jnp.where(lane==HEAD_DIM,hi,jnp.where(lane==HEAD_DIM+1,mid,jnp.where(lane==HEAD_DIM+2,lo,0.0)))
    return jnp.where(lane<HEAD_DIM,base,tail).astype(BF)

def seg_start(starts, p, segs):
    best=jnp.int32(0)
    for k in range(segs):
        s=starts[k]
        best=jnp.where(s<=p, jnp.maximum(best,s), best)
    return best

def seg_end(starts, p, segs, full):
    best=jnp.int32(full)
    for k in range(segs):
        s=starts[k]
        best=jnp.where(s>p, jnp.minimum(best,s), best)
    return best

def lanes_low(shape):
    return lax.broadcasted_iota(jnp.int32,shape,1)<HEAD_DIM

def pair_up(one, two):
    return jnp.where(lanes_low(one.shape),one,pltpu.roll(two,HEAD_DIM,1))

def pair_down(one, two):
    return jnp.where(lanes_low(one.shape),pltpu.roll(one,HEAD_DIM,1),two)

def fwd_kernel(starts, part, x_ref, low_ref, out_ref, qa_ref, ka_ref, va_ref, s_ref, q_ref, *, bq, bk, segs, group, tokens):
    i=pl.program_id(0); full=q_ref.shape[0]; half=tokens//2
    @pl.when(i==0)
    def _():
        mark=jnp.where(lax.broadcasted_iota(jnp.int32,(tokens,128),1)<HEAD_DIM+3,-1.0,0.0)
        def build(t,_):
            pair=x_ref[t,:tokens,:].astype(F32); v=x_ref[t,tokens:,:].astype(F32)
            rows=pl.ds(pl.multiple_of(t*tokens,tokens),tokens)
            low=lanes_low((tokens,128))
            q_ref[rows,:]=jnp.where(low,pair,0.0).astype(BF)
            ka_ref[rows,:]=jnp.where(low,pltpu.roll(pair,HEAD_DIM,1),mark).astype(BF)
            values=jnp.concatenate([v,pltpu.roll(v,HEAD_DIM,1)],axis=0)
            va_ref[rows,:]=jnp.where(low,values,mark).astype(BF)
            return 0
        lax.fori_loop(0,full//tokens,build,0)
    def skip():
        low_ref[...]=jnp.zeros_like(low_ref); out_ref[...]=jnp.zeros_like(out_ref)
        qa_ref[...]=with_tail(jnp.zeros((bq,128),F32),jnp.full((bq,1),1e30,F32))
    def work():
        a=i*bq; last=a+bq-1
        f0=seg_start(starts,a,segs); f1=seg_start(starts,last,segs)
        lo=f0//bk; hi=last//bk+1
        u0=jnp.minimum((f1+bk-1)//bk,hi); u1=jnp.maximum(u0,(a+1)//bk)
        qb=q_ref[pl.ds(pl.multiple_of(a,bq),bq),:]
        row=a+lax.broadcasted_iota(jnp.int32,(bq,1),0)
        first=jnp.zeros((bq,1),jnp.int32)
        for k in range(segs):
            s=starts[k]; first=jnp.where(s<=row,jnp.maximum(first,s),first)
        def score(j,top,masked):
            s=dotf(qb,ka_ref[pl.ds(pl.multiple_of(j*bk,bk),bk),:],NT)
            if masked:
                key=j*bk+lax.broadcasted_iota(jnp.int32,(bq,bk),1)
                s=jnp.where((key<=row)&(key>=first),s,NEGATIVE)
            s_ref[j]=s
            for c in range(bk//128):
                top=jnp.maximum(top,s[:,c*128:(c+1)*128])
            return top
        top=jnp.full((bq,128),NEGATIVE,F32)
        top=lax.fori_loop(lo,u0,lambda j,t:score(j,t,True),top)
        top=lax.fori_loop(u0,u1,lambda j,t:score(j,t,False),top)
        top=lax.fori_loop(u1,hi,lambda j,t:score(j,t,True),top)
        peak=jnp.max(top,axis=1,keepdims=True)
        def gather(j,acc):
            p=jnp.exp2(s_ref[j]-peak).astype(BF)
            return acc+dotf(p,va_ref[pl.ds(pl.multiple_of(j*bk,bk),bk),:],NN)
        acc=lax.fori_loop(lo,hi,gather,jnp.zeros((bq,128),F32))
        total=-acc[:,HEAD_DIM:HEAD_DIM+1]
        out=jnp.where(lanes_low((bq,128)),acc/total,0.0)
        out_ref[...]=out
        for c in range(bq//tokens):
            mid=c*tokens+half
            low_ref[c]=pair_up(out[c*tokens:mid],out[mid:mid+half]).astype(BF)
        qa_ref[...]=with_tail(qb.astype(F32),peak+jnp.log2(total))
    if group==1: work()
    else:
        own=(i%group)==part[0]
        pl.when(own)(work); pl.when(jnp.logical_not(own))(skip)

def attend(starts, part, x, *, bq, bk, group):
    ranks,rows,_=x.shape; tokens=rows//3*2; full=ranks*tokens; segs=starts.shape[0]
    if group>1: bq=tokens
    whole=lambda w: pl.BlockSpec((full,w),lambda i,*_:(0,0))
    blk=lambda w: pl.BlockSpec((bq,w),lambda i,*_:(i,0))
    return pl.pallas_call(
        functools.partial(fwd_kernel,bq=bq,bk=bk,segs=segs,group=group,tokens=tokens),
        grid_spec=pltpu.PrefetchScalarGridSpec(num_scalar_prefetch=2,grid=(full//bq,),
            in_specs=[pl.BlockSpec(x.shape,lambda i,*_:(0,0,0))],
            out_specs=[pl.BlockSpec((bq//tokens,tokens//2,128),lambda i,*_:(i,0,0)),blk(128),blk(128),whole(128),whole(128)],
            scratch_shapes=[pltpu.VMEM((full//bk,bq,bk),F32),pltpu.VMEM((full,128),BF)]),
        out_shape=[jax.ShapeDtypeStruct((ranks,tokens//2,128),BF),jax.ShapeDtypeStruct((full,128),F32)]+[jax.ShapeDtypeStruct((full,128),BF)]*3,
        compiler_params=pltpu.CompilerParams(vmem_limit_bytes=full//1024*(22<<18)),
        cost_estimate=pl.CostEstimate(flops=full*full*512,bytes_accessed=full*1600,transcendentals=full*full//2),
        name="attend")(starts,part,x)

def bwd_kernel(starts, *refs, bq, bk, segs, begin, count, first, last, tokens):
    half=tokens//2
    refs=list(refs)
    qa_ref,ka_ref,va_ref=refs[:3]; refs=refs[3:]
    full=qa_ref.shape[0]; nq=full//bq
    if first:
        do_ref,out_ref=refs[:2]; refs=refs[2:]
    else:
        da_ref,dq_in,early_ref=refs[:3]; refs=refs[3:]
    if last:
        dx_ref,dq_ref,kt_ref,kv_ref=refs[:4]; refs=refs[4:]
        if first: da_ref=refs[0]
    else:
        if first: da_ref,refs=refs[0],refs[1:]
        dq_ref,kv_ref,kt_ref=refs[:3]
    j=pl.program_id(0)
    @pl.when(j==0)
    def _():
        if first:
            def build(t,_):
                rows=pl.ds(pl.multiple_of(t*tokens,tokens),tokens)
                g=do_ref[t,:half,:].astype(F32)
                g=jnp.concatenate([g,pltpu.roll(g,HEAD_DIM,1)],axis=0)
                delta=jnp.sum(g*out_ref[rows,:],axis=1,keepdims=True)
                da_ref[rows,:]=with_tail(g,delta)
                return 0
            lax.fori_loop(0,full//tokens,build,0)
        def clear(t,_):
            dq_ref[t]=jnp.zeros(dq_ref.shape[1:],F32) if first else dq_in[t]
            return 0
        lax.fori_loop(0,nq,clear,0)
        def trans(t,_):
            kt_ref[t]=ka_ref[pl.ds(pl.multiple_of((begin+t)*bk,bk),bk),:].astype(F32).T[:HEAD_DIM].astype(BF)
            return 0
        lax.fori_loop(0,count,trans,0)
    c=(begin+j)*bk; d=c+bk
    e0=seg_end(starts,c,segs,full); e1=seg_end(starts,d-1,segs,full)
    lo=c//bq; hi=(e1+bq-1)//bq
    u0=jnp.minimum((d-1+bq-1)//bq,hi); u1=jnp.maximum(u0,e0//bq)
    rows=pl.ds(pl.multiple_of(c,bk),bk)
    ka=ka_ref[rows,:]; va=va_ref[rows,:]; kt=kt_ref[j]
    def step(i,carry,masked):
        dk,dv=carry
        qrows=pl.ds(pl.multiple_of(i*bq,bq),bq)
        qa=qa_ref[qrows,:]; da=da_ref[qrows,:]
        p=jnp.exp2(dotf(ka,qa,NT))
        if masked:
            row=i*bq+lax.broadcasted_iota(jnp.int32,(1,bq),1)
            first_key=jnp.zeros((1,bq),jnp.int32)
            for k in range(segs):
                s=starts[k]; first_key=jnp.where(s<=row,jnp.maximum(first_key,s),first_key)
            key=c+lax.broadcasted_iota(jnp.int32,(bk,bq),0)
            p=jnp.where((key<=row)&(key>=first_key),p,0.0)
        dp=dotf(va,da,NT)
        pb=p.astype(BF); ds=(p*dp).astype(BF)
        dv=dv+dotf(pb,da,NN); dk=dk+dotf(ds,qa,NN)
        dq_ref[i]+=dotf(kt,ds,NN)
        return dk,dv
    z=jnp.zeros((bk,128),F32)
    carry=lax.fori_loop(lo,u0,lambda i,t:step(i,t,True),(z,z))
    carry=lax.fori_loop(u0,u1,lambda i,t:step(i,t,False),carry)
    dk,dv=lax.fori_loop(u1,hi,lambda i,t:step(i,t,True),carry)
    mine=pair_up(dv,dk*LN2).astype(BF)
    kv_ref[pl.ds(pl.multiple_of(j*bk,bk),bk),:]=mine
    if last:
        @pl.when(j==count-1)
        def _():
            for t in range(nq):
                dq=dq_ref[t].T*HEAD_DIM**-0.5
                dq=jnp.concatenate([dq,dq],axis=1)
                for c in range(bq//tokens):
                    r=t*bq+c*tokens
                    kv=early_ref[r:r+tokens,:] if r<begin*bk else kv_ref[r-begin*bk:r-begin*bk+tokens,:]
                    kv=kv.astype(F32)
                    dx_ref[r//tokens,:tokens,:]=jnp.where(lanes_low(kv.shape),dq[c*tokens:(c+1)*tokens],kv).astype(BF)
                    dx_ref[r//tokens,tokens:,:]=pair_up(kv[:half],kv[half:]).astype(BF)

def attend_back(starts, qa, ka, va, rest, *, bq, bk, begin, count, tokens, first, last):
    full=qa.shape[0]; segs=starts.shape[0]
    fixed=lambda shape: pl.BlockSpec(shape,lambda i,*_:(0,)*len(shape))
    dq_shape=(full//bq,64,bq); kt=pltpu.VMEM((count,64,bk),BF)
    if last:
        outs=[jax.ShapeDtypeStruct((full//tokens,tokens//2*3,128),BF)]
        scratch=[pltpu.VMEM(dq_shape,F32),kt,pltpu.VMEM((count*bk,128),BF)]
        if first: scratch.append(pltpu.VMEM((full,128),BF))
    else:
        outs=[jax.ShapeDtypeStruct(dq_shape,F32),jax.ShapeDtypeStruct((count*bk,128),BF)]
        if first: outs.insert(0,jax.ShapeDtypeStruct((full,128),BF))
        scratch=[kt]
    area=full*full*(count/(full//bk))
    return pl.pallas_call(
        functools.partial(bwd_kernel,bq=bq,bk=bk,segs=segs,begin=begin,count=count,first=first,last=last,tokens=tokens),
        grid_spec=pltpu.PrefetchScalarGridSpec(num_scalar_prefetch=1,grid=(count,),
            in_specs=[fixed(v.shape) for v in (qa,ka,va)+tuple(rest)],
            out_specs=[fixed(o.shape) for o in outs],
            scratch_shapes=scratch),
        out_shape=outs,
        compiler_params=pltpu.CompilerParams(vmem_limit_bytes=full//1024*((48 if first else 24)<<18)),
        cost_estimate=pl.CostEstimate(flops=int(area*1280),bytes_accessed=full*2000,transcendentals=int(area/2)),
        name="attend_back")(starts,qa,ka,va,*rest)

def fixed_block(shape):
    return pl.BlockSpec(shape,lambda s,*_:(0,)*len(shape))

ROOM={"project": 48}

def run_kernel(kernel, ids, grid, ins, in_specs, outs, out_specs, scratch, name, flops):
    moved=sum(math.prod(v.shape)*2 for v in ins)+sum(math.prod(o.shape)*2 for o in outs)
    return pl.pallas_call(kernel,
        grid_spec=pltpu.PrefetchScalarGridSpec(num_scalar_prefetch=1,grid=grid,in_specs=in_specs,out_specs=out_specs,scratch_shapes=scratch),
        out_shape=outs,compiler_params=pltpu.CompilerParams(vmem_limit_bytes=ROOM.get(name,20)<<20),
        cost_estimate=pl.CostEstimate(flops=flops,bytes_accessed=moved,transcendentals=0),name=name)(ids,*ins)

def pick_kernel(ids, h_ref, *outs, wide):
    for k,out in enumerate(outs):
        other=lax.bitwise_xor(ids[1]*2+ids[0],jnp.int32(k+1))
        for z in range(out.shape[1]//wide):
            out[:,z*wide:(z+1)*wide]=h_ref[:,pl.ds(pl.multiple_of((4*z+other)*wide,wide),wide)]

def pick_blocks(ids, hidden, ranks):
    tokens,inner=hidden.shape; out=jax.ShapeDtypeStruct((tokens,inner//4),hidden.dtype)
    return run_kernel(functools.partial(pick_kernel,wide=inner//ranks),ids,(1,),[hidden],[fixed_block(hidden.shape)],
        [out]*3,[fixed_block(out.shape)]*3,[],"pick_blocks",0)

def down_kernel(ids, *refs):
    lefts,rights,(sent_ref,keep_ref)=refs[:4],refs[4:8],refs[8:]
    s=pl.program_id(0)
    v=dotf(lefts[0][...],rights[0][...],TN)
    for a,b in zip(lefts[1:],rights[1:]): v=v+dotf(a[...],b[...],TN)
    v=v.astype(BF)
    @pl.when(s<2)
    def _(): sent_ref[0]=v
    @pl.when(s>=2)
    def _(): keep_ref[0]=v

def grads_down(ids, hidden, others, cots, ranks):
    tokens,inner=hidden.shape; width=cots[0].shape[1]; wide=inner//ranks
    def level(s,ids): return 2*(s%2)+jnp.where(s<2,1-ids[3],ids[3])
    mine=pl.BlockSpec((tokens,wide),lambda s,ids:(0,4*level(s,ids)+2*ids[1]+ids[0]))
    got=pl.BlockSpec((tokens,wide),lambda s,ids:(0,level(s,ids)))
    shape=jax.ShapeDtypeStruct((2,wide,width),BF)
    return run_kernel(down_kernel,ids,(4,),[hidden,*others,*cots],[mine,got,got,got]+[fixed_block(cots[0].shape)]*4,[shape,shape],
        [pl.BlockSpec((1,wide,width),lambda s,ids:(jnp.minimum(s,1),0,0)),
         pl.BlockSpec((1,wide,width),lambda s,ids:(jnp.maximum(s-2,0),0,0))],[],"grads_down",2*tokens*inner*width)

def up_kernel(ids, n_ref, no_ref, a_ref, ao_ref, ua_ref, uao_ref, ub_ref, ubo_ref, ba_ref, bao_ref, bb_ref, bbo_ref,
              as_ref, ak_ref, bs_ref, bk_ref, ln_ref, la_ref, *, share):
    s=pl.program_id(0); tokens,width=n_ref.shape; tile=width//2
    @pl.when(s==0)
    def _():
        f=lax.broadcasted_iota(jnp.int32,(width,tile),0); j=lax.broadcasted_iota(jnp.int32,(width,tile),1)
        pick=jnp.where(f==(j//share*2+ids[0])*share+j%share,1.0,0.0).astype(BF)
        for ref,pair in ((ln_ref,(n_ref,no_ref)),(la_ref,(a_ref,ao_ref))):
            for e,src in enumerate(pair):
                ref[e*tokens:(e+1)*tokens,:]=dotf(src[...],pick,NN).astype(BF)
    def product(left,one,two):
        return (dotf(left[:tokens],one[...],TN)+dotf(left[tokens:],two[...],TN)).astype(BF)
    def put_a(v):
        v=v.reshape(as_ref.shape[0],2,share,tile)
        low,high=v[:,0],v[:,1]
        cols=pl.ds(pl.multiple_of(s*tile,tile),tile)
        ak_ref[:,:,cols]=jnp.where(ids[1]==0,low,high)
        as_ref[:,:,cols]=jnp.where(ids[1]==0,high,low)
    @pl.when(s<4)
    def _():
        put_a(product(ln_ref,ua_ref,uao_ref))
        v=product(ln_ref,ub_ref,ubo_ref)
        cols=pl.ds(pl.multiple_of(s%2*tile,tile),tile)
        @pl.when(s//2==ids[2])
        def _(): bk_ref[:,cols]=v
        @pl.when(s//2!=ids[2])
        def _(): bs_ref[:,cols]=v
    @pl.when(s==4)
    def _():
        put_a(product(la_ref,ba_ref,bao_ref))
        v=product(la_ref,bb_ref,bbo_ref)
        low,high=v[:,:tile//2],v[:,tile//2:]
        bk_ref[:,2*tile:]=jnp.where(ids[2]==0,low,high)
        bs_ref[:,2*tile:]=jnp.where(ids[2]==0,high,low)

def grads_up(ids, normed, normed_other, att, att_other, up, up_other, branch, branch_other, ranks):
    tokens,width=normed.shape; share=width//ranks; tile=width//2
    f=fixed_block(normed.shape)
    at=lambda base:pl.BlockSpec((tokens,tile),lambda s,ids:(0,base+jnp.minimum(s,3)))
    fix=lambda col:pl.BlockSpec((tokens,tile),lambda s,ids:(0,col))
    a=jax.ShapeDtypeStruct((ranks//4,share,5*tile),BF); b=jax.ShapeDtypeStruct((tile,5*tile//2),BF)
    return run_kernel(functools.partial(up_kernel,share=share),ids,(5,),
        [normed,normed_other,att,att_other,up,up_other,up,up_other,branch,branch_other,branch,branch_other],
        [f,f,f,f,at(0),at(0),at(4),at(4),fix(0),fix(0),fix(1),fix(1)],[a,a,b,b],[fixed_block(v.shape) for v in (a,a,b,b)],
        [pltpu.VMEM((2*tokens,tile),BF)]*2,"grads_up",2*tokens*width*(up.shape[1]+width))

def add_kernel(ids, *refs, plan):
    n=sum(len(parts) for _,_,parts in plan)
    ins,outs=list(refs[:2*n]),list(refs[2*n:])
    for mode,which,parts in plan:
        made=[outs.pop(0) for _ in range(1 if mode=="sum" else 2)]
        base=0
        for part in parts:
            k_ref,r_ref=ins.pop(0),ins.pop(0)
            def total(index): return (k_ref[index].astype(F32)+r_ref[index].astype(F32)).astype(BF)
            for o,out in enumerate(made):
                half=ids[which] if o else 1-ids[which]
                for i in range(out.shape[0]):
                    if mode=="sum": v=total((i,))
                    elif mode=="columns":
                        width=k_ref.shape[2]//2
                        v=total((i,slice(None),pl.ds(pl.multiple_of(half*width,128),width)))
                    else: v=total((2*i+half,))
                    out[i,base:base+v.shape[0],:]=v
            base+=k_ref.shape[1]

def add_split(ids, plan, arrays, name):
    outs=[]; at=0
    for mode,_,parts in plan:
        m,_,c=arrays[at].shape
        r=sum(arrays[at+2*i].shape[1] for i in range(len(parts))); at+=2*len(parts)
        outs+=[(m,r,c)] if mode=="sum" else [(m,r,c//2) if mode=="columns" else (m//2,r,c)]*2
    return run_kernel(functools.partial(add_kernel,plan=plan),ids,(1,),arrays,[fixed_block(a.shape) for a in arrays],
        [jax.ShapeDtypeStruct(s,BF) for s in outs],[fixed_block(s) for s in outs],[],name,sum(math.prod(s) for s in outs))

def project_kernel(ids, x_ref, gain_ref, shift_ref, wq_ref, wk_ref, wv_ref, bq_ref, bv_ref, packed_ref, normed_ref):
    tokens=x_ref.shape[0]; half=tokens//2
    @pl.when(pl.program_id(0)==0)
    def _():
        x=x_ref[...].astype(F32)
        x=x-jnp.mean(x,axis=1,keepdims=True)
        x=x*lax.rsqrt(jnp.mean(x*x,axis=1,keepdims=True)+EPSILON)
        normed_ref[...]=(x*gain_ref[...]+shift_ref[...]).astype(BF)
    n=normed_ref[...]
    q=(dotf(n,wq_ref[...],NN)+bq_ref[...])*(LOG2E*HEAD_DIM**-0.5)
    k=dotf(n,wk_ref[...],NN)
    v=dotf(n,wv_ref[...],NN)+bv_ref[...]
    for h in range(q.shape[1]//HEAD_DIM):
        join=pair_down if h%2 else pair_up
        cols=slice(h//2*128,h//2*128+128)
        packed_ref[h,:tokens,:]=join(q[:,cols],k[:,cols]).astype(BF)
        packed_ref[h,tokens:,:]=join(v[:half,cols],v[half:,cols]).astype(BF)

def project(ids, x, gain, shift, w_qkv, bias_qv):
    tokens,width=x.shape; tile=256; steps=width//tile
    w=lambda base:pl.BlockSpec((width,tile),lambda s,ids:(0,base+s))
    c=lambda base:pl.BlockSpec((1,tile),lambda s,ids:(0,base+s))
    outs=[jax.ShapeDtypeStruct((HEADS,tokens//2*3,128),BF),jax.ShapeDtypeStruct((tokens,width),BF)]
    return run_kernel(project_kernel,ids,(steps,),[x,gain[None],shift[None],w_qkv,w_qkv,w_qkv,bias_qv[None],bias_qv[None]],
        [fixed_block(x.shape)]+[fixed_block((1,width))]*2+[w(0),w(steps),w(2*steps),c(0),c(steps)],outs,
        [pl.BlockSpec((tile//HEAD_DIM,tokens//2*3,128),lambda s,ids:(s,0,0)),fixed_block((tokens,width))],[],"project",6*tokens*width*width)

def unpack_tile(one, two):
    return jnp.concatenate([pair_up(one,two),pair_down(one,two)],axis=0)

def mix_kernel(ids, got_ref, w_ref, x_ref, bias_ref, gain_ref, shift_ref, two_ref, att_ref, res_ref):
    s=pl.program_id(0); width=x_ref.shape[1]
    tiles=[unpack_tile(got_ref[2*p].astype(F32),got_ref[2*p+1].astype(F32)).astype(BF) for p in range(2)]
    att=jnp.concatenate(tiles,axis=1)
    att_ref[:,pl.ds(pl.multiple_of(s*256,256),256)]=att
    @pl.when(s==0)
    def _(): res_ref[...]=x_ref[...].astype(F32)+bias_ref[...]
    res_ref[...]+=dotf(att,w_ref[...],NN)
    @pl.when(s==pl.num_programs(0)-1)
    def _():
        x=res_ref[...]
        x=x-jnp.mean(x,axis=1,keepdims=True)
        x=x*lax.rsqrt(jnp.mean(x*x,axis=1,keepdims=True)+EPSILON)
        two_ref[...]=(x*gain_ref[...]+shift_ref[...]).astype(BF)

def mix(ids, got, w_out, x, bias, gain, shift):
    tokens,width=x.shape; row=fixed_block((1,width))
    return run_kernel(mix_kernel,ids,(width//256,),[got,w_out,x,bias[None],gain[None],shift[None]],
        [pl.BlockSpec((4,tokens//2,128),lambda s,ids:(s,0,0)),pl.BlockSpec((256,width),lambda s,ids:(s,0)),fixed_block(x.shape),row,row,row],
        [jax.ShapeDtypeStruct((tokens,width),t) for t in (BF,BF,F32)],[fixed_block((tokens,width))]*3,[],"mix",2*tokens*width*width)

def grad_pack_kernel(ids, g_ref, w_ref, small_ref, out_ref):
    half=g_ref.shape[0]//2
    g=dotf(g_ref[...],w_ref[...],NT)
    for h in range(4):
        join=pair_down if h%2 else pair_up
        cols=slice(h//2*128,h//2*128+128)
        out_ref[h,:half,:]=join(g[:half,cols],g[half:,cols]).astype(BF)
    out_ref[:,half:,:]=small_ref[...]

def grad_pack(ids, g, w_out, smalls):
    tokens,width=g.shape; rows=tokens//2+smalls.shape[1]
    return run_kernel(grad_pack_kernel,ids,(width//256,),[g,w_out,smalls],
        [fixed_block(g.shape),pl.BlockSpec((256,width),lambda s,ids:(s,0)),pl.BlockSpec((4,)+smalls.shape[1:],lambda s,ids:(s,0,0))],
        [jax.ShapeDtypeStruct((HEADS,rows,128),BF)],[pl.BlockSpec((4,rows,128),lambda s,ids:(s,0,0))],[],"grad_pack",2*tokens*width*width)[0]

def message_kernel(ids, n_ref, dx_ref, out_ref, acc_ref, sum_ref, *, tokens, share):
    s=pl.program_id(0); half=tokens//2
    sides=[]
    for c in range(dx_ref.shape[0]):
        v=dx_ref[c,tokens:,:].astype(F32)
        v=jnp.concatenate([v,pltpu.roll(v,HEAD_DIM,1)],axis=0)
        v=jnp.where(lanes_low(v.shape),v,0.0).astype(BF)
        out_ref[s*dx_ref.shape[0]+c,:tokens+half,:]=dx_ref[c]
        sides.append(jnp.concatenate([dx_ref[c,:tokens,:],v],axis=1))
    side=jnp.concatenate(sides,axis=0)
    @pl.when(s==0)
    def _():
        acc_ref[...]=jnp.zeros_like(acc_ref); sum_ref[...]=jnp.zeros_like(sum_ref)
    acc_ref[...]+=dotf(n_ref[...],side,TN)
    sum_ref[...]+=jnp.sum(side.astype(F32).reshape(-1,8,256),axis=0)
    @pl.when(s==pl.num_programs(0)-1)
    def _():
        total=jnp.sum(sum_ref[...],axis=0,keepdims=True)
        high=total.astype(BF).astype(F32); rest=total-high
        line=lax.broadcasted_iota(jnp.int32,(16,128),0)
        extra=jnp.where(line==0,high[:,:128],jnp.where(line==1,rest[:,:128],jnp.where(line==2,high[:,128:],jnp.where(line==3,rest[:,128:],0.0))))
        for r in range(out_ref.shape[0]):
            rows=slice(r*share,(r+1)*share)
            base=tokens+half
            out_ref[r,base:base+share,:]=acc_ref[rows,:128].astype(BF)
            v=acc_ref[rows,128:]
            out_ref[r,base+share:base+share+share//2,:]=pair_up(v[:share//2],v[share//2:]).astype(BF)
            out_ref[r,base+share+share//2:,:]=extra.astype(BF)

def weight_message(ids, normed_all, dx):
    ranks,rows,_=dx.shape; tokens=rows//3*2; full,width=normed_all.shape; share=width//ranks
    step=4; shape=(ranks,rows+share//2*3+16,128)
    return run_kernel(functools.partial(message_kernel,tokens=tokens,share=share),ids,(ranks//step,),[normed_all,dx],
        [pl.BlockSpec((step*tokens,width),lambda s,ids:(s,0)),pl.BlockSpec((step,rows,128),lambda s,ids:(s,0,0))],
        [jax.ShapeDtypeStruct(shape,BF)],[fixed_block(shape)],
        [pltpu.VMEM((width,256),F32),pltpu.VMEM((8,256),F32)],"weight_message",2*full*width*192)[0]

def finish_kernel(ids, one_ref, two_ref, w_ref, gain_ref, shift_ref, grad_ref, cols_ref, lg_ref, lb_ref):
    share=grad_ref.shape[0]; width=grad_ref.shape[1]//3
    first=jnp.zeros((share,128),F32); second=jnp.zeros((share,128),F32)
    def both(h): return one_ref[h].astype(F32)+two_ref[h].astype(F32)
    for p in range(HEADS//2):
        a,b=both(2*p),both(2*p+1)
        end=share+share//2
        q=pair_up(a[:share],b[:share]); k=pair_down(a[:share],b[:share])
        v=unpack_tile(a[share:end],b[share:end])
        la=a[end:end+8],b[end:end+8]
        cq=pair_up(*la); ck=pair_down(*la)
        for base,tile,col in ((0,q,cq[0:1]+cq[1:2]),(width,k,ck[0:1]+ck[1:2]),(2*width,v,cq[2:3]+cq[3:4])):
            at=slice(base+p*128,base+p*128+128)
            w=w_ref[:,at].astype(F32)
            grad_ref[:,at]=tile; cols_ref[:,at]=col
            first=first+w*tile; second=second+w*col
    bias=jnp.sum(second,axis=1,keepdims=True)
    lb_ref[...]=bias
    lg_ref[...]=(jnp.sum(first,axis=1,keepdims=True)-shift_ref[...]*bias)/gain_ref[...]

def finish(ids, one, two, w_qkv, gain, shift, ranks):
    width=w_qkv.shape[0]; share=width//ranks
    mine=lambda c:pl.BlockSpec((share,c),lambda s,ids:(ids[5],0))
    outs=[jax.ShapeDtypeStruct(s,F32) for s in ((share,3*width),(1,3*width),(share,1),(share,1))]
    return run_kernel(finish_kernel,ids,(1,),[one,two,w_qkv,gain[:,None],shift[:,None]],
        [fixed_block(one.shape)]*2+[mine(3*width),mine(1),mine(1)],outs,[fixed_block(o.shape) for o in outs],[],"finish",share*width*12)

def input_kernel(ids, got_ref, wq_ref, wk_ref, wv_ref, x_ref, gain_ref, res_ref, out_ref, acc_ref):
    s=pl.program_id(0); tokens=x_ref.shape[0]
    @pl.when(s==0)
    def _(): acc_ref[...]=jnp.zeros_like(acc_ref)
    q,k,v=[],[],[]
    for p in range(2):
        a,b=got_ref[2*p].astype(F32),got_ref[2*p+1].astype(F32)
        q.append(pair_up(a[:tokens],b[:tokens])); k.append(pair_down(a[:tokens],b[:tokens]))
        v.append(unpack_tile(a[tokens:tokens//2*3],b[tokens:tokens//2*3]))
    total=acc_ref[...]
    for tiles,w_ref in ((q,wq_ref),(k,wk_ref),(v,wv_ref)):
        total=total+dotf(jnp.concatenate(tiles,axis=1).astype(BF),w_ref[...],NT)
    acc_ref[...]=total
    @pl.when(s==pl.num_programs(0)-1)
    def _():
        x=x_ref[...].astype(F32)
        x=x-jnp.mean(x,axis=1,keepdims=True)
        scale=lax.rsqrt(jnp.mean(x*x,axis=1,keepdims=True)+EPSILON)
        x=x*scale
        g=acc_ref[...]*gain_ref[...]
        g=(g-jnp.mean(g,axis=1,keepdims=True)-x*jnp.mean(g*x,axis=1,keepdims=True))*scale
        out_ref[...]=(res_ref[...]+g).astype(BF)

def input_grad(ids, got, w_qkv, x, gain, residual_grad):
    tokens,width=x.shape; steps=width//256
    w=lambda base:pl.BlockSpec((width,256),lambda s,ids:(0,base+s))
    return run_kernel(input_kernel,ids,(steps,),[got,w_qkv,w_qkv,w_qkv,x,gain[None],residual_grad],
        [pl.BlockSpec((4,)+got.shape[1:],lambda s,ids:(s,0,0)),w(0),w(steps),w(2*steps),fixed_block(x.shape),fixed_block((1,width)),fixed_block(x.shape)],
        [jax.ShapeDtypeStruct((tokens,width),BF)],[fixed_block((tokens,width))],[pltpu.VMEM((tokens,width),F32)],"input_grad",6*tokens*width*width)[0]

def statistics(values):
    centre = jnp.mean(values, axis=-1, keepdims=True)
    centred = values - centre
    second = jnp.mean(centred * centred, axis=-1, keepdims=True)
    scale = lax.rsqrt(second + EPSILON)
    return centred * scale, scale


def norm_back(unit, scale, gain, grad):
    scaled = grad * gain
    first = jnp.mean(scaled, axis=-1, keepdims=True)
    second = jnp.mean(scaled * unit, axis=-1, keepdims=True)
    return (scaled - first - unit * second) * scale


def row_sum(value):
    low = lax.optimization_barrier(value.astype(BF))
    if lax.axis_size("row") == 2:
        return low.astype(F32) + lax.ppermute(low, "row", [(0, 1), (1, 0)]).astype(F32)
    return lax.psum(low.astype(F32), "row")


def exchange(value):
    return lax.all_to_all(value, "seq", 0, 0, tiled=True)


def swap(value, bit):
    return lax.ppermute(value, "seq", [(i, i ^ bit) for i in range(lax.axis_size("seq"))])


def swap_row(value):
    return lax.ppermute(value, "row", [(0, 1), (1, 0)])


def half_step(value, axis, mine, move):
    keep = lax.dynamic_index_in_dim(value, mine, axis, keepdims=False)
    sent = lax.dynamic_index_in_dim(value, 1 - mine, axis, keepdims=False)
    return (keep.astype(F32) + move(sent).astype(F32)).astype(BF)


def outer_steps(value):
    me, bit = lax.axis_index("seq"), 4
    while value.shape[0] > 1:
        value = value.reshape((value.shape[0] // 2, 2) + value.shape[1:])
        value = half_step(value, 1, me // bit % 2, lambda v, bit=bit: swap(v, bit))
        bit *= 2
    return value[0]


def row_join(value):
    other = swap_row(value)
    first = lax.axis_index("row") == 0
    return jnp.where(first, value, other).astype(F32), jnp.where(first, other, value).astype(F32)


def per_device(
    frames,
    seg_lengths,
    ln1_gain,
    ln1_bias,
    w_qkv,
    bias_qv,
    w_out,
    bias_out,
    ln2_gain,
    ln2_bias,
    w_up,
    bias_up,
    w_down,
    bias_down,
    grad_out,
):
    tokens, feature = frames.shape[1:]
    ranks = lax.axis_size("seq")
    me = lax.axis_index("seq")
    group = max(1, ranks // HEADS)
    full = ranks * tokens
    share = feature // ranks
    wide = w_up.shape[1] // ranks
    lengths = seg_lengths[0]
    starts = jnp.cumsum(lengths, dtype=jnp.int32) - lengths
    part = (me % group).astype(jnp.int32)[None]

    def spread(value):
        return jnp.repeat(value, group, axis=0) if group > 1 else value

    def fold(value):
        if group == 1:
            return value
        value = value.reshape((HEADS, group) + value.shape[1:])
        return jnp.sum(value.astype(F32), axis=1).astype(value.dtype)

    place = [me % 2, me // 2 % 2, lax.axis_index("row"), me // 4 % 2, me // 8 % 2, me]
    ids = jnp.stack(place).astype(jnp.int32)
    packed, normed_low = project(ids, frames[0], ln1_gain, ln1_bias, w_qkv, bias_qv)
    packed = exchange(spread(packed))
    cot_low = grad_out[0]
    fast = ranks == 16 and lax.axis_size("row") == 2
    if fast:
        cot_two = swap(cot_low, 2)
        cots = [cot_low, swap(cot_low, 1), cot_two, swap(cot_two, 1)]
        cots, packed = lax.optimization_barrier((cots, packed))
    gather = lambda v: lax.all_gather(v, "seq", axis=0, tiled=True)
    normed_low, packed = lax.optimization_barrier((normed_low, packed))
    normed_all = gather(normed_low)
    low, out, qa, ka, va = attend(starts, part, packed, bq=FWD_TILE[0], bk=FWD_TILE[1], group=group)
    normed_two_low, attended_low, residual = mix(ids, fold(exchange(low)), w_out, frames[0], bias_out, ln2_gain, ln2_bias)
    unit_two, scale_two = statistics(residual)
    up_proj = dotf(normed_two_low, w_up, NN) + bias_up
    phi = 0.5 * (1.0 + lax.erf(up_proj * (0.5**0.5)))
    hidden = (up_proj * phi).astype(BF)
    slope = phi + up_proj * jnp.exp(-0.5 * up_proj * up_proj) * (1.0 / math.sqrt(2.0 * math.pi))
    out_frames = (residual + (dotf(hidden, w_down, NN) + bias_down)).astype(BF)
    cot = cot_low.astype(F32)
    if fast:
        picked, cot_low = lax.optimization_barrier((pick_blocks(ids, hidden, ranks), cot_low))
    up_grad = (dotf(cot_low, w_down, NT) * slope).astype(BF)
    normed_two_grad = dotf(up_grad, w_up, NT)
    residual_grad = cot + norm_back(unit_two, scale_two, ln2_gain, normed_two_grad)
    branch_grad = residual_grad.astype(BF)
    if fast:
        a_sent, a_keep, b_sent, b_keep = grads_up(
            ids,
            normed_two_low,
            swap(normed_two_low, 1),
            attended_low,
            swap(attended_low, 1),
            up_grad,
            swap(up_grad, 1),
            branch_grad,
            swap(branch_grad, 1),
            ranks,
        )
        branch_grad, a_sent, b_sent = lax.optimization_barrier((branch_grad, a_sent, b_sent))
        others = [swap(v, k + 1) for k, v in enumerate(picked)]
        branch_grad, others = lax.optimization_barrier((branch_grad, others))
        a_got, b_got = swap(a_sent, 2), swap_row(b_sent)

    def piece(value):
        return value.reshape(ranks, -1)

    smalls = jnp.concatenate(
        [
            piece(jnp.sum(normed_two_grad * unit_two, axis=0)),
            piece(jnp.sum(normed_two_grad, axis=0)),
            piece(jnp.sum(branch_grad, axis=0, dtype=F32)),
            piece(jnp.sum(up_grad, axis=0, dtype=F32)),
            piece(jnp.sum(cot, axis=0)),
        ],
        axis=1,
    ).astype(BF)
    smalls = smalls.reshape(ranks, -1, 128)
    lines = smalls.shape[1]
    smalls = jnp.pad(smalls, ((0, 0), (0, 16 - lines), (0, 0)))
    if group == 1:
        sent = grad_pack(ids, branch_grad, w_out, smalls)
    else:
        sent = grad_pack(ids, branch_grad, w_out, jnp.zeros((HEADS, 16, 128), BF))
        sent = jnp.concatenate([spread(sent[:, : tokens // 2]), smalls], axis=1)
    sent, normed_all = lax.optimization_barrier((sent, normed_all))
    got = exchange(sent)
    small_total = row_sum(jnp.sum(got[:, tokens // 2 : tokens // 2 + lines].astype(F32), axis=0).reshape(-1))

    back = functools.partial(attend_back, starts, qa, ka, va, bq=BWD_TILE[0], bk=BWD_TILE[1], tokens=tokens)
    tiles = full // BWD_TILE[1]
    if fast:
        blocks = lambda v: v.reshape(ranks // 2, share, -1)
        a_sent, a_keep, b_sent, b_keep = add_split(
            ids, (("columns", 2, "a"), ("blocks", 1, "b")), [a_keep, a_got, blocks(b_keep), blocks(b_got)], "add_one"
        )
        got, a_sent, b_sent = lax.optimization_barrier((got, a_sent, b_sent))
        a_got, b_got = swap_row(a_sent), swap(b_sent, 2)
        down_sent, down_keep = grads_down(ids, hidden, others, cots, ranks)
        got, down_sent = lax.optimization_barrier((got, down_sent))
        down_got = swap(down_sent, 4)
        one = back((got, out), begin=tiles // 4, count=tiles // 4, first=True, last=False)
        a_got, b_got, down_got, one = lax.optimization_barrier((a_got, b_got, down_got, one))
        up_sent, up_keep, down_sent, down_keep = add_split(
            ids,
            (("blocks", 3, "ab"), ("columns", 2, "d")),
            [a_keep, a_got, b_keep, b_got, down_keep, down_got],
            "add_two",
        )
        one, up_sent, down_sent = lax.optimization_barrier((one, up_sent, down_sent))
        up_got, down_got = swap(up_sent, 4), swap_row(down_sent)
        two = back(one, begin=0, count=tiles // 4, first=False, last=False)
        two = [one[0], two[0], jnp.concatenate([two[1], one[2]], axis=0)]
        up_got, down_got, two = lax.optimization_barrier((up_got, down_got, two))
        up_sent, up_keep, down_sent, down_keep = add_split(
            ids, (("blocks", 4, "u"), ("blocks", 4, "d")), [up_keep, up_got, down_keep, down_got], "add_three"
        )
        two, up_sent, down_sent = lax.optimization_barrier((two, up_sent, down_sent))
        up_got, down_got = swap(up_sent, 8), swap(down_sent, 8)
        (dx,) = back(two, begin=tiles // 2, count=tiles // 2, first=False, last=True)
        everything = weight_message(ids, normed_all, dx)
        up_got, down_got, everything = lax.optimization_barrier((up_got, down_got, everything))
        up_part, down_part = add_split(
            ids, (("sum", 0, "u"), ("sum", 0, "d")), [up_keep, up_got, down_keep, down_got], "add_four"
        )
        one_half, other_half = row_join(up_part[0])
        rows_a, rows_b = slice(0, share), slice(share, 2 * share)
        width = feature
        total_up = jnp.concatenate(
            [
                one_half[rows_a],
                other_half[rows_a, : 3 * width // 4],
                one_half[rows_b, :width],
                other_half[rows_b, :width],
            ],
            axis=1,
        )
        total_out = jnp.concatenate(
            [other_half[rows_a, 3 * width // 4 :], one_half[rows_b, width:], other_half[rows_b, width:]], axis=1
        )
        total_down = jnp.concatenate(row_join(down_part[0]), axis=1)
    else:
        core, across = me % 2, me // 2 % 2

        def halves(value):
            parts = value.reshape(tokens, ranks // 2, 2, -1)
            keep = lax.dynamic_index_in_dim(parts, core, 2, keepdims=False).reshape(tokens, -1)
            sent = lax.dynamic_index_in_dim(parts, 1 - core, 2, keepdims=False).reshape(tokens, -1)
            return jnp.concatenate([keep, swap(sent, 1)], axis=0)

        def both(value):
            return jnp.concatenate([value, swap(value, 1)], axis=0)

        def reduced(value):
            value = value.astype(BF).reshape(ranks // 4, 2, -1, value.shape[-1])
            return row_sum(outer_steps(half_step(value, 1, across, lambda v: swap(v, 2))))

        total_down = reduced(dotf(halves(hidden), both(cot_low), TN))
        total_up = reduced(dotf(halves(normed_two_low), both(up_grad), TN))
        total_out = reduced(dotf(halves(attended_low), both(branch_grad), TN))
        (dx,) = back((got, out), begin=0, count=tiles, first=True, last=True)
        everything = weight_message(ids, normed_all, dx)
    returned = fold(exchange(everything))
    grad_frames = input_grad(ids, returned, w_qkv, frames[0], ln1_gain, residual_grad)
    mine = returned[:, tokens // 2 * 3 :]
    if lax.axis_size("row") == 2:
        theirs = swap_row(mine)
    else:
        mine = lax.psum(mine.astype(F32), "row")
        theirs = jnp.zeros_like(mine)
    grad_w_qkv, column_total, grad_ln1_gain, grad_ln1_bias = finish(ids, mine, theirs, w_qkv, ln1_gain, ln1_bias, ranks)
    grad_ln1_gain, grad_ln1_bias = grad_ln1_gain[:, 0], grad_ln1_bias[:, 0]
    grad_bias_qv = jnp.concatenate([column_total[0, :feature], column_total[0, 2 * feature :]])
    grad_bias_qv = lax.dynamic_slice(grad_bias_qv, (me * 2 * share,), (2 * share,))

    ends = [share, 2 * share, 3 * share, 3 * share + wide]
    grad_ln2_gain, grad_ln2_bias, grad_bias_out, grad_bias_up, grad_bias_down = jnp.split(small_total, ends)
    return (
        out_frames[None],
        grad_frames[None],
        grad_ln1_gain,
        grad_ln1_bias,
        grad_w_qkv,
        grad_bias_qv,
        total_out,
        grad_bias_out,
        grad_ln2_gain,
        grad_ln2_bias,
        total_up,
        grad_bias_up,
        total_down,
        grad_bias_down,
    )


def solution(mesh):
    frames_spec = P("row", "seq", None)
    vector, matrix = P("seq"), P("seq", None)
    return jax.shard_map(
        per_device,
        mesh=mesh,
        in_specs=(frames_spec, P("row", None)) + (P(),) * 12 + (frames_spec,),
        out_specs=(
            frames_spec,
            frames_spec,
            vector,
            vector,
            matrix,
            vector,
            matrix,
            vector,
            vector,
            vector,
            matrix,
            vector,
            matrix,
            vector,
        ),
        check_vma=False,
    )
```

```python
import functools
import math

import jax
import jax.numpy as jnp
from jax import lax
from jax.experimental import pallas as pl
from jax.experimental.pallas import tpu as pltpu
from jax.sharding import PartitionSpec as P

EPSILON = 1e-05
HEADS=16; HEAD_DIM=64; NEGATIVE=-1e30
FWD_TILE=(1024,1024); BWD_TILE=(1024,1024)
LOG2E=math.log2(math.e); LN2=math.log(2.0)
BF=jnp.bfloat16; F32=jnp.float32
NT=(((1,),(1,)),((),())); TN=(((0,),(0,)),((),())); NN=(((1,),(0,)),((),()))

def dotf(a,b,dims):
    return lax.dot_general(a,b,dims,preferred_element_type=F32)

def split3(v):
    hi=v.astype(BF); r=v-hi.astype(F32); mid=r.astype(BF); lo=(r-mid.astype(F32)).astype(BF)
    return hi.astype(F32),mid.astype(F32),lo.astype(F32)

def with_tail(base, stat):
    lane=lax.broadcasted_iota(jnp.int32, base.shape, 1)
    hi,mid,lo=split3(stat)
    tail=jnp.where(lane==HEAD_DIM,hi,jnp.where(lane==HEAD_DIM+1,mid,jnp.where(lane==HEAD_DIM+2,lo,0.0)))
    return jnp.where(lane<HEAD_DIM,base,tail).astype(BF)

def seg_start(starts, p, segs):
    best=jnp.int32(0)
    for k in range(segs):
        s=starts[k]
        best=jnp.where(s<=p, jnp.maximum(best,s), best)
    return best

def seg_end(starts, p, segs, full):
    best=jnp.int32(full)
    for k in range(segs):
        s=starts[k]
        best=jnp.where(s>p, jnp.minimum(best,s), best)
    return best

def lanes_low(shape):
    return lax.broadcasted_iota(jnp.int32,shape,1)<HEAD_DIM

def pair_up(one, two):
    return jnp.where(lanes_low(one.shape),one,pltpu.roll(two,HEAD_DIM,1))

def pair_down(one, two):
    return jnp.where(lanes_low(one.shape),pltpu.roll(one,HEAD_DIM,1),two)

def fwd_kernel(starts, part, x_ref, low_ref, qa_ref, s_ref, q_ref, ka_ref, va_ref, *, bq, bk, segs, group, tokens):
    i=pl.program_id(0); full=q_ref.shape[0]; half=tokens//2
    @pl.when(i==0)
    def _():
        mark=jnp.where(lax.broadcasted_iota(jnp.int32,(tokens,128),1)<HEAD_DIM+3,-1.0,0.0)
        def build(t,_):
            pair=x_ref[t,:tokens,:].astype(F32); v=x_ref[t,tokens:,:].astype(F32)
            rows=pl.ds(pl.multiple_of(t*tokens,tokens),tokens)
            low=lanes_low((tokens,128))
            q_ref[rows,:]=jnp.where(low,pair,0.0).astype(BF)
            ka_ref[rows,:]=jnp.where(low,pltpu.roll(pair,HEAD_DIM,1),mark).astype(BF)
            values=jnp.concatenate([v,pltpu.roll(v,HEAD_DIM,1)],axis=0)
            va_ref[rows,:]=jnp.where(low,values,mark).astype(BF)
            return 0
        lax.fori_loop(0,full//tokens,build,0)
    def skip():
        low_ref[...]=jnp.zeros_like(low_ref)
        qa_ref[...]=with_tail(jnp.zeros((bq,128),F32),jnp.full((bq,1),1e30,F32))
    def work():
        a=i*bq; last=a+bq-1
        f0=seg_start(starts,a,segs); f1=seg_start(starts,last,segs)
        lo=f0//bk; hi=last//bk+1
        u0=jnp.minimum((f1+bk-1)//bk,hi); u1=jnp.maximum(u0,(a+1)//bk)
        qb=q_ref[pl.ds(pl.multiple_of(a,bq),bq),:]
        row=a+lax.broadcasted_iota(jnp.int32,(bq,1),0)
        first=jnp.zeros((bq,1),jnp.int32)
        for k in range(segs):
            s=starts[k]; first=jnp.where(s<=row,jnp.maximum(first,s),first)
        def score(j,top,masked):
            s=dotf(qb,ka_ref[pl.ds(pl.multiple_of(j*bk,bk),bk),:],NT)
            if masked:
                key=j*bk+lax.broadcasted_iota(jnp.int32,(bq,bk),1)
                s=jnp.where((key<=row)&(key>=first),s,NEGATIVE)
            s_ref[j]=s
            for c in range(bk//128):
                top=jnp.maximum(top,s[:,c*128:(c+1)*128])
            return top
        top=jnp.full((bq,128),NEGATIVE,F32)
        top=lax.fori_loop(lo,u0,lambda j,t:score(j,t,True),top)
        top=lax.fori_loop(u0,u1,lambda j,t:score(j,t,False),top)
        top=lax.fori_loop(u1,hi,lambda j,t:score(j,t,True),top)
        peak=jnp.max(top,axis=1,keepdims=True)
        def gather(j,acc):
            p=jnp.exp2(s_ref[j]-peak).astype(BF)
            return acc+dotf(p,va_ref[pl.ds(pl.multiple_of(j*bk,bk),bk),:],NN)
        acc=lax.fori_loop(lo,hi,gather,jnp.zeros((bq,128),F32))
        total=-acc[:,HEAD_DIM:HEAD_DIM+1]
        out=acc/total
        for c in range(bq//tokens):
            mid=c*tokens+half
            low_ref[c]=pair_up(out[c*tokens:mid],out[mid:mid+half]).astype(BF)
        qa_ref[...]=with_tail(qb.astype(F32),peak+jnp.log2(total))
    if group==1: work()
    else:
        own=(i%group)==part[0]
        pl.when(own)(work); pl.when(jnp.logical_not(own))(skip)

def attend(starts, part, x, *, bq, bk, group):
    ranks,rows,_=x.shape; tokens=rows//3*2; full=ranks*tokens; segs=starts.shape[0]
    if group>1: bq=tokens
    return pl.pallas_call(
        functools.partial(fwd_kernel,bq=bq,bk=bk,segs=segs,group=group,tokens=tokens),
        grid_spec=pltpu.PrefetchScalarGridSpec(num_scalar_prefetch=2,grid=(full//bq,),
            in_specs=[pl.BlockSpec(x.shape,lambda i,*_:(0,0,0))],
            out_specs=[pl.BlockSpec((bq//tokens,tokens//2,128),lambda i,*_:(i,0,0)),pl.BlockSpec((bq,128),lambda i,*_:(i,0))],
            scratch_shapes=[pltpu.VMEM((full//bk,bq,bk),F32)]+[pltpu.VMEM((full,128),BF)]*3),
        out_shape=[jax.ShapeDtypeStruct((ranks,tokens//2,128),BF),jax.ShapeDtypeStruct((full,128),BF)],
        compiler_params=pltpu.CompilerParams(vmem_limit_bytes=min(60<<20,full//1024*(40<<18))),
        cost_estimate=pl.CostEstimate(flops=full*full*512,bytes_accessed=full*1600,transcendentals=full*full//2),
        name="attend")(starts,part,x)

def bwd_kernel(starts, *refs, bq, bk, segs, begin, count, first, last, tokens):
    half=tokens//2
    refs=list(refs)
    x_ref,qa_ref=refs[:2]; refs=refs[2:]
    full=qa_ref.shape[0]; nq=full//bq
    if first: do_ref,low_ref=refs[:2]; refs=refs[2:]
    else: da_ref,dq_in,early_ref=refs[:3]; refs=refs[3:]
    if last: dx_ref,refs=refs[0],refs[1:]
    elif first: da_ref,refs=refs[0],refs[1:]
    dq_ref,kv_ref=refs[:2]
    if first and last: da_ref=refs[2]
    j=pl.program_id(0)
    low=lanes_low((tokens,128))
    unfold=lambda v: jnp.concatenate([v,pltpu.roll(v,HEAD_DIM,1)],axis=0)
    @pl.when(j==0)
    def _():
        if first:
            def build(t,_):
                rows=pl.ds(pl.multiple_of(t*tokens,tokens),tokens)
                g=unfold(do_ref[t,:half,:].astype(F32))
                delta=jnp.sum(jnp.where(low,g*unfold(low_ref[t].astype(F32)),0.0),axis=1,keepdims=True)
                da_ref[rows,:]=with_tail(g,delta)
                return 0
            lax.fori_loop(0,full//tokens,build,0)
        def clear(t,_):
            dq_ref[t]=jnp.zeros(dq_ref.shape[1:],F32) if first else dq_in[t]
            return 0
        lax.fori_loop(0,nq,clear,0)
    c=(begin+j)*bk; d=c+bk
    e0=seg_end(starts,c,segs,full); e1=seg_end(starts,d-1,segs,full)
    lo=c//bq; hi=(e1+bq-1)//bq
    u0=jnp.minimum((d-1+bq-1)//bq,hi); u1=jnp.maximum(u0,e0//bq)
    mark=jnp.where(lax.broadcasted_iota(jnp.int32,(tokens,128),1)<HEAD_DIM+3,-1.0,0.0)
    keys=[jnp.where(low,pltpu.roll(x_ref[t,:tokens,:].astype(F32),HEAD_DIM,1),mark) for t in range(bk//tokens)]
    keys=jnp.concatenate(keys,axis=0)
    values=[jnp.where(low,unfold(x_ref[t,tokens:,:].astype(F32)),mark) for t in range(bk//tokens)]
    ka=keys.astype(BF); va=jnp.concatenate(values,axis=0).astype(BF); kt=keys.T[:HEAD_DIM].astype(BF)
    def step(i,carry,masked):
        dk,dv=carry
        qrows=pl.ds(pl.multiple_of(i*bq,bq),bq)
        qa=qa_ref[qrows,:]; da=da_ref[qrows,:]
        p=jnp.exp2(dotf(ka,qa,NT))
        if masked:
            row=i*bq+lax.broadcasted_iota(jnp.int32,(1,bq),1)
            first_key=jnp.zeros((1,bq),jnp.int32)
            for k in range(segs):
                s=starts[k]; first_key=jnp.where(s<=row,jnp.maximum(first_key,s),first_key)
            key=c+lax.broadcasted_iota(jnp.int32,(bk,bq),0)
            p=jnp.where((key<=row)&(key>=first_key),p,0.0)
        dp=dotf(va,da,NT)
        pb=p.astype(BF); ds=(p*dp).astype(BF)
        dv=dv+dotf(pb,da,NN); dk=dk+dotf(ds,qa,NN)
        dq_ref[i]+=dotf(kt,ds,NN)
        return dk,dv
    z=jnp.zeros((bk,128),F32)
    carry=lax.fori_loop(lo,u0,lambda i,t:step(i,t,True),(z,z))
    carry=lax.fori_loop(u0,u1,lambda i,t:step(i,t,False),carry)
    dk,dv=lax.fori_loop(u1,hi,lambda i,t:step(i,t,True),carry)
    kv_ref[pl.ds(pl.multiple_of(j*bk,bk),bk),:]=pair_up(dv,dk*LN2).astype(BF)
    if last:
        @pl.when(j==count-1)
        def _():
            for t in range(nq):
                dq=dq_ref[t].T*HEAD_DIM**-0.5
                dq=jnp.concatenate([dq,dq],axis=1)
                for c in range(bq//tokens):
                    r=t*bq+c*tokens
                    kv=early_ref[r:r+tokens,:] if r<begin*bk else kv_ref[r-begin*bk:r-begin*bk+tokens,:]
                    kv=kv.astype(F32)
                    dx_ref[r//tokens,:tokens,:]=jnp.where(low,dq[c*tokens:(c+1)*tokens],kv).astype(BF)
                    dx_ref[r//tokens,tokens:,:]=pair_up(kv[:half],kv[half:]).astype(BF)

def attend_back(starts, x, qa, rest, *, bq, bk, begin, count, tokens, first, last):
    full=qa.shape[0]; segs=starts.shape[0]
    fixed=lambda shape: pl.BlockSpec(shape,lambda i,*_:(0,)*len(shape))
    dq_shape=(full//bq,64,bq)
    if last:
        outs=[jax.ShapeDtypeStruct(x.shape,BF)]
        scratch=[pltpu.VMEM(dq_shape,F32),pltpu.VMEM((count*bk,128),BF)]
        if first: scratch+=[pltpu.VMEM((full,128),BF)]
    else:
        outs=[jax.ShapeDtypeStruct(dq_shape,F32),jax.ShapeDtypeStruct((count*bk,128),BF)]
        if first: outs=[jax.ShapeDtypeStruct((full,128),BF)]+outs
        scratch=[]
    area=full*full*(count/(full//bk))
    return pl.pallas_call(
        functools.partial(bwd_kernel,bq=bq,bk=bk,segs=segs,begin=begin,count=count,first=first,last=last,tokens=tokens),
        grid_spec=pltpu.PrefetchScalarGridSpec(num_scalar_prefetch=1,grid=(count,),
            in_specs=[pl.BlockSpec((bk//tokens,)+x.shape[1:],lambda j,*_:(begin+j,0,0))]+[fixed(v.shape) for v in (qa,)+tuple(rest)],
            out_specs=[fixed(o.shape) for o in outs],
            scratch_shapes=scratch),
        out_shape=outs,
        compiler_params=pltpu.CompilerParams(vmem_limit_bytes=min(60<<20,full//1024*((48 if first else 24)<<18))),
        cost_estimate=pl.CostEstimate(flops=int(area*1280),bytes_accessed=full*2000,transcendentals=int(area/2)),
        name="attend_back")(starts,x,qa,*rest)

def fixed_block(shape):
    return pl.BlockSpec(shape,lambda s,*_:(0,)*len(shape))

ROOM={"project": 60}

def run_kernel(kernel, ids, grid, ins, in_specs, outs, out_specs, scratch, name, flops):
    moved=sum(math.prod(v.shape)*2 for v in ins)+sum(math.prod(o.shape)*2 for o in outs)
    return pl.pallas_call(kernel,
        grid_spec=pltpu.PrefetchScalarGridSpec(num_scalar_prefetch=1,grid=grid,in_specs=in_specs,out_specs=out_specs,scratch_shapes=scratch),
        out_shape=outs,compiler_params=pltpu.CompilerParams(vmem_limit_bytes=ROOM.get(name,20)<<20),
        cost_estimate=pl.CostEstimate(flops=flops,bytes_accessed=moved,transcendentals=0),name=name)(ids,*ins)

def pick_kernel(ids, h_ref, *outs, wide):
    for k,out in enumerate(outs):
        other=lax.bitwise_xor(ids[1]*2+ids[0],jnp.int32(k+1))
        for z in range(out.shape[1]//wide):
            out[:,z*wide:(z+1)*wide]=h_ref[:,pl.ds(pl.multiple_of((4*z+other)*wide,wide),wide)]

def pick_blocks(ids, hidden, ranks):
    tokens,inner=hidden.shape; out=jax.ShapeDtypeStruct((tokens,inner//4),hidden.dtype)
    return run_kernel(functools.partial(pick_kernel,wide=inner//ranks),ids,(1,),[hidden],[fixed_block(hidden.shape)],
        [out]*3,[fixed_block(out.shape)]*3,[],"pick_blocks",0)

def down_kernel(ids, *refs):
    lefts,rights,(sent_ref,keep_ref)=refs[:4],refs[4:8],refs[8:]
    s=pl.program_id(0)
    v=dotf(lefts[0][...],rights[0][...],TN)
    for a,b in zip(lefts[1:],rights[1:]): v=v+dotf(a[...],b[...],TN)
    v=v.astype(BF)
    @pl.when(s<2)
    def _(): sent_ref[0]=v
    @pl.when(s>=2)
    def _(): keep_ref[0]=v

def grads_down(ids, hidden, others, cots, ranks):
    tokens,inner=hidden.shape; width=cots[0].shape[1]; wide=inner//ranks
    def level(s,ids): return 2*(s%2)+jnp.where(s<2,1-ids[3],ids[3])
    mine=pl.BlockSpec((tokens,wide),lambda s,ids:(0,4*level(s,ids)+2*ids[1]+ids[0]))
    got=pl.BlockSpec((tokens,wide),lambda s,ids:(0,level(s,ids)))
    shape=jax.ShapeDtypeStruct((2,wide,width),BF)
    return run_kernel(down_kernel,ids,(4,),[hidden,*others,*cots],[mine,got,got,got]+[fixed_block(cots[0].shape)]*4,[shape,shape],
        [pl.BlockSpec((1,wide,width),lambda s,ids:(jnp.minimum(s,1),0,0)),
         pl.BlockSpec((1,wide,width),lambda s,ids:(jnp.maximum(s-2,0),0,0))],[],"grads_down",2*tokens*inner*width)

def up_kernel(ids, n_ref, no_ref, a_ref, ao_ref, ua_ref, uao_ref, ub_ref, ubo_ref, ba_ref, bao_ref, bb_ref, bbo_ref,
              as_ref, ak_ref, bs_ref, bk_ref, ln_ref, la_ref, *, share):
    s=pl.program_id(0); tokens,width=n_ref.shape; tile=width//2
    @pl.when(s==0)
    def _():
        f=lax.broadcasted_iota(jnp.int32,(width,tile),0); j=lax.broadcasted_iota(jnp.int32,(width,tile),1)
        pick=jnp.where(f==(j//share*2+ids[0])*share+j%share,1.0,0.0).astype(BF)
        for ref,pair in ((ln_ref,(n_ref,no_ref)),(la_ref,(a_ref,ao_ref))):
            for e,src in enumerate(pair):
                ref[e*tokens:(e+1)*tokens,:]=dotf(src[...],pick,NN).astype(BF)
    def product(left,one,two):
        return (dotf(left[:tokens],one[...],TN)+dotf(left[tokens:],two[...],TN)).astype(BF)
    def put_a(v):
        v=v.reshape(as_ref.shape[0],2,share,tile)
        low,high=v[:,0],v[:,1]
        cols=pl.ds(pl.multiple_of(s*tile,tile),tile)
        ak_ref[:,:,cols]=jnp.where(ids[1]==0,low,high)
        as_ref[:,:,cols]=jnp.where(ids[1]==0,high,low)
    @pl.when(s<4)
    def _():
        put_a(product(ln_ref,ua_ref,uao_ref))
        v=product(ln_ref,ub_ref,ubo_ref)
        cols=pl.ds(pl.multiple_of(s%2*tile,tile),tile)
        @pl.when(s//2==ids[2])
        def _(): bk_ref[:,cols]=v
        @pl.when(s//2!=ids[2])
        def _(): bs_ref[:,cols]=v
    @pl.when(s==4)
    def _():
        put_a(product(la_ref,ba_ref,bao_ref))
        v=product(la_ref,bb_ref,bbo_ref)
        low,high=v[:,:tile//2],v[:,tile//2:]
        bk_ref[:,2*tile:]=jnp.where(ids[2]==0,low,high)
        bs_ref[:,2*tile:]=jnp.where(ids[2]==0,high,low)

def grads_up(ids, normed, normed_other, att, att_other, up, up_other, branch, branch_other, ranks):
    tokens,width=normed.shape; share=width//ranks; tile=width//2
    f=fixed_block(normed.shape)
    at=lambda base:pl.BlockSpec((tokens,tile),lambda s,ids:(0,base+jnp.minimum(s,3)))
    fix=lambda col:pl.BlockSpec((tokens,tile),lambda s,ids:(0,col))
    a=jax.ShapeDtypeStruct((ranks//4,share,5*tile),BF); b=jax.ShapeDtypeStruct((tile,5*tile//2),BF)
    return run_kernel(functools.partial(up_kernel,share=share),ids,(5,),
        [normed,normed_other,att,att_other,up,up_other,up,up_other,branch,branch_other,branch,branch_other],
        [f,f,f,f,at(0),at(0),at(4),at(4),fix(0),fix(0),fix(1),fix(1)],[a,a,b,b],[fixed_block(v.shape) for v in (a,a,b,b)],
        [pltpu.VMEM((2*tokens,tile),BF)]*2,"grads_up",2*tokens*width*(up.shape[1]+width))

def add_kernel(ids, *refs, plan):
    n=sum(len(parts) for _,_,parts in plan)
    ins,outs=list(refs[:2*n]),list(refs[2*n:])
    for mode,which,parts in plan:
        made=[outs.pop(0) for _ in range(1 if mode=="sum" else 2)]
        base=0
        for part in parts:
            k_ref,r_ref=ins.pop(0),ins.pop(0)
            def total(index): return (k_ref[index].astype(F32)+r_ref[index].astype(F32)).astype(BF)
            for o,out in enumerate(made):
                half=ids[which] if o else 1-ids[which]
                for i in range(out.shape[0]):
                    if mode=="sum": v=total((i,))
                    elif mode=="columns":
                        width=k_ref.shape[2]//2
                        v=total((i,slice(None),pl.ds(pl.multiple_of(half*width,128),width)))
                    else: v=total((2*i+half,))
                    out[i,base:base+v.shape[0],:]=v
            base+=k_ref.shape[1]

def add_split(ids, plan, arrays, name):
    outs=[]; at=0
    for mode,_,parts in plan:
        m,_,c=arrays[at].shape
        r=sum(arrays[at+2*i].shape[1] for i in range(len(parts))); at+=2*len(parts)
        outs+=[(m,r,c)] if mode=="sum" else [(m,r,c//2) if mode=="columns" else (m//2,r,c)]*2
    return run_kernel(functools.partial(add_kernel,plan=plan),ids,(1,),arrays,[fixed_block(a.shape) for a in arrays],
        [jax.ShapeDtypeStruct(s,BF) for s in outs],[fixed_block(s) for s in outs],[],name,sum(math.prod(s) for s in outs))

def project_kernel(ids, x_ref, gain_ref, shift_ref, wq_ref, wk_ref, wv_ref, bq_ref, bv_ref, packed_ref, normed_ref):
    tokens=x_ref.shape[0]; half=tokens//2
    @pl.when(pl.program_id(0)==0)
    def _():
        x=x_ref[...].astype(F32)
        x=x-jnp.mean(x,axis=1,keepdims=True)
        x=x*lax.rsqrt(jnp.mean(x*x,axis=1,keepdims=True)+EPSILON)
        normed_ref[...]=(x*gain_ref[...]+shift_ref[...]).astype(BF)
    n=normed_ref[...]
    q=(dotf(n,wq_ref[...],NN)+bq_ref[...])*(LOG2E*HEAD_DIM**-0.5)
    k=dotf(n,wk_ref[...],NN)
    v=dotf(n,wv_ref[...],NN)+bv_ref[...]
    for h in range(q.shape[1]//HEAD_DIM):
        join=pair_down if h%2 else pair_up
        cols=slice(h//2*128,h//2*128+128)
        packed_ref[h,:tokens,:]=join(q[:,cols],k[:,cols]).astype(BF)
        packed_ref[h,tokens:,:]=join(v[:half,cols],v[half:,cols]).astype(BF)

def project(ids, x, gain, shift, w_qkv, bias_qv):
    tokens,width=x.shape; tile=256; steps=width//tile
    w=lambda base:pl.BlockSpec((width,tile),lambda s,ids:(0,base+s))
    c=lambda base:pl.BlockSpec((1,tile),lambda s,ids:(0,base+s))
    outs=[jax.ShapeDtypeStruct((HEADS,tokens//2*3,128),BF),jax.ShapeDtypeStruct((tokens,width),BF)]
    return run_kernel(project_kernel,ids,(steps,),[x,gain[None],shift[None],w_qkv,w_qkv,w_qkv,bias_qv[None],bias_qv[None]],
        [fixed_block(x.shape)]+[fixed_block((1,width))]*2+[w(0),w(steps),w(2*steps),c(0),c(steps)],outs,
        [pl.BlockSpec((tile//HEAD_DIM,tokens//2*3,128),lambda s,ids:(s,0,0)),fixed_block((tokens,width))],[],"project",6*tokens*width*width)

def unpack_tile(one, two):
    return jnp.concatenate([pair_up(one,two),pair_down(one,two)],axis=0)

def mix_kernel(ids, got_ref, w_ref, x_ref, bias_ref, gain_ref, shift_ref, two_ref, att_ref, res_ref):
    s=pl.program_id(0); width=x_ref.shape[1]
    tiles=[unpack_tile(got_ref[2*p].astype(F32),got_ref[2*p+1].astype(F32)).astype(BF) for p in range(2)]
    att=jnp.concatenate(tiles,axis=1)
    att_ref[:,pl.ds(pl.multiple_of(s*256,256),256)]=att
    @pl.when(s==0)
    def _(): res_ref[...]=x_ref[...].astype(F32)+bias_ref[...]
    res_ref[...]+=dotf(att,w_ref[...],NN)
    @pl.when(s==pl.num_programs(0)-1)
    def _():
        x=res_ref[...]
        x=x-jnp.mean(x,axis=1,keepdims=True)
        x=x*lax.rsqrt(jnp.mean(x*x,axis=1,keepdims=True)+EPSILON)
        two_ref[...]=(x*gain_ref[...]+shift_ref[...]).astype(BF)

def mix(ids, got, w_out, x, bias, gain, shift):
    tokens,width=x.shape; row=fixed_block((1,width))
    return run_kernel(mix_kernel,ids,(width//256,),[got,w_out,x,bias[None],gain[None],shift[None]],
        [pl.BlockSpec((4,tokens//2,128),lambda s,ids:(s,0,0)),pl.BlockSpec((256,width),lambda s,ids:(s,0)),fixed_block(x.shape),row,row,row],
        [jax.ShapeDtypeStruct((tokens,width),t) for t in (BF,BF,F32)],[fixed_block((tokens,width))]*3,[],"mix",2*tokens*width*width)

def grad_pack_kernel(ids, g_ref, w_ref, small_ref, out_ref):
    half=g_ref.shape[0]//2
    g=dotf(g_ref[...],w_ref[...],NT)
    for h in range(4):
        join=pair_down if h%2 else pair_up
        cols=slice(h//2*128,h//2*128+128)
        out_ref[h,:half,:]=join(g[:half,cols],g[half:,cols]).astype(BF)
    out_ref[:,half:,:]=small_ref[...]

def grad_pack(ids, g, w_out, smalls):
    tokens,width=g.shape; rows=tokens//2+smalls.shape[1]
    return run_kernel(grad_pack_kernel,ids,(width//256,),[g,w_out,smalls],
        [fixed_block(g.shape),pl.BlockSpec((256,width),lambda s,ids:(s,0)),pl.BlockSpec((4,)+smalls.shape[1:],lambda s,ids:(s,0,0))],
        [jax.ShapeDtypeStruct((HEADS,rows,128),BF)],[pl.BlockSpec((4,rows,128),lambda s,ids:(s,0,0))],[],"grad_pack",2*tokens*width*width)[0]

def message_kernel(ids, n_ref, dx_ref, out_ref, acc_ref, sum_ref, *, tokens, share):
    s=pl.program_id(0); half=tokens//2
    sides=[]
    for c in range(dx_ref.shape[0]):
        v=dx_ref[c,tokens:,:].astype(F32)
        v=jnp.concatenate([v,pltpu.roll(v,HEAD_DIM,1)],axis=0)
        v=jnp.where(lanes_low(v.shape),v,0.0).astype(BF)
        out_ref[s*dx_ref.shape[0]+c,:tokens+half,:]=dx_ref[c]
        sides.append(jnp.concatenate([dx_ref[c,:tokens,:],v],axis=1))
    side=jnp.concatenate(sides,axis=0)
    @pl.when(s==0)
    def _():
        acc_ref[...]=jnp.zeros_like(acc_ref); sum_ref[...]=jnp.zeros_like(sum_ref)
    acc_ref[...]+=dotf(n_ref[...],side,TN)
    sum_ref[...]+=jnp.sum(side.astype(F32).reshape(-1,8,256),axis=0)
    @pl.when(s==pl.num_programs(0)-1)
    def _():
        total=jnp.sum(sum_ref[...],axis=0,keepdims=True)
        high=total.astype(BF).astype(F32); rest=total-high
        line=lax.broadcasted_iota(jnp.int32,(16,128),0)
        extra=jnp.where(line==0,high[:,:128],jnp.where(line==1,rest[:,:128],jnp.where(line==2,high[:,128:],jnp.where(line==3,rest[:,128:],0.0))))
        for r in range(out_ref.shape[0]):
            rows=slice(r*share,(r+1)*share)
            base=tokens+half
            out_ref[r,base:base+share,:]=acc_ref[rows,:128].astype(BF)
            v=acc_ref[rows,128:]
            out_ref[r,base+share:base+share+share//2,:]=pair_up(v[:share//2],v[share//2:]).astype(BF)
            out_ref[r,base+share+share//2:,:]=extra.astype(BF)

def weight_message(ids, normed_all, dx):
    ranks,rows,_=dx.shape; tokens=rows//3*2; full,width=normed_all.shape; share=width//ranks
    step=4; shape=(ranks,rows+share//2*3+16,128)
    return run_kernel(functools.partial(message_kernel,tokens=tokens,share=share),ids,(ranks//step,),[normed_all,dx],
        [pl.BlockSpec((step*tokens,width),lambda s,ids:(s,0)),pl.BlockSpec((step,rows,128),lambda s,ids:(s,0,0))],
        [jax.ShapeDtypeStruct(shape,BF)],[fixed_block(shape)],
        [pltpu.VMEM((width,256),F32),pltpu.VMEM((8,256),F32)],"weight_message",2*full*width*192)[0]

def finish_kernel(ids, one_ref, two_ref, w_ref, gain_ref, shift_ref, grad_ref, cols_ref, lg_ref, lb_ref):
    share=grad_ref.shape[0]; width=grad_ref.shape[1]//3
    first=jnp.zeros((share,128),F32); second=jnp.zeros((share,128),F32)
    def both(h): return one_ref[h].astype(F32)+two_ref[h].astype(F32)
    for p in range(HEADS//2):
        a,b=both(2*p),both(2*p+1)
        end=share+share//2
        q=pair_up(a[:share],b[:share]); k=pair_down(a[:share],b[:share])
        v=unpack_tile(a[share:end],b[share:end])
        la=a[end:end+8],b[end:end+8]
        cq=pair_up(*la); ck=pair_down(*la)
        for base,tile,col in ((0,q,cq[0:1]+cq[1:2]),(width,k,ck[0:1]+ck[1:2]),(2*width,v,cq[2:3]+cq[3:4])):
            at=slice(base+p*128,base+p*128+128)
            w=w_ref[:,at].astype(F32)
            grad_ref[:,at]=tile; cols_ref[:,at]=col
            first=first+w*tile; second=second+w*col
    bias=jnp.sum(second,axis=1,keepdims=True)
    lb_ref[...]=bias
    lg_ref[...]=(jnp.sum(first,axis=1,keepdims=True)-shift_ref[...]*bias)/gain_ref[...]

def finish(ids, one, two, w_qkv, gain, shift, ranks):
    width=w_qkv.shape[0]; share=width//ranks
    mine=lambda c:pl.BlockSpec((share,c),lambda s,ids:(ids[5],0))
    outs=[jax.ShapeDtypeStruct(s,F32) for s in ((share,3*width),(1,3*width),(share,1),(share,1))]
    return run_kernel(finish_kernel,ids,(1,),[one,two,w_qkv,gain[:,None],shift[:,None]],
        [fixed_block(one.shape)]*2+[mine(3*width),mine(1),mine(1)],outs,[fixed_block(o.shape) for o in outs],[],"finish",share*width*12)

def input_kernel(ids, got_ref, wq_ref, wk_ref, wv_ref, x_ref, gain_ref, res_ref, out_ref, acc_ref):
    s=pl.program_id(0); tokens=x_ref.shape[0]
    @pl.when(s==0)
    def _(): acc_ref[...]=jnp.zeros_like(acc_ref)
    q,k,v=[],[],[]
    for p in range(2):
        a,b=got_ref[2*p].astype(F32),got_ref[2*p+1].astype(F32)
        q.append(pair_up(a[:tokens],b[:tokens])); k.append(pair_down(a[:tokens],b[:tokens]))
        v.append(unpack_tile(a[tokens:tokens//2*3],b[tokens:tokens//2*3]))
    total=acc_ref[...]
    for tiles,w_ref in ((q,wq_ref),(k,wk_ref),(v,wv_ref)):
        total=total+dotf(jnp.concatenate(tiles,axis=1).astype(BF),w_ref[...],NT)
    acc_ref[...]=total
    @pl.when(s==pl.num_programs(0)-1)
    def _():
        x=x_ref[...].astype(F32)
        x=x-jnp.mean(x,axis=1,keepdims=True)
        scale=lax.rsqrt(jnp.mean(x*x,axis=1,keepdims=True)+EPSILON)
        x=x*scale
        g=acc_ref[...]*gain_ref[...]
        g=(g-jnp.mean(g,axis=1,keepdims=True)-x*jnp.mean(g*x,axis=1,keepdims=True))*scale
        out_ref[...]=(res_ref[...]+g).astype(BF)

def input_grad(ids, got, w_qkv, x, gain, residual_grad):
    tokens,width=x.shape; steps=width//256
    w=lambda base:pl.BlockSpec((width,256),lambda s,ids:(0,base+s))
    return run_kernel(input_kernel,ids,(steps,),[got,w_qkv,w_qkv,w_qkv,x,gain[None],residual_grad],
        [pl.BlockSpec((4,)+got.shape[1:],lambda s,ids:(s,0,0)),w(0),w(steps),w(2*steps),fixed_block(x.shape),fixed_block((1,width)),fixed_block(x.shape)],
        [jax.ShapeDtypeStruct((tokens,width),BF)],[fixed_block((tokens,width))],[pltpu.VMEM((tokens,width),F32)],"input_grad",6*tokens*width*width)[0]

def statistics(values):
    centre = jnp.mean(values, axis=-1, keepdims=True)
    centred = values - centre
    second = jnp.mean(centred * centred, axis=-1, keepdims=True)
    scale = lax.rsqrt(second + EPSILON)
    return centred * scale, scale


def norm_back(unit, scale, gain, grad):
    scaled = grad * gain
    first = jnp.mean(scaled, axis=-1, keepdims=True)
    second = jnp.mean(scaled * unit, axis=-1, keepdims=True)
    return (scaled - first - unit * second) * scale


def row_sum(value):
    low = lax.optimization_barrier(value.astype(BF))
    if lax.axis_size("row") == 2:
        return low.astype(F32) + lax.ppermute(low, "row", [(0, 1), (1, 0)]).astype(F32)
    return lax.psum(low.astype(F32), "row")


def exchange(value):
    return lax.all_to_all(value, "seq", 0, 0, tiled=True)


def swap(value, bit):
    return lax.ppermute(value, "seq", [(i, i ^ bit) for i in range(lax.axis_size("seq"))])


def swap_row(value):
    return lax.ppermute(value, "row", [(0, 1), (1, 0)])


def half_step(value, axis, mine, move):
    keep = lax.dynamic_index_in_dim(value, mine, axis, keepdims=False)
    sent = lax.dynamic_index_in_dim(value, 1 - mine, axis, keepdims=False)
    return (keep.astype(F32) + move(sent).astype(F32)).astype(BF)


def outer_steps(value):
    me, bit = lax.axis_index("seq"), 4
    while value.shape[0] > 1:
        value = value.reshape((value.shape[0] // 2, 2) + value.shape[1:])
        value = half_step(value, 1, me // bit % 2, lambda v, bit=bit: swap(v, bit))
        bit *= 2
    return value[0]


def row_join(value):
    other = swap_row(value)
    first = lax.axis_index("row") == 0
    return jnp.where(first, value, other).astype(F32), jnp.where(first, other, value).astype(F32)


def per_device(
    frames,
    seg_lengths,
    ln1_gain,
    ln1_bias,
    w_qkv,
    bias_qv,
    w_out,
    bias_out,
    ln2_gain,
    ln2_bias,
    w_up,
    bias_up,
    w_down,
    bias_down,
    grad_out,
):
    tokens, feature = frames.shape[1:]
    ranks = lax.axis_size("seq")
    me = lax.axis_index("seq")
    group = max(1, ranks // HEADS)
    full = ranks * tokens
    share = feature // ranks
    wide = w_up.shape[1] // ranks
    lengths = seg_lengths[0]
    starts = jnp.cumsum(lengths, dtype=jnp.int32) - lengths
    part = (me % group).astype(jnp.int32)[None]

    def spread(value):
        return jnp.repeat(value, group, axis=0) if group > 1 else value

    def fold(value):
        if group == 1:
            return value
        value = value.reshape((HEADS, group) + value.shape[1:])
        return jnp.sum(value.astype(F32), axis=1).astype(value.dtype)

    place = [me % 2, me // 2 % 2, lax.axis_index("row"), me // 4 % 2, me // 8 % 2, me]
    ids = jnp.stack(place).astype(jnp.int32)
    packed, normed_low = project(ids, frames[0], ln1_gain, ln1_bias, w_qkv, bias_qv)
    packed = exchange(spread(packed))
    cot_low = grad_out[0]
    fast = ranks == 16 and lax.axis_size("row") == 2
    if fast:
        cot_two = swap(cot_low, 2)
        cots = [cot_low, swap(cot_low, 1), cot_two, swap(cot_two, 1)]
        cots, packed = lax.optimization_barrier((cots, packed))
    gather = lambda v: lax.all_gather(v, "seq", axis=0, tiled=True)
    normed_low, packed = lax.optimization_barrier((normed_low, packed))
    normed_all = gather(normed_low)
    low, qa = attend(starts, part, packed, bq=FWD_TILE[0], bk=FWD_TILE[1], group=group)
    normed_two_low, attended_low, residual = mix(ids, fold(exchange(low)), w_out, frames[0], bias_out, ln2_gain, ln2_bias)
    unit_two, scale_two = statistics(residual)
    up_proj = dotf(normed_two_low, w_up, NN) + bias_up
    phi = 0.5 * (1.0 + lax.erf(up_proj * (0.5**0.5)))
    hidden = (up_proj * phi).astype(BF)
    slope = phi + up_proj * jnp.exp(-0.5 * up_proj * up_proj) * (1.0 / math.sqrt(2.0 * math.pi))
    out_frames = (residual + (dotf(hidden, w_down, NN) + bias_down)).astype(BF)
    cot = cot_low.astype(F32)
    if fast:
        picked, cot_low = lax.optimization_barrier((pick_blocks(ids, hidden, ranks), cot_low))
    up_grad = (dotf(cot_low, w_down, NT) * slope).astype(BF)
    normed_two_grad = dotf(up_grad, w_up, NT)
    gain_two = ln2_gain
    if fast:
        others = [swap(v, k + 1) for k, v in enumerate(picked)]
    residual_grad = cot + norm_back(unit_two, scale_two, gain_two, normed_two_grad)
    branch_grad = residual_grad.astype(BF)
    if fast:
        others[1], branch_grad = lax.optimization_barrier((others[1], branch_grad))
    if fast:
        a_sent, a_keep, b_sent, b_keep = grads_up(
            ids,
            normed_two_low,
            swap(normed_two_low, 1),
            attended_low,
            swap(attended_low, 1),
            up_grad,
            swap(up_grad, 1),
            branch_grad,
            swap(branch_grad, 1),
            ranks,
        )
        branch_grad, a_sent, b_sent = lax.optimization_barrier((branch_grad, a_sent, b_sent))
        branch_grad, others = lax.optimization_barrier((branch_grad, others))
        a_got, b_got = swap(a_sent, 2), swap_row(b_sent)

    def piece(value):
        return value.reshape(ranks, -1)

    smalls = jnp.concatenate(
        [
            piece(jnp.sum(normed_two_grad * unit_two, axis=0)),
            piece(jnp.sum(normed_two_grad, axis=0)),
            piece(jnp.sum(branch_grad, axis=0, dtype=F32)),
            piece(jnp.sum(up_grad, axis=0, dtype=F32)),
            piece(jnp.sum(cot, axis=0)),
        ],
        axis=1,
    ).astype(BF)
    smalls = smalls.reshape(ranks, -1, 128)
    lines = smalls.shape[1]
    smalls = jnp.pad(smalls, ((0, 0), (0, 16 - lines), (0, 0)))
    if group == 1:
        sent = grad_pack(ids, branch_grad, w_out, smalls)
    else:
        sent = grad_pack(ids, branch_grad, w_out, jnp.zeros((HEADS, 16, 128), BF))
        sent = jnp.concatenate([spread(sent[:, : tokens // 2]), smalls], axis=1)
    sent, normed_all = lax.optimization_barrier((sent, normed_all))
    got = exchange(sent)
    small_total = row_sum(jnp.sum(got[:, tokens // 2 : tokens // 2 + lines].astype(F32), axis=0).reshape(-1))

    back = functools.partial(attend_back, starts, packed, qa, bq=BWD_TILE[0], bk=BWD_TILE[1], tokens=tokens)
    tiles = full // BWD_TILE[1]
    if fast:
        blocks = lambda v: v.reshape(ranks // 2, share, -1)
        a_sent, a_keep, b_sent, b_keep = add_split(
            ids, (("columns", 2, "a"), ("blocks", 1, "b")), [a_keep, a_got, blocks(b_keep), blocks(b_got)], "add_one"
        )
        got, _, _ = lax.optimization_barrier((got, a_sent, b_sent))
        a_got, b_got = swap_row(a_sent), swap(b_sent, 2)
        down_sent, down_keep = grads_down(ids, hidden, others, cots, ranks)
        got, _ = lax.optimization_barrier((got, down_sent))
        down_got = swap(down_sent, 4)
        one = back((got, low), begin=tiles // 4, count=tiles // 4, first=True, last=False)
        a_got, b_got, down_got, one = lax.optimization_barrier((a_got, b_got, down_got, one))
        up_sent, up_keep, down_sent, down_keep = add_split(
            ids,
            (("blocks", 3, "ab"), ("columns", 2, "d")),
            [a_keep, a_got, b_keep, b_got, down_keep, down_got],
            "add_two",
        )
        one, up_sent, down_sent = lax.optimization_barrier((one, up_sent, down_sent))
        up_got, down_got = swap(up_sent, 4), swap_row(down_sent)
        two = back(one, begin=0, count=tiles // 4, first=False, last=False)
        two = [one[0], two[0], jnp.concatenate([two[1], one[2]], axis=0)]
        up_got, down_got, two = lax.optimization_barrier((up_got, down_got, two))
        up_sent, up_keep, down_sent, down_keep = add_split(
            ids, (("blocks", 4, "u"), ("blocks", 4, "d")), [up_keep, up_got, down_keep, down_got], "add_three"
        )
        two, up_sent, down_sent = lax.optimization_barrier((two, up_sent, down_sent))
        up_got, down_got = swap(up_sent, 8), swap(down_sent, 8)
        (dx,) = back(two, begin=tiles // 2, count=tiles // 2, first=False, last=True)
        everything = weight_message(ids, normed_all, dx)
        up_got, down_got, everything = lax.optimization_barrier((up_got, down_got, everything))
        up_part, down_part = add_split(
            ids, (("sum", 0, "u"), ("sum", 0, "d")), [up_keep, up_got, down_keep, down_got], "add_four"
        )
        one_half, other_half = row_join(up_part[0])
        rows_a, rows_b = slice(0, share), slice(share, 2 * share)
        width = feature
        total_up = jnp.concatenate(
            [
                one_half[rows_a],
                other_half[rows_a, : 3 * width // 4],
                one_half[rows_b, :width],
                other_half[rows_b, :width],
            ],
            axis=1,
        )
        total_out = jnp.concatenate(
            [other_half[rows_a, 3 * width // 4 :], one_half[rows_b, width:], other_half[rows_b, width:]], axis=1
        )
        total_down = jnp.concatenate(row_join(down_part[0]), axis=1)
    else:
        core, across = me % 2, me // 2 % 2

        def halves(value):
            parts = value.reshape(tokens, ranks // 2, 2, -1)
            keep = lax.dynamic_index_in_dim(parts, core, 2, keepdims=False).reshape(tokens, -1)
            sent = lax.dynamic_index_in_dim(parts, 1 - core, 2, keepdims=False).reshape(tokens, -1)
            return jnp.concatenate([keep, swap(sent, 1)], axis=0)

        def both(value):
            return jnp.concatenate([value, swap(value, 1)], axis=0)

        def reduced(value):
            value = value.astype(BF).reshape(ranks // 4, 2, -1, value.shape[-1])
            return row_sum(outer_steps(half_step(value, 1, across, lambda v: swap(v, 2))))

        total_down = reduced(dotf(halves(hidden), both(cot_low), TN))
        total_up = reduced(dotf(halves(normed_two_low), both(up_grad), TN))
        total_out = reduced(dotf(halves(attended_low), both(branch_grad), TN))
        (dx,) = back((got, low), begin=0, count=tiles, first=True, last=True)
        everything = weight_message(ids, normed_all, dx)
    returned = fold(exchange(everything))
    grad_frames = input_grad(ids, returned, w_qkv, frames[0], ln1_gain, residual_grad)
    mine = returned[:, tokens // 2 * 3 :]
    if lax.axis_size("row") == 2:
        theirs = swap_row(mine)
    else:
        mine = lax.psum(mine.astype(F32), "row")
        theirs = jnp.zeros_like(mine)
    grad_w_qkv, column_total, grad_ln1_gain, grad_ln1_bias = finish(ids, mine, theirs, w_qkv, ln1_gain, ln1_bias, ranks)
    grad_ln1_gain, grad_ln1_bias = grad_ln1_gain[:, 0], grad_ln1_bias[:, 0]
    grad_bias_qv = jnp.concatenate([column_total[0, :feature], column_total[0, 2 * feature :]])
    grad_bias_qv = lax.dynamic_slice(grad_bias_qv, (me * 2 * share,), (2 * share,))

    ends = [share, 2 * share, 3 * share, 3 * share + wide]
    grad_ln2_gain, grad_ln2_bias, grad_bias_out, grad_bias_up, grad_bias_down = jnp.split(small_total, ends)
    return (
        out_frames[None],
        grad_frames[None],
        grad_ln1_gain,
        grad_ln1_bias,
        grad_w_qkv,
        grad_bias_qv,
        total_out,
        grad_bias_out,
        grad_ln2_gain,
        grad_ln2_bias,
        total_up,
        grad_bias_up,
        total_down,
        grad_bias_down,
    )


def solution(mesh):
    frames_spec = P("row", "seq", None)
    vector, matrix = P("seq"), P("seq", None)
    return jax.shard_map(
        per_device,
        mesh=mesh,
        in_specs=(frames_spec, P("row", None)) + (P(),) * 12 + (frames_spec,),
        out_specs=(
            frames_spec,
            frames_spec,
            vector,
            vector,
            matrix,
            vector,
            matrix,
            vector,
            vector,
            vector,
            matrix,
            vector,
            matrix,
            vector,
        ),
        check_vma=False,
    )
```

```python
import functools
import math

import jax
import jax.numpy as jnp
from jax import lax
from jax.experimental import pallas as pl
from jax.experimental.pallas import tpu as pltpu
from jax.sharding import PartitionSpec as P

EPSILON = 1e-05
HEADS=16; HEAD_DIM=64; NEGATIVE=-1e30
FWD_TILE=(1024,1024); BWD_TILE=(1024,1024)
LOG2E=math.log2(math.e); LN2=math.log(2.0)
BF=jnp.bfloat16; F32=jnp.float32
NT=(((1,),(1,)),((),())); TN=(((0,),(0,)),((),())); NN=(((1,),(0,)),((),()))

def dotf(a,b,dims):
    return lax.dot_general(a,b,dims,preferred_element_type=F32)

def split3(v):
    hi=v.astype(BF); r=v-hi.astype(F32); mid=r.astype(BF); lo=(r-mid.astype(F32)).astype(BF)
    return hi.astype(F32),mid.astype(F32),lo.astype(F32)

def with_tail(base, stat):
    lane=lax.broadcasted_iota(jnp.int32, base.shape, 1)
    hi,mid,lo=split3(stat)
    tail=jnp.where(lane==HEAD_DIM,hi,jnp.where(lane==HEAD_DIM+1,mid,jnp.where(lane==HEAD_DIM+2,lo,0.0)))
    return jnp.where(lane<HEAD_DIM,base,tail).astype(BF)

def seg_start(starts, p, segs):
    best=jnp.int32(0)
    for k in range(segs):
        s=starts[k]
        best=jnp.where(s<=p, jnp.maximum(best,s), best)
    return best

def seg_end(starts, p, segs, full):
    best=jnp.int32(full)
    for k in range(segs):
        s=starts[k]
        best=jnp.where(s>p, jnp.minimum(best,s), best)
    return best

def lanes_low(shape):
    return lax.broadcasted_iota(jnp.int32,shape,1)<HEAD_DIM

def pair_up(one, two):
    return jnp.where(lanes_low(one.shape),one,pltpu.roll(two,HEAD_DIM,1))

def pair_down(one, two):
    return jnp.where(lanes_low(one.shape),pltpu.roll(one,HEAD_DIM,1),two)

def fwd_kernel(starts, part, x_ref, low_ref, qa_ref, s_ref, q_ref, ka_ref, va_ref, *, bq, bk, segs, group, tokens):
    i=pl.program_id(0); full=q_ref.shape[0]; half=tokens//2
    @pl.when(i==0)
    def _():
        mark=jnp.where(lax.broadcasted_iota(jnp.int32,(tokens,128),1)<HEAD_DIM+3,-1.0,0.0)
        def build(t,_):
            pair=x_ref[t,:tokens,:].astype(F32); v=x_ref[t,tokens:,:].astype(F32)
            rows=pl.ds(pl.multiple_of(t*tokens,tokens),tokens)
            low=lanes_low((tokens,128))
            q_ref[rows,:]=jnp.where(low,pair,0.0).astype(BF)
            ka_ref[rows,:]=jnp.where(low,pltpu.roll(pair,HEAD_DIM,1),mark).astype(BF)
            values=jnp.concatenate([v,pltpu.roll(v,HEAD_DIM,1)],axis=0)
            va_ref[rows,:]=jnp.where(low,values,mark).astype(BF)
            return 0
        lax.fori_loop(0,full//tokens,build,0)
    def skip():
        low_ref[...]=jnp.zeros_like(low_ref)
        qa_ref[...]=with_tail(jnp.zeros((bq,128),F32),jnp.full((bq,1),1e30,F32))
    def work():
        a=i*bq; last=a+bq-1
        f0=seg_start(starts,a,segs); f1=seg_start(starts,last,segs)
        lo=f0//bk; hi=last//bk+1
        u0=jnp.minimum((f1+bk-1)//bk,hi); u1=jnp.maximum(u0,(a+1)//bk)
        qb=q_ref[pl.ds(pl.multiple_of(a,bq),bq),:]
        row=a+lax.broadcasted_iota(jnp.int32,(bq,1),0)
        first=jnp.zeros((bq,1),jnp.int32)
        for k in range(segs):
            s=starts[k]; first=jnp.where(s<=row,jnp.maximum(first,s),first)
        def score(j,top,masked):
            s=dotf(qb,ka_ref[pl.ds(pl.multiple_of(j*bk,bk),bk),:],NT)
            if masked:
                key=j*bk+lax.broadcasted_iota(jnp.int32,(bq,bk),1)
                s=jnp.where((key<=row)&(key>=first),s,NEGATIVE)
            s_ref[j]=s
            for c in range(bk//128):
                top=jnp.maximum(top,s[:,c*128:(c+1)*128])
            return top
        top=jnp.full((bq,128),NEGATIVE,F32)
        top=lax.fori_loop(lo,u0,lambda j,t:score(j,t,True),top)
        top=lax.fori_loop(u0,u1,lambda j,t:score(j,t,False),top)
        top=lax.fori_loop(u1,hi,lambda j,t:score(j,t,True),top)
        peak=jnp.max(top,axis=1,keepdims=True)
        def gather(j,acc):
            p=jnp.exp2(s_ref[j]-peak).astype(BF)
            return acc+dotf(p,va_ref[pl.ds(pl.multiple_of(j*bk,bk),bk),:],NN)
        acc=lax.fori_loop(lo,hi,gather,jnp.zeros((bq,128),F32))
        total=-acc[:,HEAD_DIM:HEAD_DIM+1]
        out=acc/total
        for c in range(bq//tokens):
            mid=c*tokens+half
            low_ref[c]=pair_up(out[c*tokens:mid],out[mid:mid+half]).astype(BF)
        qa_ref[...]=with_tail(qb.astype(F32),peak+jnp.log2(total))
    if group==1: work()
    else:
        own=(i%group)==part[0]
        pl.when(own)(work); pl.when(jnp.logical_not(own))(skip)

def attend(starts, part, x, *, bq, bk, group):
    ranks,rows,_=x.shape; tokens=rows//3*2; full=ranks*tokens; segs=starts.shape[0]
    if group>1: bq=tokens
    return pl.pallas_call(
        functools.partial(fwd_kernel,bq=bq,bk=bk,segs=segs,group=group,tokens=tokens),
        grid_spec=pltpu.PrefetchScalarGridSpec(num_scalar_prefetch=2,grid=(full//bq,),
            in_specs=[pl.BlockSpec(x.shape,lambda i,*_:(0,0,0))],
            out_specs=[pl.BlockSpec((bq//tokens,tokens//2,128),lambda i,*_:(i,0,0)),pl.BlockSpec((bq,128),lambda i,*_:(i,0))],
            scratch_shapes=[pltpu.VMEM((full//bk,bq,bk),F32)]+[pltpu.VMEM((full,128),BF)]*3),
        out_shape=[jax.ShapeDtypeStruct((ranks,tokens//2,128),BF),jax.ShapeDtypeStruct((full,128),BF)],
        compiler_params=pltpu.CompilerParams(vmem_limit_bytes=min(60<<20,full//1024*(40<<18))),
        cost_estimate=pl.CostEstimate(flops=full*full*512,bytes_accessed=full*1600,transcendentals=full*full//2),
        name="attend")(starts,part,x)

def bwd_kernel(starts, *refs, bq, bk, segs, begin, count, first, last, tokens):
    half=tokens//2
    refs=list(refs)
    x_ref,qa_ref=refs[:2]; refs=refs[2:]
    full=qa_ref.shape[0]; nq=full//bq
    if first: do_ref,low_ref=refs[:2]; refs=refs[2:]
    else: da_ref,dq_in,early_ref=refs[:3]; refs=refs[3:]
    if last: dx_ref,refs=refs[0],refs[1:]
    elif first: da_ref,refs=refs[0],refs[1:]
    dq_ref,kv_ref=refs[:2]
    if first and last: da_ref=refs[2]
    j=pl.program_id(0)
    low=lanes_low((tokens,128))
    unfold=lambda v: jnp.concatenate([v,pltpu.roll(v,HEAD_DIM,1)],axis=0)
    @pl.when(j==0)
    def _():
        if first:
            def build(t,_):
                rows=pl.ds(pl.multiple_of(t*tokens,tokens),tokens)
                g=unfold(do_ref[t,:half,:].astype(F32))
                delta=jnp.sum(jnp.where(low,g*unfold(low_ref[t].astype(F32)),0.0),axis=1,keepdims=True)
                da_ref[rows,:]=with_tail(g,delta)
                return 0
            lax.fori_loop(0,full//tokens,build,0)
        def clear(t,_):
            dq_ref[t]=jnp.zeros(dq_ref.shape[1:],F32) if first else dq_in[t]
            return 0
        lax.fori_loop(0,nq,clear,0)
    c=(begin+j)*bk; d=c+bk
    e0=seg_end(starts,c,segs,full); e1=seg_end(starts,d-1,segs,full)
    lo=c//bq; hi=(e1+bq-1)//bq
    u0=jnp.minimum((d-1+bq-1)//bq,hi); u1=jnp.maximum(u0,e0//bq)
    mark=jnp.where(lax.broadcasted_iota(jnp.int32,(tokens,128),1)<HEAD_DIM+3,-1.0,0.0)
    keys=[jnp.where(low,pltpu.roll(x_ref[t,:tokens,:].astype(F32),HEAD_DIM,1),mark) for t in range(bk//tokens)]
    keys=jnp.concatenate(keys,axis=0)
    values=[jnp.where(low,unfold(x_ref[t,tokens:,:].astype(F32)),mark) for t in range(bk//tokens)]
    ka=keys.astype(BF); va=jnp.concatenate(values,axis=0).astype(BF); kt=keys.T[:HEAD_DIM].astype(BF)
    def step(i,carry,masked):
        dk,dv=carry
        qrows=pl.ds(pl.multiple_of(i*bq,bq),bq)
        qa=qa_ref[qrows,:]; da=da_ref[qrows,:]
        p=jnp.exp2(dotf(ka,qa,NT))
        if masked:
            row=i*bq+lax.broadcasted_iota(jnp.int32,(1,bq),1)
            first_key=jnp.zeros((1,bq),jnp.int32)
            for k in range(segs):
                s=starts[k]; first_key=jnp.where(s<=row,jnp.maximum(first_key,s),first_key)
            key=c+lax.broadcasted_iota(jnp.int32,(bk,bq),0)
            p=jnp.where((key<=row)&(key>=first_key),p,0.0)
        dp=dotf(va,da,NT)
        pb=p.astype(BF); ds=(p*dp).astype(BF)
        dv=dv+dotf(pb,da,NN); dk=dk+dotf(ds,qa,NN)
        dq_ref[i]+=dotf(kt,ds,NN)
        return dk,dv
    z=jnp.zeros((bk,128),F32)
    carry=lax.fori_loop(lo,u0,lambda i,t:step(i,t,True),(z,z))
    carry=lax.fori_loop(u0,u1,lambda i,t:step(i,t,False),carry)
    dk,dv=lax.fori_loop(u1,hi,lambda i,t:step(i,t,True),carry)
    kv_ref[pl.ds(pl.multiple_of(j*bk,bk),bk),:]=pair_up(dv,dk*LN2).astype(BF)
    if last:
        @pl.when(j==count-1)
        def _():
            for t in range(nq):
                dq=dq_ref[t].T*HEAD_DIM**-0.5
                dq=jnp.concatenate([dq,dq],axis=1)
                for c in range(bq//tokens):
                    r=t*bq+c*tokens
                    kv=early_ref[r:r+tokens,:] if r<begin*bk else kv_ref[r-begin*bk:r-begin*bk+tokens,:]
                    kv=kv.astype(F32)
                    dx_ref[r//tokens,:tokens,:]=jnp.where(low,dq[c*tokens:(c+1)*tokens],kv).astype(BF)
                    dx_ref[r//tokens,tokens:,:]=pair_up(kv[:half],kv[half:]).astype(BF)

def attend_back(starts, x, qa, rest, *, bq, bk, begin, count, tokens, first, last):
    full=qa.shape[0]; segs=starts.shape[0]
    fixed=lambda shape: pl.BlockSpec(shape,lambda i,*_:(0,)*len(shape))
    dq_shape=(full//bq,64,bq)
    if last:
        outs=[jax.ShapeDtypeStruct(x.shape,BF)]
        scratch=[pltpu.VMEM(dq_shape,F32),pltpu.VMEM((count*bk,128),BF)]
        if first: scratch+=[pltpu.VMEM((full,128),BF)]
    else:
        outs=[jax.ShapeDtypeStruct(dq_shape,F32),jax.ShapeDtypeStruct((count*bk,128),BF)]
        if first: outs=[jax.ShapeDtypeStruct((full,128),BF)]+outs
        scratch=[]
    area=full*full*(count/(full//bk))
    return pl.pallas_call(
        functools.partial(bwd_kernel,bq=bq,bk=bk,segs=segs,begin=begin,count=count,first=first,last=last,tokens=tokens),
        grid_spec=pltpu.PrefetchScalarGridSpec(num_scalar_prefetch=1,grid=(count,),
            in_specs=[pl.BlockSpec((bk//tokens,)+x.shape[1:],lambda j,*_:(begin+j,0,0))]+[fixed(v.shape) for v in (qa,)+tuple(rest)],
            out_specs=[fixed(o.shape) for o in outs],
            scratch_shapes=scratch),
        out_shape=outs,
        compiler_params=pltpu.CompilerParams(vmem_limit_bytes=min(60<<20,full//1024*((48 if first else 24)<<18))),
        cost_estimate=pl.CostEstimate(flops=int(area*1280),bytes_accessed=full*2000,transcendentals=int(area/2)),
        name="attend_back")(starts,x,qa,*rest)

def fixed_block(shape):
    return pl.BlockSpec(shape,lambda s,*_:(0,)*len(shape))

ROOM={"project": 60}

def run_kernel(kernel, ids, grid, ins, in_specs, outs, out_specs, scratch, name, flops):
    moved=sum(math.prod(v.shape)*2 for v in ins)+sum(math.prod(o.shape)*2 for o in outs)
    return pl.pallas_call(kernel,
        grid_spec=pltpu.PrefetchScalarGridSpec(num_scalar_prefetch=1,grid=grid,in_specs=in_specs,out_specs=out_specs,scratch_shapes=scratch),
        out_shape=outs,compiler_params=pltpu.CompilerParams(vmem_limit_bytes=ROOM.get(name,20)<<20),
        cost_estimate=pl.CostEstimate(flops=flops,bytes_accessed=moved,transcendentals=0),name=name)(ids,*ins)

def pick_kernel(ids, h_ref, *outs, wide):
    for k,out in enumerate(outs):
        other=lax.bitwise_xor(ids[1]*2+ids[0],jnp.int32(k+1))
        for z in range(out.shape[1]//wide):
            out[:,z*wide:(z+1)*wide]=h_ref[:,pl.ds(pl.multiple_of((4*z+other)*wide,wide),wide)]

def pick_blocks(ids, hidden, ranks):
    tokens,inner=hidden.shape; out=jax.ShapeDtypeStruct((tokens,inner//4),hidden.dtype)
    return run_kernel(functools.partial(pick_kernel,wide=inner//ranks),ids,(1,),[hidden],[fixed_block(hidden.shape)],
        [out]*3,[fixed_block(out.shape)]*3,[],"pick_blocks",0)

def down_kernel(ids, *refs):
    lefts,rights,(sent_ref,keep_ref)=refs[:4],refs[4:8],refs[8:]
    s=pl.program_id(0)
    v=dotf(lefts[0][...],rights[0][...],TN)
    for a,b in zip(lefts[1:],rights[1:]): v=v+dotf(a[...],b[...],TN)
    v=v.astype(BF)
    @pl.when(s<2)
    def _(): sent_ref[0]=v
    @pl.when(s>=2)
    def _(): keep_ref[0]=v

def grads_down(ids, hidden, others, cots, ranks):
    tokens,inner=hidden.shape; width=cots[0].shape[1]; wide=inner//ranks
    def level(s,ids): return 2*(s%2)+jnp.where(s<2,1-ids[3],ids[3])
    mine=pl.BlockSpec((tokens,wide),lambda s,ids:(0,4*level(s,ids)+2*ids[1]+ids[0]))
    got=pl.BlockSpec((tokens,wide),lambda s,ids:(0,level(s,ids)))
    shape=jax.ShapeDtypeStruct((2,wide,width),BF)
    return run_kernel(down_kernel,ids,(4,),[hidden,*others,*cots],[mine,got,got,got]+[fixed_block(cots[0].shape)]*4,[shape,shape],
        [pl.BlockSpec((1,wide,width),lambda s,ids:(jnp.minimum(s,1),0,0)),
         pl.BlockSpec((1,wide,width),lambda s,ids:(jnp.maximum(s-2,0),0,0))],[],"grads_down",2*tokens*inner*width)

def up_kernel(ids, n_ref, no_ref, a_ref, ao_ref, ua_ref, uao_ref, ub_ref, ubo_ref, ba_ref, bao_ref, bb_ref, bbo_ref,
              a_out, b_out, left_ref, part_ref, *, share, keep):
    s=pl.program_id(0); tokens,width=n_ref.shape; tile=width//2
    across=ids[1] if keep else 1-ids[1]
    @pl.when(s==0)
    def _():
        f=lax.broadcasted_iota(jnp.int32,(tile,width),1); j=lax.broadcasted_iota(jnp.int32,(tile,width),0)
        pick=jnp.where(f==(j//share*2+ids[0])*share+j%share,1.0,0.0).astype(BF)
        for p,pair in enumerate(((n_ref,no_ref),(a_ref,ao_ref))):
            for e,src in enumerate(pair):
                v=dotf(pick,src[...],NT)
                left_ref[p,:,e*tokens:(e+1)*tokens]=v.astype(BF)
                v=v.reshape(-1,2,share,tokens)
                part_ref[p,:,e*tokens:(e+1)*tokens]=jnp.where(across==0,v[:,0],v[:,1]).reshape(tile//2,tokens).astype(BF)
    def product(left,one,two):
        return (dotf(left[:,:tokens],one[...],NN)+dotf(left[:,tokens:],two[...],NN)).astype(BF)
    @pl.when(s<4)
    def _(): a_out[...]=product(part_ref[0],ua_ref,uao_ref).reshape(a_out.shape)
    @pl.when(s==4)
    def _(): a_out[...]=product(part_ref[1],ba_ref,bao_ref).reshape(a_out.shape)
    for t in range(2):
        @pl.when(s==t)
        def _(): b_out[:,t*tile:(t+1)*tile]=product(left_ref[0],ub_ref,ubo_ref)
    @pl.when(s==2)
    def _(): b_out[:,2*tile:]=product(left_ref[1],bb_ref,bbo_ref)

def grads_up(ids, normed, normed_other, att, att_other, up, up_other, branch, branch_other, ranks, keep):
    tokens,width=normed.shape; share=width//ranks; tile=width//2
    f=fixed_block(normed.shape)
    side=lambda ids: ids[2] if keep else 1-ids[2]
    ua=pl.BlockSpec((tokens,tile),lambda s,ids:(0,jnp.minimum(s,3)))
    ub=pl.BlockSpec((tokens,tile),lambda s,ids:(0,4+2*side(ids)+jnp.minimum(s,1)))
    ba=pl.BlockSpec((tokens,tile),lambda s,ids:(0,0))
    bb=pl.BlockSpec((tokens,tile//2),lambda s,ids:(0,2+side(ids)))
    outs=[jax.ShapeDtypeStruct((ranks//4,share,5*tile),BF),jax.ShapeDtypeStruct((tile,5*tile//2),BF)]
    return run_kernel(functools.partial(up_kernel,share=share,keep=keep),ids,(5,),
        [normed,normed_other,att,att_other,up,up_other,up,up_other,branch,branch_other,branch,branch_other],
        [f,f,f,f,ua,ua,ub,ub,ba,ba,bb,bb],outs,
        [pl.BlockSpec((ranks//4,share,tile),lambda s,ids:(0,0,s)),fixed_block(outs[1].shape)],
        [pltpu.VMEM((2,tile,2*tokens),BF),pltpu.VMEM((2,tile//2,2*tokens),BF)],"grads_up",tokens*width*(up.shape[1]+width))

def add_kernel(ids, *refs, plan):
    n=sum(len(parts) for _,_,parts in plan)
    ins,outs=list(refs[:2*n]),list(refs[2*n:])
    for mode,which,parts in plan:
        made=[outs.pop(0) for _ in range(1 if mode=="sum" else 2)]
        base=0
        for part in parts:
            k_ref,r_ref=ins.pop(0),ins.pop(0)
            def total(index): return (k_ref[index].astype(F32)+r_ref[index].astype(F32)).astype(BF)
            for o,out in enumerate(made):
                half=ids[which] if o else 1-ids[which]
                for i in range(out.shape[0]):
                    if mode=="sum": v=total((i,))
                    elif mode=="columns":
                        width=k_ref.shape[2]//2
                        v=total((i,slice(None),pl.ds(pl.multiple_of(half*width,128),width)))
                    else: v=total((2*i+half,))
                    out[i,base:base+v.shape[0],:]=v
            base+=k_ref.shape[1]

def add_split(ids, plan, arrays, name):
    outs=[]; at=0
    for mode,_,parts in plan:
        m,_,c=arrays[at].shape
        r=sum(arrays[at+2*i].shape[1] for i in range(len(parts))); at+=2*len(parts)
        outs+=[(m,r,c)] if mode=="sum" else [(m,r,c//2) if mode=="columns" else (m//2,r,c)]*2
    return run_kernel(functools.partial(add_kernel,plan=plan),ids,(1,),arrays,[fixed_block(a.shape) for a in arrays],
        [jax.ShapeDtypeStruct(s,BF) for s in outs],[fixed_block(s) for s in outs],[],name,sum(math.prod(s) for s in outs))

def project_kernel(ids, x_ref, gain_ref, shift_ref, wq_ref, wk_ref, wv_ref, bq_ref, bv_ref, packed_ref, normed_ref):
    tokens=x_ref.shape[0]; half=tokens//2
    @pl.when(pl.program_id(0)==0)
    def _():
        x=x_ref[...].astype(F32)
        x=x-jnp.mean(x,axis=1,keepdims=True)
        x=x*lax.rsqrt(jnp.mean(x*x,axis=1,keepdims=True)+EPSILON)
        normed_ref[...]=(x*gain_ref[...]+shift_ref[...]).astype(BF)
    n=normed_ref[...]
    q=(dotf(n,wq_ref[...],NN)+bq_ref[...])*(LOG2E*HEAD_DIM**-0.5)
    k=dotf(n,wk_ref[...],NN)
    v=dotf(n,wv_ref[...],NN)+bv_ref[...]
    for h in range(q.shape[1]//HEAD_DIM):
        join=pair_down if h%2 else pair_up
        cols=slice(h//2*128,h//2*128+128)
        packed_ref[h,:tokens,:]=join(q[:,cols],k[:,cols]).astype(BF)
        packed_ref[h,tokens:,:]=join(v[:half,cols],v[half:,cols]).astype(BF)

def project(ids, x, gain, shift, w_qkv, bias_qv):
    tokens,width=x.shape; tile=256; steps=width//tile
    w=lambda base:pl.BlockSpec((width,tile),lambda s,ids:(0,base+s))
    c=lambda base:pl.BlockSpec((1,tile),lambda s,ids:(0,base+s))
    outs=[jax.ShapeDtypeStruct((HEADS,tokens//2*3,128),BF),jax.ShapeDtypeStruct((tokens,width),BF)]
    return run_kernel(project_kernel,ids,(steps,),[x,gain[None],shift[None],w_qkv,w_qkv,w_qkv,bias_qv[None],bias_qv[None]],
        [fixed_block(x.shape)]+[fixed_block((1,width))]*2+[w(0),w(steps),w(2*steps),c(0),c(steps)],outs,
        [pl.BlockSpec((tile//HEAD_DIM,tokens//2*3,128),lambda s,ids:(s,0,0)),fixed_block((tokens,width))],[],"project",6*tokens*width*width)

def unpack_tile(one, two):
    return jnp.concatenate([pair_up(one,two),pair_down(one,two)],axis=0)

def mix_kernel(ids, got_ref, w_ref, x_ref, bias_ref, gain_ref, shift_ref, two_ref, att_ref, res_ref):
    s=pl.program_id(0); width=x_ref.shape[1]
    tiles=[unpack_tile(got_ref[2*p].astype(F32),got_ref[2*p+1].astype(F32)).astype(BF) for p in range(2)]
    att=jnp.concatenate(tiles,axis=1)
    att_ref[:,pl.ds(pl.multiple_of(s*256,256),256)]=att
    @pl.when(s==0)
    def _(): res_ref[...]=x_ref[...].astype(F32)+bias_ref[...]
    res_ref[...]+=dotf(att,w_ref[...],NN)
    @pl.when(s==pl.num_programs(0)-1)
    def _():
        x=res_ref[...]
        x=x-jnp.mean(x,axis=1,keepdims=True)
        x=x*lax.rsqrt(jnp.mean(x*x,axis=1,keepdims=True)+EPSILON)
        two_ref[...]=(x*gain_ref[...]+shift_ref[...]).astype(BF)

def mix(ids, got, w_out, x, bias, gain, shift):
    tokens,width=x.shape; row=fixed_block((1,width))
    return run_kernel(mix_kernel,ids,(width//256,),[got,w_out,x,bias[None],gain[None],shift[None]],
        [pl.BlockSpec((4,tokens//2,128),lambda s,ids:(s,0,0)),pl.BlockSpec((256,width),lambda s,ids:(s,0)),fixed_block(x.shape),row,row,row],
        [jax.ShapeDtypeStruct((tokens,width),t) for t in (BF,BF,F32)],[fixed_block((tokens,width))]*3,[],"mix",2*tokens*width*width)

def grad_pack_kernel(ids, g_ref, w_ref, small_ref, out_ref):
    half=g_ref.shape[0]//2
    g=dotf(g_ref[...],w_ref[...],NT)
    for h in range(4):
        join=pair_down if h%2 else pair_up
        cols=slice(h//2*128,h//2*128+128)
        out_ref[h,:half,:]=join(g[:half,cols],g[half:,cols]).astype(BF)
    out_ref[:,half:,:]=small_ref[...]

def grad_pack(ids, g, w_out, smalls):
    tokens,width=g.shape; rows=tokens//2+smalls.shape[1]
    return run_kernel(grad_pack_kernel,ids,(width//256,),[g,w_out,smalls],
        [fixed_block(g.shape),pl.BlockSpec((256,width),lambda s,ids:(s,0)),pl.BlockSpec((4,)+smalls.shape[1:],lambda s,ids:(s,0,0))],
        [jax.ShapeDtypeStruct((HEADS,rows,128),BF)],[pl.BlockSpec((4,rows,128),lambda s,ids:(s,0,0))],[],"grad_pack",2*tokens*width*width)[0]

def message_kernel(ids, n_ref, dx_ref, out_ref, acc_ref, sum_ref, *, tokens, share):
    s=pl.program_id(0); half=tokens//2
    sides=[]
    for c in range(dx_ref.shape[0]):
        v=dx_ref[c,tokens:,:].astype(F32)
        v=jnp.concatenate([v,pltpu.roll(v,HEAD_DIM,1)],axis=0)
        v=jnp.where(lanes_low(v.shape),v,0.0).astype(BF)
        out_ref[s*dx_ref.shape[0]+c,:tokens+half,:]=dx_ref[c]
        sides.append(jnp.concatenate([dx_ref[c,:tokens,:],v],axis=1))
    side=jnp.concatenate(sides,axis=0)
    @pl.when(s==0)
    def _():
        acc_ref[...]=jnp.zeros_like(acc_ref); sum_ref[...]=jnp.zeros_like(sum_ref)
    acc_ref[...]+=dotf(n_ref[...],side,TN)
    sum_ref[...]+=jnp.sum(side.astype(F32).reshape(-1,8,256),axis=0)
    @pl.when(s==pl.num_programs(0)-1)
    def _():
        total=jnp.sum(sum_ref[...],axis=0,keepdims=True)
        high=total.astype(BF).astype(F32); rest=total-high
        line=lax.broadcasted_iota(jnp.int32,(16,128),0)
        extra=jnp.where(line==0,high[:,:128],jnp.where(line==1,rest[:,:128],jnp.where(line==2,high[:,128:],jnp.where(line==3,rest[:,128:],0.0))))
        for r in range(out_ref.shape[0]):
            rows=slice(r*share,(r+1)*share)
            base=tokens+half
            out_ref[r,base:base+share,:]=acc_ref[rows,:128].astype(BF)
            v=acc_ref[rows,128:]
            out_ref[r,base+share:base+share+share//2,:]=pair_up(v[:share//2],v[share//2:]).astype(BF)
            out_ref[r,base+share+share//2:,:]=extra.astype(BF)

def weight_message(ids, normed_all, dx):
    ranks,rows,_=dx.shape; tokens=rows//3*2; full,width=normed_all.shape; share=width//ranks
    step=4; shape=(ranks,rows+share//2*3+16,128)
    return run_kernel(functools.partial(message_kernel,tokens=tokens,share=share),ids,(ranks//step,),[normed_all,dx],
        [pl.BlockSpec((step*tokens,width),lambda s,ids:(s,0)),pl.BlockSpec((step,rows,128),lambda s,ids:(s,0,0))],
        [jax.ShapeDtypeStruct(shape,BF)],[fixed_block(shape)],
        [pltpu.VMEM((width,256),F32),pltpu.VMEM((8,256),F32)],"weight_message",2*full*width*192)[0]

def finish_kernel(ids, one_ref, two_ref, w_ref, gain_ref, shift_ref, grad_ref, cols_ref, lg_ref, lb_ref):
    share=grad_ref.shape[0]; width=grad_ref.shape[1]//3
    first=jnp.zeros((share,128),F32); second=jnp.zeros((share,128),F32)
    def both(h): return one_ref[h].astype(F32)+two_ref[h].astype(F32)
    for p in range(HEADS//2):
        a,b=both(2*p),both(2*p+1)
        end=share+share//2
        q=pair_up(a[:share],b[:share]); k=pair_down(a[:share],b[:share])
        v=unpack_tile(a[share:end],b[share:end])
        la=a[end:end+8],b[end:end+8]
        cq=pair_up(*la); ck=pair_down(*la)
        for base,tile,col in ((0,q,cq[0:1]+cq[1:2]),(width,k,ck[0:1]+ck[1:2]),(2*width,v,cq[2:3]+cq[3:4])):
            at=slice(base+p*128,base+p*128+128)
            w=w_ref[:,at].astype(F32)
            grad_ref[:,at]=tile; cols_ref[:,at]=col
            first=first+w*tile; second=second+w*col
    bias=jnp.sum(second,axis=1,keepdims=True)
    lb_ref[...]=bias
    lg_ref[...]=(jnp.sum(first,axis=1,keepdims=True)-shift_ref[...]*bias)/gain_ref[...]

def finish(ids, one, two, w_qkv, gain, shift, ranks):
    width=w_qkv.shape[0]; share=width//ranks
    mine=lambda c:pl.BlockSpec((share,c),lambda s,ids:(ids[5],0))
    outs=[jax.ShapeDtypeStruct(s,F32) for s in ((share,3*width),(1,3*width),(share,1),(share,1))]
    return run_kernel(finish_kernel,ids,(1,),[one,two,w_qkv,gain[:,None],shift[:,None]],
        [fixed_block(one.shape)]*2+[mine(3*width),mine(1),mine(1)],outs,[fixed_block(o.shape) for o in outs],[],"finish",share*width*12)

def input_kernel(ids, got_ref, wq_ref, wk_ref, wv_ref, x_ref, gain_ref, res_ref, out_ref, acc_ref):
    s=pl.program_id(0); tokens=x_ref.shape[0]
    @pl.when(s==0)
    def _(): acc_ref[...]=jnp.zeros_like(acc_ref)
    q,k,v=[],[],[]
    for p in range(2):
        a,b=got_ref[2*p].astype(F32),got_ref[2*p+1].astype(F32)
        q.append(pair_up(a[:tokens],b[:tokens])); k.append(pair_down(a[:tokens],b[:tokens]))
        v.append(unpack_tile(a[tokens:tokens//2*3],b[tokens:tokens//2*3]))
    total=acc_ref[...]
    for tiles,w_ref in ((q,wq_ref),(k,wk_ref),(v,wv_ref)):
        total=total+dotf(jnp.concatenate(tiles,axis=1).astype(BF),w_ref[...],NT)
    acc_ref[...]=total
    @pl.when(s==pl.num_programs(0)-1)
    def _():
        x=x_ref[...].astype(F32)
        x=x-jnp.mean(x,axis=1,keepdims=True)
        scale=lax.rsqrt(jnp.mean(x*x,axis=1,keepdims=True)+EPSILON)
        x=x*scale
        g=acc_ref[...]*gain_ref[...]
        g=(g-jnp.mean(g,axis=1,keepdims=True)-x*jnp.mean(g*x,axis=1,keepdims=True))*scale
        out_ref[...]=(res_ref[...]+g).astype(BF)

def input_grad(ids, got, w_qkv, x, gain, residual_grad):
    tokens,width=x.shape; steps=width//256
    w=lambda base:pl.BlockSpec((width,256),lambda s,ids:(0,base+s))
    return run_kernel(input_kernel,ids,(steps,),[got,w_qkv,w_qkv,w_qkv,x,gain[None],residual_grad],
        [pl.BlockSpec((4,)+got.shape[1:],lambda s,ids:(s,0,0)),w(0),w(steps),w(2*steps),fixed_block(x.shape),fixed_block((1,width)),fixed_block(x.shape)],
        [jax.ShapeDtypeStruct((tokens,width),BF)],[fixed_block((tokens,width))],[pltpu.VMEM((tokens,width),F32)],"input_grad",6*tokens*width*width)[0]

def statistics(values):
    centre = jnp.mean(values, axis=-1, keepdims=True)
    centred = values - centre
    second = jnp.mean(centred * centred, axis=-1, keepdims=True)
    scale = lax.rsqrt(second + EPSILON)
    return centred * scale, scale


def norm_back(unit, scale, gain, grad):
    scaled = grad * gain
    first = jnp.mean(scaled, axis=-1, keepdims=True)
    second = jnp.mean(scaled * unit, axis=-1, keepdims=True)
    return (scaled - first - unit * second) * scale


def row_sum(value):
    low = lax.optimization_barrier(value.astype(BF))
    if lax.axis_size("row") == 2:
        return low.astype(F32) + lax.ppermute(low, "row", [(0, 1), (1, 0)]).astype(F32)
    return lax.psum(low.astype(F32), "row")


def exchange(value):
    return lax.all_to_all(value, "seq", 0, 0, tiled=True)


def swap(value, bit):
    return lax.ppermute(value, "seq", [(i, i ^ bit) for i in range(lax.axis_size("seq"))])


def swap_row(value):
    return lax.ppermute(value, "row", [(0, 1), (1, 0)])


def half_step(value, axis, mine, move):
    keep = lax.dynamic_index_in_dim(value, mine, axis, keepdims=False)
    sent = lax.dynamic_index_in_dim(value, 1 - mine, axis, keepdims=False)
    return (keep.astype(F32) + move(sent).astype(F32)).astype(BF)


def outer_steps(value):
    me, bit = lax.axis_index("seq"), 4
    while value.shape[0] > 1:
        value = value.reshape((value.shape[0] // 2, 2) + value.shape[1:])
        value = half_step(value, 1, me // bit % 2, lambda v, bit=bit: swap(v, bit))
        bit *= 2
    return value[0]


def row_join(value):
    other = swap_row(value)
    first = lax.axis_index("row") == 0
    return jnp.where(first, value, other).astype(F32), jnp.where(first, other, value).astype(F32)


def per_device(
    frames,
    seg_lengths,
    ln1_gain,
    ln1_bias,
    w_qkv,
    bias_qv,
    w_out,
    bias_out,
    ln2_gain,
    ln2_bias,
    w_up,
    bias_up,
    w_down,
    bias_down,
    grad_out,
):
    tokens, feature = frames.shape[1:]
    ranks = lax.axis_size("seq")
    me = lax.axis_index("seq")
    group = max(1, ranks // HEADS)
    full = ranks * tokens
    share = feature // ranks
    wide = w_up.shape[1] // ranks
    lengths = seg_lengths[0]
    starts = jnp.cumsum(lengths, dtype=jnp.int32) - lengths
    part = (me % group).astype(jnp.int32)[None]

    def spread(value):
        return jnp.repeat(value, group, axis=0) if group > 1 else value

    def fold(value):
        if group == 1:
            return value
        value = value.reshape((HEADS, group) + value.shape[1:])
        return jnp.sum(value.astype(F32), axis=1).astype(value.dtype)

    place = [me % 2, me // 2 % 2, lax.axis_index("row"), me // 4 % 2, me // 8 % 2, me]
    ids = jnp.stack(place).astype(jnp.int32)
    packed, normed_low = project(ids, frames[0], ln1_gain, ln1_bias, w_qkv, bias_qv)
    packed = exchange(spread(packed))
    cot_low = grad_out[0]
    fast = ranks == 16 and lax.axis_size("row") == 2
    if fast:
        cot_two = swap(cot_low, 2)
        cots = [cot_low, swap(cot_low, 1), cot_two, swap(cot_two, 1)]
        cots, packed = lax.optimization_barrier((cots, packed))
    gather = lambda v: lax.all_gather(v, "seq", axis=0, tiled=True)
    normed_low, packed = lax.optimization_barrier((normed_low, packed))
    normed_all = gather(normed_low)
    low, qa = attend(starts, part, packed, bq=FWD_TILE[0], bk=FWD_TILE[1], group=group)
    normed_two_low, attended_low, residual = mix(ids, fold(exchange(low)), w_out, frames[0], bias_out, ln2_gain, ln2_bias)
    unit_two, scale_two = statistics(residual)
    up_proj = dotf(normed_two_low, w_up, NN) + bias_up
    phi = 0.5 * (1.0 + lax.erf(up_proj * (0.5**0.5)))
    hidden = (up_proj * phi).astype(BF)
    slope = phi + up_proj * jnp.exp(-0.5 * up_proj * up_proj) * (1.0 / math.sqrt(2.0 * math.pi))
    out_frames = (residual + (dotf(hidden, w_down, NN) + bias_down)).astype(BF)
    cot = cot_low.astype(F32)
    if fast:
        picked, cot_low = lax.optimization_barrier((pick_blocks(ids, hidden, ranks), cot_low))
    up_grad = (dotf(cot_low, w_down, NT) * slope).astype(BF)
    normed_two_grad = dotf(up_grad, w_up, NT)
    gain_two = ln2_gain
    if fast:
        others = [swap(v, k + 1) for k, v in enumerate(picked)]
    residual_grad = cot + norm_back(unit_two, scale_two, gain_two, normed_two_grad)
    branch_grad = residual_grad.astype(BF)
    if fast:
        others[1], branch_grad = lax.optimization_barrier((others[1], branch_grad))
    if fast:
        factors = [
            normed_two_low,
            swap(normed_two_low, 1),
            attended_low,
            swap(attended_low, 1),
            up_grad,
            swap(up_grad, 1),
            branch_grad,
            swap(branch_grad, 1),
        ]
        a_sent, b_sent = grads_up(ids, *factors, ranks, False)
        branch_grad, a_sent, b_sent = lax.optimization_barrier((branch_grad, a_sent, b_sent))
        branch_grad, others = lax.optimization_barrier((branch_grad, others))
        a_got, b_got = swap(a_sent, 2), swap_row(b_sent)

    def piece(value):
        return value.reshape(ranks, -1)

    smalls = jnp.concatenate(
        [
            piece(jnp.sum(normed_two_grad * unit_two, axis=0)),
            piece(jnp.sum(normed_two_grad, axis=0)),
            piece(jnp.sum(branch_grad, axis=0, dtype=F32)),
            piece(jnp.sum(up_grad, axis=0, dtype=F32)),
            piece(jnp.sum(cot, axis=0)),
        ],
        axis=1,
    ).astype(BF)
    smalls = smalls.reshape(ranks, -1, 128)
    lines = smalls.shape[1]
    smalls = jnp.pad(smalls, ((0, 0), (0, 16 - lines), (0, 0)))
    if group == 1:
        sent = grad_pack(ids, branch_grad, w_out, smalls)
    else:
        sent = grad_pack(ids, branch_grad, w_out, jnp.zeros((HEADS, 16, 128), BF))
        sent = jnp.concatenate([spread(sent[:, : tokens // 2]), smalls], axis=1)
    sent, normed_all = lax.optimization_barrier((sent, normed_all))
    got = exchange(sent)
    small_total = row_sum(jnp.sum(got[:, tokens // 2 : tokens // 2 + lines].astype(F32), axis=0).reshape(-1))

    back = functools.partial(attend_back, starts, packed, qa, bq=BWD_TILE[0], bk=BWD_TILE[1], tokens=tokens)
    tiles = full // BWD_TILE[1]
    if fast:
        blocks = lambda v: v.reshape(ranks // 2, share, -1)
        factors, _ = lax.optimization_barrier((factors, sent))
        a_keep, b_keep = grads_up(ids, *factors, ranks, True)
        a_sent, a_keep, b_sent, b_keep = add_split(
            ids, (("columns", 2, "a"), ("blocks", 1, "b")), [a_keep, a_got, blocks(b_keep), blocks(b_got)], "add_one"
        )
        got, _, _ = lax.optimization_barrier((got, a_sent, b_sent))
        a_got, b_got = swap_row(a_sent), swap(b_sent, 2)
        down_sent, down_keep = grads_down(ids, hidden, others, cots, ranks)
        got, _ = lax.optimization_barrier((got, down_sent))
        down_got = swap(down_sent, 4)
        one = back((got, low), begin=tiles // 4, count=tiles // 4, first=True, last=False)
        a_got, b_got, down_got, one = lax.optimization_barrier((a_got, b_got, down_got, one))
        up_sent, up_keep, down_sent, down_keep = add_split(
            ids,
            (("blocks", 3, "ab"), ("columns", 2, "d")),
            [a_keep, a_got, b_keep, b_got, down_keep, down_got],
            "add_two",
        )
        one, up_sent, down_sent = lax.optimization_barrier((one, up_sent, down_sent))
        up_got, down_got = swap(up_sent, 4), swap_row(down_sent)
        two = back(one, begin=0, count=tiles // 4, first=False, last=False)
        two = [one[0], two[0], jnp.concatenate([two[1], one[2]], axis=0)]
        up_got, down_got, two = lax.optimization_barrier((up_got, down_got, two))
        up_sent, up_keep, down_sent, down_keep = add_split(
            ids, (("blocks", 4, "u"), ("blocks", 4, "d")), [up_keep, up_got, down_keep, down_got], "add_three"
        )
        two, up_sent, down_sent = lax.optimization_barrier((two, up_sent, down_sent))
        up_got, down_got = swap(up_sent, 8), swap(down_sent, 8)
        (dx,) = back(two, begin=tiles // 2, count=tiles // 2, first=False, last=True)
        everything = weight_message(ids, normed_all, dx)
        up_got, down_got, everything = lax.optimization_barrier((up_got, down_got, everything))
        up_part, down_part = add_split(
            ids, (("sum", 0, "u"), ("sum", 0, "d")), [up_keep, up_got, down_keep, down_got], "add_four"
        )
        one_half, other_half = row_join(up_part[0])
        rows_a, rows_b = slice(0, share), slice(share, 2 * share)
        width = feature
        total_up = jnp.concatenate(
            [
                one_half[rows_a],
                other_half[rows_a, : 3 * width // 4],
                one_half[rows_b, :width],
                other_half[rows_b, :width],
            ],
            axis=1,
        )
        total_out = jnp.concatenate(
            [other_half[rows_a, 3 * width // 4 :], one_half[rows_b, width:], other_half[rows_b, width:]], axis=1
        )
        total_down = jnp.concatenate(row_join(down_part[0]), axis=1)
    else:
        core, across = me % 2, me // 2 % 2

        def halves(value):
            parts = value.reshape(tokens, ranks // 2, 2, -1)
            keep = lax.dynamic_index_in_dim(parts, core, 2, keepdims=False).reshape(tokens, -1)
            sent = lax.dynamic_index_in_dim(parts, 1 - core, 2, keepdims=False).reshape(tokens, -1)
            return jnp.concatenate([keep, swap(sent, 1)], axis=0)

        def both(value):
            return jnp.concatenate([value, swap(value, 1)], axis=0)

        def reduced(value):
            value = value.astype(BF).reshape(ranks // 4, 2, -1, value.shape[-1])
            return row_sum(outer_steps(half_step(value, 1, across, lambda v: swap(v, 2))))

        total_down = reduced(dotf(halves(hidden), both(cot_low), TN))
        total_up = reduced(dotf(halves(normed_two_low), both(up_grad), TN))
        total_out = reduced(dotf(halves(attended_low), both(branch_grad), TN))
        (dx,) = back((got, low), begin=0, count=tiles, first=True, last=True)
        everything = weight_message(ids, normed_all, dx)
    returned = fold(exchange(everything))
    grad_frames = input_grad(ids, returned, w_qkv, frames[0], ln1_gain, residual_grad)
    mine = returned[:, tokens // 2 * 3 :]
    if lax.axis_size("row") == 2:
        theirs = swap_row(mine)
    else:
        mine = lax.psum(mine.astype(F32), "row")
        theirs = jnp.zeros_like(mine)
    grad_w_qkv, column_total, grad_ln1_gain, grad_ln1_bias = finish(ids, mine, theirs, w_qkv, ln1_gain, ln1_bias, ranks)
    grad_ln1_gain, grad_ln1_bias = grad_ln1_gain[:, 0], grad_ln1_bias[:, 0]
    grad_bias_qv = jnp.concatenate([column_total[0, :feature], column_total[0, 2 * feature :]])
    grad_bias_qv = lax.dynamic_slice(grad_bias_qv, (me * 2 * share,), (2 * share,))

    ends = [share, 2 * share, 3 * share, 3 * share + wide]
    grad_ln2_gain, grad_ln2_bias, grad_bias_out, grad_bias_up, grad_bias_down = jnp.split(small_total, ends)
    return (
        out_frames[None],
        grad_frames[None],
        grad_ln1_gain,
        grad_ln1_bias,
        grad_w_qkv,
        grad_bias_qv,
        total_out,
        grad_bias_out,
        grad_ln2_gain,
        grad_ln2_bias,
        total_up,
        grad_bias_up,
        total_down,
        grad_bias_down,
    )


def solution(mesh):
    frames_spec = P("row", "seq", None)
    vector, matrix = P("seq"), P("seq", None)
    return jax.shard_map(
        per_device,
        mesh=mesh,
        in_specs=(frames_spec, P("row", None)) + (P(),) * 12 + (frames_spec,),
        out_specs=(
            frames_spec,
            frames_spec,
            vector,
            vector,
            matrix,
            vector,
            matrix,
            vector,
            vector,
            vector,
            matrix,
            vector,
            matrix,
            vector,
        ),
        check_vma=False,
    )
```

```python
import functools
import math

import jax
import jax.numpy as jnp
from jax import lax
from jax.experimental import pallas as pl
from jax.experimental.pallas import tpu as pltpu
from jax.sharding import PartitionSpec as P

EPSILON = 1e-05
HEADS=16; HEAD_DIM=64; NEGATIVE=-1e30
FWD_TILE=(1024,1024); BWD_TILE=(1024,1024)
LOG2E=math.log2(math.e); LN2=math.log(2.0)
BF=jnp.bfloat16; F32=jnp.float32
NT=(((1,),(1,)),((),())); TN=(((0,),(0,)),((),())); NN=(((1,),(0,)),((),()))

def dotf(a,b,dims):
    return lax.dot_general(a,b,dims,preferred_element_type=F32)

def split3(v):
    hi=v.astype(BF); r=v-hi.astype(F32); mid=r.astype(BF); lo=(r-mid.astype(F32)).astype(BF)
    return hi.astype(F32),mid.astype(F32),lo.astype(F32)

def with_tail(base, stat):
    lane=lax.broadcasted_iota(jnp.int32, base.shape, 1)
    hi,mid,lo=split3(stat)
    tail=jnp.where(lane==HEAD_DIM,hi,jnp.where(lane==HEAD_DIM+1,mid,jnp.where(lane==HEAD_DIM+2,lo,0.0)))
    return jnp.where(lane<HEAD_DIM,base,tail).astype(BF)

def seg_start(starts, p, segs):
    best=jnp.int32(0)
    for k in range(segs):
        s=starts[k]
        best=jnp.where(s<=p, jnp.maximum(best,s), best)
    return best

def seg_end(starts, p, segs, full):
    best=jnp.int32(full)
    for k in range(segs):
        s=starts[k]
        best=jnp.where(s>p, jnp.minimum(best,s), best)
    return best

def lanes_low(shape):
    return lax.broadcasted_iota(jnp.int32,shape,1)<HEAD_DIM

def pair_up(one, two):
    return jnp.where(lanes_low(one.shape),one,pltpu.roll(two,HEAD_DIM,1))

def pair_down(one, two):
    return jnp.where(lanes_low(one.shape),pltpu.roll(one,HEAD_DIM,1),two)

def fwd_kernel(starts, part, x_ref, low_ref, qa_ref, s_ref, q_ref, ka_ref, va_ref, *, bq, bk, segs, group, tokens):
    i=pl.program_id(0); full=q_ref.shape[0]; half=tokens//2
    @pl.when(i==0)
    def _():
        mark=jnp.where(lax.broadcasted_iota(jnp.int32,(tokens,128),1)<HEAD_DIM+3,-1.0,0.0)
        def build(t,_):
            pair=x_ref[t,:tokens,:].astype(F32); v=x_ref[t,tokens:,:].astype(F32)
            rows=pl.ds(pl.multiple_of(t*tokens,tokens),tokens)
            low=lanes_low((tokens,128))
            q_ref[rows,:]=jnp.where(low,pair,0.0).astype(BF)
            ka_ref[rows,:]=jnp.where(low,pltpu.roll(pair,HEAD_DIM,1),mark).astype(BF)
            values=jnp.concatenate([v,pltpu.roll(v,HEAD_DIM,1)],axis=0)
            va_ref[rows,:]=jnp.where(low,values,mark).astype(BF)
            return 0
        lax.fori_loop(0,full//tokens,build,0)
    def skip():
        low_ref[...]=jnp.zeros_like(low_ref)
        qa_ref[...]=with_tail(jnp.zeros((bq,128),F32),jnp.full((bq,1),1e30,F32))
    def work():
        a=i*bq; last=a+bq-1
        f0=seg_start(starts,a,segs); f1=seg_start(starts,last,segs)
        lo=f0//bk; hi=last//bk+1
        u0=jnp.minimum((f1+bk-1)//bk,hi); u1=jnp.maximum(u0,(a+1)//bk)
        qb=q_ref[pl.ds(pl.multiple_of(a,bq),bq),:]
        row=a+lax.broadcasted_iota(jnp.int32,(bq,1),0)
        first=jnp.zeros((bq,1),jnp.int32)
        for k in range(segs):
            s=starts[k]; first=jnp.where(s<=row,jnp.maximum(first,s),first)
        def score(j,top,masked):
            s=dotf(qb,ka_ref[pl.ds(pl.multiple_of(j*bk,bk),bk),:],NT)
            if masked:
                key=j*bk+lax.broadcasted_iota(jnp.int32,(bq,bk),1)
                keep=key>=first if masked=="start" else key<=row
                s=jnp.where(keep&(key>=first) if masked=="both" else keep,s,NEGATIVE)
            s_ref[j]=s
            for c in range(bk//128):
                top=jnp.maximum(top,s[:,c*128:(c+1)*128])
            return top
        top=jnp.full((bq,128),NEGATIVE,F32)
        below=(a+1)//bk
        top=lax.fori_loop(lo,jnp.minimum(u0,below),lambda j,t:score(j,t,"start"),top)
        top=lax.fori_loop(u0,u1,lambda j,t:score(j,t,""),top)
        top=lax.fori_loop(jnp.maximum(below,lo),u0,lambda j,t:score(j,t,"both"),top)
        top=lax.fori_loop(u1,hi,lambda j,t:score(j,t,"order"),top)
        peak=jnp.max(top,axis=1,keepdims=True)
        def gather(j,acc):
            p=jnp.exp2(s_ref[j]-peak).astype(BF)
            return acc+dotf(p,va_ref[pl.ds(pl.multiple_of(j*bk,bk),bk),:],NN)
        acc=lax.fori_loop(lo,hi,gather,jnp.zeros((bq,128),F32))
        total=-acc[:,HEAD_DIM:HEAD_DIM+1]
        out=acc/total
        for c in range(bq//tokens):
            mid=c*tokens+half
            low_ref[c]=pair_up(out[c*tokens:mid],out[mid:mid+half]).astype(BF)
        qa_ref[...]=with_tail(qb.astype(F32),peak+jnp.log2(total))
    if group==1: work()
    else:
        own=(i%group)==part[0]
        pl.when(own)(work); pl.when(jnp.logical_not(own))(skip)

def attend(starts, part, x, *, bq, bk, group):
    ranks,rows,_=x.shape; tokens=rows//3*2; full=ranks*tokens; segs=starts.shape[0]
    if group>1: bq=tokens
    return pl.pallas_call(
        functools.partial(fwd_kernel,bq=bq,bk=bk,segs=segs,group=group,tokens=tokens),
        grid_spec=pltpu.PrefetchScalarGridSpec(num_scalar_prefetch=2,grid=(full//bq,),
            in_specs=[pl.BlockSpec(x.shape,lambda i,*_:(0,0,0))],
            out_specs=[pl.BlockSpec((bq//tokens,tokens//2,128),lambda i,*_:(i,0,0)),pl.BlockSpec((bq,128),lambda i,*_:(i,0))],
            scratch_shapes=[pltpu.VMEM((full//bk,bq,bk),F32)]+[pltpu.VMEM((full,128),BF)]*3),
        out_shape=[jax.ShapeDtypeStruct((ranks,tokens//2,128),BF),jax.ShapeDtypeStruct((full,128),BF)],
        compiler_params=pltpu.CompilerParams(vmem_limit_bytes=min(60<<20,full//1024*(40<<18))),
        cost_estimate=pl.CostEstimate(flops=full*full*512,bytes_accessed=full*1600,transcendentals=full*full//2),
        name="attend")(starts,part,x)

def bwd_kernel(starts, *refs, bq, bk, segs, begin, count, first, last, tokens):
    half=tokens//2
    refs=list(refs)
    x_ref,qa_ref=refs[:2]; refs=refs[2:]
    full=qa_ref.shape[0]; nq=full//bq
    if first: do_ref,low_ref=refs[:2]; refs=refs[2:]
    else: da_ref,dq_in,early_ref=refs[:3]; refs=refs[3:]
    if last: dx_ref,refs=refs[0],refs[1:]
    elif first: da_ref,refs=refs[0],refs[1:]
    dq_ref,kv_ref=refs[:2]
    if first and last: da_ref=refs[2]
    j=pl.program_id(0)
    low=lanes_low((tokens,128))
    unfold=lambda v: jnp.concatenate([v,pltpu.roll(v,HEAD_DIM,1)],axis=0)
    @pl.when(j==0)
    def _():
        if first:
            def build(t,_):
                rows=pl.ds(pl.multiple_of(t*tokens,tokens),tokens)
                g=unfold(do_ref[t,:half,:].astype(F32))
                delta=jnp.sum(jnp.where(low,g*unfold(low_ref[t].astype(F32)),0.0),axis=1,keepdims=True)
                da_ref[rows,:]=with_tail(g,delta)
                return 0
            lax.fori_loop(0,full//tokens,build,0)
        def clear(t,_):
            dq_ref[t]=jnp.zeros(dq_ref.shape[1:],F32) if first else dq_in[t]
            return 0
        lax.fori_loop(0,nq,clear,0)
    c=(begin+j)*bk; d=c+bk
    e0=seg_end(starts,c,segs,full); e1=seg_end(starts,d-1,segs,full)
    lo=c//bq; hi=(e1+bq-1)//bq
    u0=jnp.minimum((d-1+bq-1)//bq,hi); u1=jnp.maximum(u0,e0//bq)
    mark=jnp.where(lax.broadcasted_iota(jnp.int32,(tokens,128),1)<HEAD_DIM+3,-1.0,0.0)
    keys=[jnp.where(low,pltpu.roll(x_ref[t,:tokens,:].astype(F32),HEAD_DIM,1),mark) for t in range(bk//tokens)]
    keys=jnp.concatenate(keys,axis=0)
    values=[jnp.where(low,unfold(x_ref[t,tokens:,:].astype(F32)),mark) for t in range(bk//tokens)]
    ka=keys.astype(BF); va=jnp.concatenate(values,axis=0).astype(BF); kt=keys.T[:HEAD_DIM].astype(BF)
    def step(i,carry,masked):
        dk,dv=carry
        qrows=pl.ds(pl.multiple_of(i*bq,bq),bq)
        qa=qa_ref[qrows,:]; da=da_ref[qrows,:]
        p=jnp.exp2(dotf(ka,qa,NT))
        if masked:
            row=i*bq+lax.broadcasted_iota(jnp.int32,(1,bq),1)
            first_key=jnp.zeros((1,bq),jnp.int32)
            for k in range(segs):
                s=starts[k]; first_key=jnp.where(s<=row,jnp.maximum(first_key,s),first_key)
            key=c+lax.broadcasted_iota(jnp.int32,(bk,bq),0)
            p=jnp.where((key<=row)&(key>=first_key),p,0.0)
        dp=dotf(va,da,NT)
        pb=p.astype(BF); ds=(p*dp).astype(BF)
        dv=dv+dotf(pb,da,NN); dk=dk+dotf(ds,qa,NN)
        dq_ref[i]+=dotf(kt,ds,NN)
        return dk,dv
    z=jnp.zeros((bk,128),F32)
    carry=lax.fori_loop(lo,u0,lambda i,t:step(i,t,True),(z,z))
    carry=lax.fori_loop(u0,u1,lambda i,t:step(i,t,False),carry)
    dk,dv=lax.fori_loop(u1,hi,lambda i,t:step(i,t,True),carry)
    kv_ref[pl.ds(pl.multiple_of(j*bk,bk),bk),:]=pair_up(dv,dk*LN2).astype(BF)
    if last:
        @pl.when(j==count-1)
        def _():
            for t in range(nq):
                dq=dq_ref[t].T*HEAD_DIM**-0.5
                dq=jnp.concatenate([dq,dq],axis=1)
                for c in range(bq//tokens):
                    r=t*bq+c*tokens
                    kv=early_ref[r:r+tokens,:] if r<begin*bk else kv_ref[r-begin*bk:r-begin*bk+tokens,:]
                    kv=kv.astype(F32)
                    dx_ref[r//tokens,:tokens,:]=jnp.where(low,dq[c*tokens:(c+1)*tokens],kv).astype(BF)
                    dx_ref[r//tokens,tokens:,:]=pair_up(kv[:half],kv[half:]).astype(BF)

def attend_back(starts, x, qa, rest, *, bq, bk, begin, count, tokens, first, last):
    full=qa.shape[0]; segs=starts.shape[0]
    fixed=lambda shape: pl.BlockSpec(shape,lambda i,*_:(0,)*len(shape))
    dq_shape=(full//bq,64,bq)
    if last:
        outs=[jax.ShapeDtypeStruct(x.shape,BF)]
        scratch=[pltpu.VMEM(dq_shape,F32),pltpu.VMEM((count*bk,128),BF)]
        if first: scratch+=[pltpu.VMEM((full,128),BF)]
    else:
        outs=[jax.ShapeDtypeStruct(dq_shape,F32),jax.ShapeDtypeStruct((count*bk,128),BF)]
        if first: outs=[jax.ShapeDtypeStruct((full,128),BF)]+outs
        scratch=[]
    area=full*full*(count/(full//bk))
    return pl.pallas_call(
        functools.partial(bwd_kernel,bq=bq,bk=bk,segs=segs,begin=begin,count=count,first=first,last=last,tokens=tokens),
        grid_spec=pltpu.PrefetchScalarGridSpec(num_scalar_prefetch=1,grid=(count,),
            in_specs=[pl.BlockSpec((bk//tokens,)+x.shape[1:],lambda j,*_:(begin+j,0,0))]+[fixed(v.shape) for v in (qa,)+tuple(rest)],
            out_specs=[fixed(o.shape) for o in outs],
            scratch_shapes=scratch),
        out_shape=outs,
        compiler_params=pltpu.CompilerParams(vmem_limit_bytes=min(60<<20,full//1024*((48 if first else 24)<<18))),
        cost_estimate=pl.CostEstimate(flops=int(area*1280),bytes_accessed=full*2000,transcendentals=int(area/2)),
        name="attend_back")(starts,x,qa,*rest)

def fixed_block(shape):
    return pl.BlockSpec(shape,lambda s,*_:(0,)*len(shape))

ROOM={"project": 60}

def run_kernel(kernel, ids, grid, ins, in_specs, outs, out_specs, scratch, name, flops):
    moved=sum(math.prod(v.shape)*2 for v in ins)+sum(math.prod(o.shape)*2 for o in outs)
    return pl.pallas_call(kernel,
        grid_spec=pltpu.PrefetchScalarGridSpec(num_scalar_prefetch=1,grid=grid,in_specs=in_specs,out_specs=out_specs,scratch_shapes=scratch),
        out_shape=outs,compiler_params=pltpu.CompilerParams(vmem_limit_bytes=ROOM.get(name,20)<<20),
        cost_estimate=pl.CostEstimate(flops=flops,bytes_accessed=moved,transcendentals=0),name=name)(ids,*ins)

def pick_kernel(ids, h_ref, *outs, wide):
    for k,out in enumerate(outs):
        other=lax.bitwise_xor(ids[1]*2+ids[0],jnp.int32(k+1))
        for z in range(out.shape[1]//wide):
            out[:,z*wide:(z+1)*wide]=h_ref[:,pl.ds(pl.multiple_of((4*z+other)*wide,wide),wide)]

def pick_blocks(ids, hidden, ranks):
    tokens,inner=hidden.shape; out=jax.ShapeDtypeStruct((tokens,inner//4),hidden.dtype)
    return run_kernel(functools.partial(pick_kernel,wide=inner//ranks),ids,(1,),[hidden],[fixed_block(hidden.shape)],
        [out]*3,[fixed_block(out.shape)]*3,[],"pick_blocks",0)

def down_kernel(ids, *refs):
    lefts,rights,(sent_ref,keep_ref)=refs[:4],refs[4:8],refs[8:]
    s=pl.program_id(0)
    v=dotf(lefts[0][...],rights[0][...],TN)
    for a,b in zip(lefts[1:],rights[1:]): v=v+dotf(a[...],b[...],TN)
    v=v.astype(BF)
    @pl.when(s<2)
    def _(): sent_ref[0]=v
    @pl.when(s>=2)
    def _(): keep_ref[0]=v

def grads_down(ids, hidden, others, cots, ranks):
    tokens,inner=hidden.shape; width=cots[0].shape[1]; wide=inner//ranks
    def level(s,ids): return 2*(s%2)+jnp.where(s<2,1-ids[3],ids[3])
    mine=pl.BlockSpec((tokens,wide),lambda s,ids:(0,4*level(s,ids)+2*ids[1]+ids[0]))
    got=pl.BlockSpec((tokens,wide),lambda s,ids:(0,level(s,ids)))
    shape=jax.ShapeDtypeStruct((2,wide,width),BF)
    return run_kernel(down_kernel,ids,(4,),[hidden,*others,*cots],[mine,got,got,got]+[fixed_block(cots[0].shape)]*4,[shape,shape],
        [pl.BlockSpec((1,wide,width),lambda s,ids:(jnp.minimum(s,1),0,0)),
         pl.BlockSpec((1,wide,width),lambda s,ids:(jnp.maximum(s-2,0),0,0))],[],"grads_down",2*tokens*inner*width)

def up_kernel(ids, n_ref, no_ref, a_ref, ao_ref, ua_ref, uao_ref, ub_ref, ubo_ref, ba_ref, bao_ref, bb_ref, bbo_ref,
              a_out, b_out, left_ref, part_ref, *, share, keep):
    s=pl.program_id(0); tokens,width=n_ref.shape; tile=width//2
    across=ids[1] if keep else 1-ids[1]
    @pl.when(s==0)
    def _():
        f=lax.broadcasted_iota(jnp.int32,(tile,width),1); j=lax.broadcasted_iota(jnp.int32,(tile,width),0)
        pick=jnp.where(f==(j//share*2+ids[0])*share+j%share,1.0,0.0).astype(BF)
        for p,pair in enumerate(((n_ref,no_ref),(a_ref,ao_ref))):
            for e,src in enumerate(pair):
                v=dotf(pick,src[...],NT)
                left_ref[p,:,e*tokens:(e+1)*tokens]=v.astype(BF)
                v=v.reshape(-1,2,share,tokens)
                part_ref[p,:,e*tokens:(e+1)*tokens]=jnp.where(across==0,v[:,0],v[:,1]).reshape(tile//2,tokens).astype(BF)
    def product(left,one,two):
        return (dotf(left[:,:tokens],one[...],NN)+dotf(left[:,tokens:],two[...],NN)).astype(BF)
    @pl.when(s<4)
    def _(): a_out[...]=product(part_ref[0],ua_ref,uao_ref).reshape(a_out.shape)
    @pl.when(s==4)
    def _(): a_out[...]=product(part_ref[1],ba_ref,bao_ref).reshape(a_out.shape)
    for t in range(2):
        @pl.when(s==t)
        def _(): b_out[:,t*tile:(t+1)*tile]=product(left_ref[0],ub_ref,ubo_ref)
    @pl.when(s==2)
    def _(): b_out[:,2*tile:]=product(left_ref[1],bb_ref,bbo_ref)

def grads_up(ids, normed, normed_other, att, att_other, up, up_other, branch, branch_other, ranks, keep):
    tokens,width=normed.shape; share=width//ranks; tile=width//2
    f=fixed_block(normed.shape)
    side=lambda ids: ids[2] if keep else 1-ids[2]
    ua=pl.BlockSpec((tokens,tile),lambda s,ids:(0,jnp.minimum(s,3)))
    ub=pl.BlockSpec((tokens,tile),lambda s,ids:(0,4+2*side(ids)+jnp.minimum(s,1)))
    ba=pl.BlockSpec((tokens,tile),lambda s,ids:(0,0))
    bb=pl.BlockSpec((tokens,tile//2),lambda s,ids:(0,2+side(ids)))
    outs=[jax.ShapeDtypeStruct((ranks//4,share,5*tile),BF),jax.ShapeDtypeStruct((tile,5*tile//2),BF)]
    return run_kernel(functools.partial(up_kernel,share=share,keep=keep),ids,(5,),
        [normed,normed_other,att,att_other,up,up_other,up,up_other,branch,branch_other,branch,branch_other],
        [f,f,f,f,ua,ua,ub,ub,ba,ba,bb,bb],outs,
        [pl.BlockSpec((ranks//4,share,tile),lambda s,ids:(0,0,s)),fixed_block(outs[1].shape)],
        [pltpu.VMEM((2,tile,2*tokens),BF),pltpu.VMEM((2,tile//2,2*tokens),BF)],"grads_up",tokens*width*(up.shape[1]+width))

def add_kernel(ids, *refs, plan):
    n=sum(len(parts) for _,_,parts in plan)
    ins,outs=list(refs[:2*n]),list(refs[2*n:])
    for mode,which,parts in plan:
        made=[outs.pop(0) for _ in range(1 if mode=="sum" else 2)]
        base=0
        for part in parts:
            k_ref,r_ref=ins.pop(0),ins.pop(0)
            def total(index): return (k_ref[index].astype(F32)+r_ref[index].astype(F32)).astype(BF)
            for o,out in enumerate(made):
                half=ids[which] if o else 1-ids[which]
                for i in range(out.shape[0]):
                    if mode=="sum": v=total((i,))
                    elif mode=="columns":
                        width=k_ref.shape[2]//2
                        v=total((i,slice(None),pl.ds(pl.multiple_of(half*width,128),width)))
                    else: v=total((2*i+half,))
                    out[i,base:base+v.shape[0],:]=v
            base+=k_ref.shape[1]

def add_split(ids, plan, arrays, name):
    outs=[]; at=0
    for mode,_,parts in plan:
        m,_,c=arrays[at].shape
        r=sum(arrays[at+2*i].shape[1] for i in range(len(parts))); at+=2*len(parts)
        outs+=[(m,r,c)] if mode=="sum" else [(m,r,c//2) if mode=="columns" else (m//2,r,c)]*2
    return run_kernel(functools.partial(add_kernel,plan=plan),ids,(1,),arrays,[fixed_block(a.shape) for a in arrays],
        [jax.ShapeDtypeStruct(s,BF) for s in outs],[fixed_block(s) for s in outs],[],name,sum(math.prod(s) for s in outs))

def project_kernel(ids, x_ref, gain_ref, shift_ref, wq_ref, wk_ref, wv_ref, bq_ref, bv_ref, packed_ref, normed_ref):
    tokens=x_ref.shape[0]; half=tokens//2
    @pl.when(pl.program_id(0)==0)
    def _():
        x=x_ref[...].astype(F32)
        x=x-jnp.mean(x,axis=1,keepdims=True)
        x=x*lax.rsqrt(jnp.mean(x*x,axis=1,keepdims=True)+EPSILON)
        normed_ref[...]=(x*gain_ref[...]+shift_ref[...]).astype(BF)
    n=normed_ref[...]
    q=(dotf(n,wq_ref[...],NN)+bq_ref[...])*(LOG2E*HEAD_DIM**-0.5)
    k=dotf(n,wk_ref[...],NN)
    v=dotf(n,wv_ref[...],NN)+bv_ref[...]
    for h in range(q.shape[1]//HEAD_DIM):
        join=pair_down if h%2 else pair_up
        cols=slice(h//2*128,h//2*128+128)
        packed_ref[h,:tokens,:]=join(q[:,cols],k[:,cols]).astype(BF)
        packed_ref[h,tokens:,:]=join(v[:half,cols],v[half:,cols]).astype(BF)

def project(ids, x, gain, shift, w_qkv, bias_qv):
    tokens,width=x.shape; tile=256; steps=width//tile
    w=lambda base:pl.BlockSpec((width,tile),lambda s,ids:(0,base+s))
    c=lambda base:pl.BlockSpec((1,tile),lambda s,ids:(0,base+s))
    outs=[jax.ShapeDtypeStruct((HEADS,tokens//2*3,128),BF),jax.ShapeDtypeStruct((tokens,width),BF)]
    return run_kernel(project_kernel,ids,(steps,),[x,gain[None],shift[None],w_qkv,w_qkv,w_qkv,bias_qv[None],bias_qv[None]],
        [fixed_block(x.shape)]+[fixed_block((1,width))]*2+[w(0),w(steps),w(2*steps),c(0),c(steps)],outs,
        [pl.BlockSpec((tile//HEAD_DIM,tokens//2*3,128),lambda s,ids:(s,0,0)),fixed_block((tokens,width))],[],"project",6*tokens*width*width)

def unpack_tile(one, two):
    return jnp.concatenate([pair_up(one,two),pair_down(one,two)],axis=0)

def mix_kernel(ids, got_ref, w_ref, x_ref, bias_ref, gain_ref, shift_ref, two_ref, att_ref, res_ref):
    s=pl.program_id(0); width=x_ref.shape[1]
    tiles=[unpack_tile(got_ref[2*p].astype(F32),got_ref[2*p+1].astype(F32)).astype(BF) for p in range(2)]
    att=jnp.concatenate(tiles,axis=1)
    att_ref[:,pl.ds(pl.multiple_of(s*256,256),256)]=att
    @pl.when(s==0)
    def _(): res_ref[...]=x_ref[...].astype(F32)+bias_ref[...]
    res_ref[...]+=dotf(att,w_ref[...],NN)
    @pl.when(s==pl.num_programs(0)-1)
    def _():
        x=res_ref[...]
        x=x-jnp.mean(x,axis=1,keepdims=True)
        x=x*lax.rsqrt(jnp.mean(x*x,axis=1,keepdims=True)+EPSILON)
        two_ref[...]=(x*gain_ref[...]+shift_ref[...]).astype(BF)

def mix(ids, got, w_out, x, bias, gain, shift):
    tokens,width=x.shape; row=fixed_block((1,width))
    return run_kernel(mix_kernel,ids,(width//256,),[got,w_out,x,bias[None],gain[None],shift[None]],
        [pl.BlockSpec((4,tokens//2,128),lambda s,ids:(s,0,0)),pl.BlockSpec((256,width),lambda s,ids:(s,0)),fixed_block(x.shape),row,row,row],
        [jax.ShapeDtypeStruct((tokens,width),t) for t in (BF,BF,F32)],[fixed_block((tokens,width))]*3,[],"mix",2*tokens*width*width)

def grad_pack_kernel(ids, g_ref, w_ref, small_ref, out_ref):
    half=g_ref.shape[0]//2
    g=dotf(g_ref[...],w_ref[...],NT)
    for h in range(4):
        join=pair_down if h%2 else pair_up
        cols=slice(h//2*128,h//2*128+128)
        out_ref[h,:half,:]=join(g[:half,cols],g[half:,cols]).astype(BF)
    out_ref[:,half:,:]=small_ref[...]

def grad_pack(ids, g, w_out, smalls):
    tokens,width=g.shape; rows=tokens//2+smalls.shape[1]
    return run_kernel(grad_pack_kernel,ids,(width//256,),[g,w_out,smalls],
        [fixed_block(g.shape),pl.BlockSpec((256,width),lambda s,ids:(s,0)),pl.BlockSpec((4,)+smalls.shape[1:],lambda s,ids:(s,0,0))],
        [jax.ShapeDtypeStruct((HEADS,rows,128),BF)],[pl.BlockSpec((4,rows,128),lambda s,ids:(s,0,0))],[],"grad_pack",2*tokens*width*width)[0]

def message_kernel(ids, n_ref, dx_ref, out_ref, acc_ref, sum_ref, *, tokens, share):
    s=pl.program_id(0); half=tokens//2
    sides=[]
    for c in range(dx_ref.shape[0]):
        v=dx_ref[c,tokens:,:].astype(F32)
        v=jnp.concatenate([v,pltpu.roll(v,HEAD_DIM,1)],axis=0)
        v=jnp.where(lanes_low(v.shape),v,0.0).astype(BF)
        out_ref[s*dx_ref.shape[0]+c,:tokens+half,:]=dx_ref[c]
        sides.append(jnp.concatenate([dx_ref[c,:tokens,:],v],axis=1))
    side=jnp.concatenate(sides,axis=0)
    @pl.when(s==0)
    def _():
        acc_ref[...]=jnp.zeros_like(acc_ref); sum_ref[...]=jnp.zeros_like(sum_ref)
    acc_ref[...]+=dotf(n_ref[...],side,TN)
    sum_ref[...]+=jnp.sum(side.astype(F32).reshape(-1,8,256),axis=0)
    @pl.when(s==pl.num_programs(0)-1)
    def _():
        total=jnp.sum(sum_ref[...],axis=0,keepdims=True)
        high=total.astype(BF).astype(F32); rest=total-high
        line=lax.broadcasted_iota(jnp.int32,(16,128),0)
        extra=jnp.where(line==0,high[:,:128],jnp.where(line==1,rest[:,:128],jnp.where(line==2,high[:,128:],jnp.where(line==3,rest[:,128:],0.0))))
        for r in range(out_ref.shape[0]):
            rows=slice(r*share,(r+1)*share)
            base=tokens+half
            out_ref[r,base:base+share,:]=acc_ref[rows,:128].astype(BF)
            v=acc_ref[rows,128:]
            out_ref[r,base+share:base+share+share//2,:]=pair_up(v[:share//2],v[share//2:]).astype(BF)
            out_ref[r,base+share+share//2:,:]=extra.astype(BF)

def weight_message(ids, normed_all, dx):
    ranks,rows,_=dx.shape; tokens=rows//3*2; full,width=normed_all.shape; share=width//ranks
    step=4; shape=(ranks,rows+share//2*3+16,128)
    return run_kernel(functools.partial(message_kernel,tokens=tokens,share=share),ids,(ranks//step,),[normed_all,dx],
        [pl.BlockSpec((step*tokens,width),lambda s,ids:(s,0)),pl.BlockSpec((step,rows,128),lambda s,ids:(s,0,0))],
        [jax.ShapeDtypeStruct(shape,BF)],[fixed_block(shape)],
        [pltpu.VMEM((width,256),F32),pltpu.VMEM((8,256),F32)],"weight_message",2*full*width*192)[0]

def finish_kernel(ids, one_ref, two_ref, w_ref, gain_ref, shift_ref, grad_ref, cols_ref, lg_ref, lb_ref):
    share=grad_ref.shape[0]; width=grad_ref.shape[1]//3
    first=jnp.zeros((share,128),F32); second=jnp.zeros((share,128),F32)
    def both(h): return one_ref[h].astype(F32)+two_ref[h].astype(F32)
    for p in range(HEADS//2):
        a,b=both(2*p),both(2*p+1)
        end=share+share//2
        q=pair_up(a[:share],b[:share]); k=pair_down(a[:share],b[:share])
        v=unpack_tile(a[share:end],b[share:end])
        la=a[end:end+8],b[end:end+8]
        cq=pair_up(*la); ck=pair_down(*la)
        for base,tile,col in ((0,q,cq[0:1]+cq[1:2]),(width,k,ck[0:1]+ck[1:2]),(2*width,v,cq[2:3]+cq[3:4])):
            at=slice(base+p*128,base+p*128+128)
            w=w_ref[:,at].astype(F32)
            grad_ref[:,at]=tile; cols_ref[:,at]=col
            first=first+w*tile; second=second+w*col
    bias=jnp.sum(second,axis=1,keepdims=True)
    lb_ref[...]=bias
    lg_ref[...]=(jnp.sum(first,axis=1,keepdims=True)-shift_ref[...]*bias)/gain_ref[...]

def finish(ids, one, two, w_qkv, gain, shift, ranks):
    width=w_qkv.shape[0]; share=width//ranks
    mine=lambda c:pl.BlockSpec((share,c),lambda s,ids:(ids[5],0))
    outs=[jax.ShapeDtypeStruct(s,F32) for s in ((share,3*width),(1,3*width),(share,1),(share,1))]
    return run_kernel(finish_kernel,ids,(1,),[one,two,w_qkv,gain[:,None],shift[:,None]],
        [fixed_block(one.shape)]*2+[mine(3*width),mine(1),mine(1)],outs,[fixed_block(o.shape) for o in outs],[],"finish",share*width*12)

def input_kernel(ids, got_ref, wq_ref, wk_ref, wv_ref, x_ref, gain_ref, res_ref, out_ref, acc_ref):
    s=pl.program_id(0); tokens=x_ref.shape[0]
    @pl.when(s==0)
    def _(): acc_ref[...]=jnp.zeros_like(acc_ref)
    q,k,v=[],[],[]
    for p in range(2):
        a,b=got_ref[2*p].astype(F32),got_ref[2*p+1].astype(F32)
        q.append(pair_up(a[:tokens],b[:tokens])); k.append(pair_down(a[:tokens],b[:tokens]))
        v.append(unpack_tile(a[tokens:tokens//2*3],b[tokens:tokens//2*3]))
    total=acc_ref[...]
    for tiles,w_ref in ((q,wq_ref),(k,wk_ref),(v,wv_ref)):
        total=total+dotf(jnp.concatenate(tiles,axis=1).astype(BF),w_ref[...],NT)
    acc_ref[...]=total
    @pl.when(s==pl.num_programs(0)-1)
    def _():
        x=x_ref[...].astype(F32)
        x=x-jnp.mean(x,axis=1,keepdims=True)
        scale=lax.rsqrt(jnp.mean(x*x,axis=1,keepdims=True)+EPSILON)
        x=x*scale
        g=acc_ref[...]*gain_ref[...]
        g=(g-jnp.mean(g,axis=1,keepdims=True)-x*jnp.mean(g*x,axis=1,keepdims=True))*scale
        out_ref[...]=(res_ref[...]+g).astype(BF)

def input_grad(ids, got, w_qkv, x, gain, residual_grad):
    tokens,width=x.shape; steps=width//256
    w=lambda base:pl.BlockSpec((width,256),lambda s,ids:(0,base+s))
    return run_kernel(input_kernel,ids,(steps,),[got,w_qkv,w_qkv,w_qkv,x,gain[None],residual_grad],
        [pl.BlockSpec((4,)+got.shape[1:],lambda s,ids:(s,0,0)),w(0),w(steps),w(2*steps),fixed_block(x.shape),fixed_block((1,width)),fixed_block(x.shape)],
        [jax.ShapeDtypeStruct((tokens,width),BF)],[fixed_block((tokens,width))],[pltpu.VMEM((tokens,width),F32)],"input_grad",6*tokens*width*width)[0]

def statistics(values):
    centre = jnp.mean(values, axis=-1, keepdims=True)
    centred = values - centre
    second = jnp.mean(centred * centred, axis=-1, keepdims=True)
    scale = lax.rsqrt(second + EPSILON)
    return centred * scale, scale


def norm_back(unit, scale, gain, grad):
    scaled = grad * gain
    first = jnp.mean(scaled, axis=-1, keepdims=True)
    second = jnp.mean(scaled * unit, axis=-1, keepdims=True)
    return (scaled - first - unit * second) * scale


def row_sum(value):
    low = lax.optimization_barrier(value.astype(BF))
    if lax.axis_size("row") == 2:
        return low.astype(F32) + lax.ppermute(low, "row", [(0, 1), (1, 0)]).astype(F32)
    return lax.psum(low.astype(F32), "row")


def exchange(value):
    return lax.all_to_all(value, "seq", 0, 0, tiled=True)


def swap(value, bit):
    return lax.ppermute(value, "seq", [(i, i ^ bit) for i in range(lax.axis_size("seq"))])


def swap_row(value):
    return lax.ppermute(value, "row", [(0, 1), (1, 0)])


def half_step(value, axis, mine, move):
    keep = lax.dynamic_index_in_dim(value, mine, axis, keepdims=False)
    sent = lax.dynamic_index_in_dim(value, 1 - mine, axis, keepdims=False)
    return (keep.astype(F32) + move(sent).astype(F32)).astype(BF)


def outer_steps(value):
    me, bit = lax.axis_index("seq"), 4
    while value.shape[0] > 1:
        value = value.reshape((value.shape[0] // 2, 2) + value.shape[1:])
        value = half_step(value, 1, me // bit % 2, lambda v, bit=bit: swap(v, bit))
        bit *= 2
    return value[0]


def row_join(value):
    other = swap_row(value)
    first = lax.axis_index("row") == 0
    return jnp.where(first, value, other).astype(F32), jnp.where(first, other, value).astype(F32)


def per_device(
    frames,
    seg_lengths,
    ln1_gain,
    ln1_bias,
    w_qkv,
    bias_qv,
    w_out,
    bias_out,
    ln2_gain,
    ln2_bias,
    w_up,
    bias_up,
    w_down,
    bias_down,
    grad_out,
):
    tokens, feature = frames.shape[1:]
    ranks = lax.axis_size("seq")
    me = lax.axis_index("seq")
    group = max(1, ranks // HEADS)
    full = ranks * tokens
    share = feature // ranks
    wide = w_up.shape[1] // ranks
    lengths = seg_lengths[0]
    starts = jnp.cumsum(lengths, dtype=jnp.int32) - lengths
    part = (me % group).astype(jnp.int32)[None]

    def spread(value):
        return jnp.repeat(value, group, axis=0) if group > 1 else value

    def fold(value):
        if group == 1:
            return value
        value = value.reshape((HEADS, group) + value.shape[1:])
        return jnp.sum(value.astype(F32), axis=1).astype(value.dtype)

    place = [me % 2, me // 2 % 2, lax.axis_index("row"), me // 4 % 2, me // 8 % 2, me]
    ids = jnp.stack(place).astype(jnp.int32)
    packed, normed_low = project(ids, frames[0], ln1_gain, ln1_bias, w_qkv, bias_qv)
    packed = exchange(spread(packed))
    cot_low = grad_out[0]
    fast = ranks == 16 and lax.axis_size("row") == 2
    if fast:
        cot_two = swap(cot_low, 2)
        cots = [cot_low, swap(cot_low, 1), cot_two, swap(cot_two, 1)]
        cots, packed = lax.optimization_barrier((cots, packed))
    gather = lambda v: lax.all_gather(v, "seq", axis=0, tiled=True)
    normed_low, packed = lax.optimization_barrier((normed_low, packed))
    normed_all = gather(normed_low)
    low, qa = attend(starts, part, packed, bq=FWD_TILE[0], bk=FWD_TILE[1], group=group)
    normed_two_low, attended_low, residual = mix(ids, fold(exchange(low)), w_out, frames[0], bias_out, ln2_gain, ln2_bias)
    unit_two, scale_two = statistics(residual)
    up_proj = dotf(normed_two_low, w_up, NN) + bias_up
    phi = 0.5 * (1.0 + lax.erf(up_proj * (0.5**0.5)))
    hidden = (up_proj * phi).astype(BF)
    slope = phi + up_proj * jnp.exp(-0.5 * up_proj * up_proj) * (1.0 / math.sqrt(2.0 * math.pi))
    out_frames = (residual + (dotf(hidden, w_down, NN) + bias_down)).astype(BF)
    cot = cot_low.astype(F32)
    if fast:
        picked, cot_low = lax.optimization_barrier((pick_blocks(ids, hidden, ranks), cot_low))
    up_grad = (dotf(cot_low, w_down, NT) * slope).astype(BF)
    normed_two_grad = dotf(up_grad, w_up, NT)
    gain_two = ln2_gain
    if fast:
        others = [swap(v, k + 1) for k, v in enumerate(picked)]
    residual_grad = cot + norm_back(unit_two, scale_two, gain_two, normed_two_grad)
    branch_grad = residual_grad.astype(BF)
    if fast:
        others[1], branch_grad = lax.optimization_barrier((others[1], branch_grad))
    if fast:
        factors = [
            normed_two_low,
            swap(normed_two_low, 1),
            attended_low,
            swap(attended_low, 1),
            up_grad,
            swap(up_grad, 1),
            branch_grad,
            swap(branch_grad, 1),
        ]
        a_sent, b_sent = grads_up(ids, *factors, ranks, False)
        branch_grad, a_sent, b_sent = lax.optimization_barrier((branch_grad, a_sent, b_sent))
        branch_grad, others = lax.optimization_barrier((branch_grad, others))
        a_got, b_got = swap(a_sent, 2), swap_row(b_sent)

    def piece(value):
        return value.reshape(ranks, -1)

    smalls = jnp.concatenate(
        [
            piece(jnp.sum(normed_two_grad * unit_two, axis=0)),
            piece(jnp.sum(normed_two_grad, axis=0)),
            piece(jnp.sum(branch_grad, axis=0, dtype=F32)),
            piece(jnp.sum(up_grad, axis=0, dtype=F32)),
            piece(jnp.sum(cot, axis=0)),
        ],
        axis=1,
    ).astype(BF)
    smalls = smalls.reshape(ranks, -1, 128)
    lines = smalls.shape[1]
    smalls = jnp.pad(smalls, ((0, 0), (0, 16 - lines), (0, 0)))
    if group == 1:
        sent = grad_pack(ids, branch_grad, w_out, smalls)
    else:
        sent = grad_pack(ids, branch_grad, w_out, jnp.zeros((HEADS, 16, 128), BF))
        sent = jnp.concatenate([spread(sent[:, : tokens // 2]), smalls], axis=1)
    sent, normed_all = lax.optimization_barrier((sent, normed_all))
    got = exchange(sent)
    small_total = row_sum(jnp.sum(got[:, tokens // 2 : tokens // 2 + lines].astype(F32), axis=0).reshape(-1))

    back = functools.partial(attend_back, starts, packed, qa, bq=BWD_TILE[0], bk=BWD_TILE[1], tokens=tokens)
    tiles = full // BWD_TILE[1]
    if fast:
        blocks = lambda v: v.reshape(ranks // 2, share, -1)
        factors, _ = lax.optimization_barrier((factors, sent))
        a_keep, b_keep = grads_up(ids, *factors, ranks, True)
        a_sent, a_keep, b_sent, b_keep = add_split(
            ids, (("columns", 2, "a"), ("blocks", 1, "b")), [a_keep, a_got, blocks(b_keep), blocks(b_got)], "add_one"
        )
        got, _, _ = lax.optimization_barrier((got, a_sent, b_sent))
        a_got, b_got = swap_row(a_sent), swap(b_sent, 2)
        down_sent, down_keep = grads_down(ids, hidden, others, cots, ranks)
        got, _ = lax.optimization_barrier((got, down_sent))
        down_got = swap(down_sent, 4)
        one = back((got, low), begin=tiles // 4, count=tiles // 4, first=True, last=False)
        a_got, b_got, down_got, one = lax.optimization_barrier((a_got, b_got, down_got, one))
        up_sent, up_keep, down_sent, down_keep = add_split(
            ids,
            (("blocks", 3, "ab"), ("columns", 2, "d")),
            [a_keep, a_got, b_keep, b_got, down_keep, down_got],
            "add_two",
        )
        one, up_sent, down_sent = lax.optimization_barrier((one, up_sent, down_sent))
        up_got, down_got = swap(up_sent, 4), swap_row(down_sent)
        two = back(one, begin=0, count=tiles // 4, first=False, last=False)
        two = [one[0], two[0], jnp.concatenate([two[1], one[2]], axis=0)]
        up_got, down_got, two = lax.optimization_barrier((up_got, down_got, two))
        up_sent, up_keep, down_sent, down_keep = add_split(
            ids, (("blocks", 4, "u"), ("blocks", 4, "d")), [up_keep, up_got, down_keep, down_got], "add_three"
        )
        two, up_sent, down_sent = lax.optimization_barrier((two, up_sent, down_sent))
        up_got, down_got = swap(up_sent, 8), swap(down_sent, 8)
        (dx,) = back(two, begin=tiles // 2, count=tiles // 2, first=False, last=True)
        everything = weight_message(ids, normed_all, dx)
        up_got, down_got, everything = lax.optimization_barrier((up_got, down_got, everything))
        up_part, down_part = add_split(
            ids, (("sum", 0, "u"), ("sum", 0, "d")), [up_keep, up_got, down_keep, down_got], "add_four"
        )
        one_half, other_half = row_join(up_part[0])
        rows_a, rows_b = slice(0, share), slice(share, 2 * share)
        width = feature
        total_up = jnp.concatenate(
            [
                one_half[rows_a],
                other_half[rows_a, : 3 * width // 4],
                one_half[rows_b, :width],
                other_half[rows_b, :width],
            ],
            axis=1,
        )
        total_out = jnp.concatenate(
            [other_half[rows_a, 3 * width // 4 :], one_half[rows_b, width:], other_half[rows_b, width:]], axis=1
        )
        total_down = jnp.concatenate(row_join(down_part[0]), axis=1)
    else:
        core, across = me % 2, me // 2 % 2

        def halves(value):
            parts = value.reshape(tokens, ranks // 2, 2, -1)
            keep = lax.dynamic_index_in_dim(parts, core, 2, keepdims=False).reshape(tokens, -1)
            sent = lax.dynamic_index_in_dim(parts, 1 - core, 2, keepdims=False).reshape(tokens, -1)
            return jnp.concatenate([keep, swap(sent, 1)], axis=0)

        def both(value):
            return jnp.concatenate([value, swap(value, 1)], axis=0)

        def reduced(value):
            value = value.astype(BF).reshape(ranks // 4, 2, -1, value.shape[-1])
            return row_sum(outer_steps(half_step(value, 1, across, lambda v: swap(v, 2))))

        total_down = reduced(dotf(halves(hidden), both(cot_low), TN))
        total_up = reduced(dotf(halves(normed_two_low), both(up_grad), TN))
        total_out = reduced(dotf(halves(attended_low), both(branch_grad), TN))
        (dx,) = back((got, low), begin=0, count=tiles, first=True, last=True)
        everything = weight_message(ids, normed_all, dx)
    returned = fold(exchange(everything))
    grad_frames = input_grad(ids, returned, w_qkv, frames[0], ln1_gain, residual_grad)
    mine = returned[:, tokens // 2 * 3 :]
    if lax.axis_size("row") == 2:
        theirs = swap_row(mine)
    else:
        mine = lax.psum(mine.astype(F32), "row")
        theirs = jnp.zeros_like(mine)
    grad_w_qkv, column_total, grad_ln1_gain, grad_ln1_bias = finish(ids, mine, theirs, w_qkv, ln1_gain, ln1_bias, ranks)
    grad_ln1_gain, grad_ln1_bias = grad_ln1_gain[:, 0], grad_ln1_bias[:, 0]
    grad_bias_qv = jnp.concatenate([column_total[0, :feature], column_total[0, 2 * feature :]])
    grad_bias_qv = lax.dynamic_slice(grad_bias_qv, (me * 2 * share,), (2 * share,))

    ends = [share, 2 * share, 3 * share, 3 * share + wide]
    grad_ln2_gain, grad_ln2_bias, grad_bias_out, grad_bias_up, grad_bias_down = jnp.split(small_total, ends)
    return (
        out_frames[None],
        grad_frames[None],
        grad_ln1_gain,
        grad_ln1_bias,
        grad_w_qkv,
        grad_bias_qv,
        total_out,
        grad_bias_out,
        grad_ln2_gain,
        grad_ln2_bias,
        total_up,
        grad_bias_up,
        total_down,
        grad_bias_down,
    )


def solution(mesh):
    frames_spec = P("row", "seq", None)
    vector, matrix = P("seq"), P("seq", None)
    return jax.shard_map(
        per_device,
        mesh=mesh,
        in_specs=(frames_spec, P("row", None)) + (P(),) * 12 + (frames_spec,),
        out_specs=(
            frames_spec,
            frames_spec,
            vector,
            vector,
            matrix,
            vector,
            matrix,
            vector,
            vector,
            vector,
            matrix,
            vector,
            matrix,
            vector,
        ),
        check_vma=False,
    )
```
